128 devices in a mesh: group: 8 (over y, core), tensor: 16 (over z, x).
Axes of the slice: x: 4, y: 4, z: 4, core: 2. Of those that a mesh axis runs over, the one named last changes fastest.
Arguments:
- tokens: bfloat16 [4096, 4096], P('group', 'tensor'), may hold values from -11 to 11
- w_query: bfloat16 [4096, 4096], P(None, 'tensor'), may hold values from -2 to 2
- w_key: bfloat16 [4096, 1024], P(None, 'tensor'), may hold values from -2 to 2
- w_value: bfloat16 [4096, 1024], P(None, 'tensor'), may hold values from -0.09375 to 0.09375
- w_out: bfloat16 [4096, 4096], P('tensor'), may hold values from -0.09375 to 0.09375
- out_grad: bfloat16 [4096, 4096], P('group', 'tensor'), may hold values from -6 to 6
- lengths: int32 [4], replicated, may hold values from 1 to 3584, 4096 in all
- kv_first: int32 [16], replicated, may hold values from 0 to 7, as said below
Outputs:
- mixed: bfloat16 [4096, 4096], P('group', 'tensor')
- tokens_grad: bfloat16 [4096, 4096], P('group', 'tensor')
The draws below stay inside these ranges and needn't reach their ends.
Inputs may be any that keep to these rules, and one draw needn't show every extreme that they name: kv_first of query block b lies between 0 and b, and for b >= 8 between 0 and b - 8.
All inputs are finite; a program needn't handle non-finite values.
Results may differ from the reference program's by a relative error of at most 0.027.
Values may be sent and summed in bfloat16 or wider, within the bound.
A program may use at most 128 MiB of HBM per device.

```python
import math
import jax
import jax.numpy as jnp
import numpy as np
from jax import lax

D = 4096
HEADS = 32
KV_HEADS = 8
HD = 128
DOCS = 4
QB = 256
TOKENS = 4096
QBLOCKS = 16
DOC_MAX = 3584


def common_columns(key):
    return jnp.clip(jax.random.normal(key, (D, KV_HEADS * HD), jnp.float32), -6.0, 6.0)


def blend_weights(common, fresh, portion):
    return (portion ** 0.5 * common + (1.0 - portion) ** 0.5 * fresh) * D ** (-0.5)


def draw_w_query(key, part):
    common = common_columns(key)
    key = jax.random.fold_in(key, 11)
    share = HEADS // KV_HEADS
    portion = 0.4
    fresh = jnp.clip(jax.random.normal(key, (D, HEADS * HD), jnp.float32), -6.0, 6.0)
    spread = jnp.broadcast_to(common.reshape(D, KV_HEADS, 1, HD), (D, KV_HEADS, share, HD)).reshape(D, HEADS * HD)
    return blend_weights(spread, fresh, portion).astype(jnp.bfloat16)


def draw_w_key(key, part):
    common = common_columns(key)
    key = jax.random.fold_in(key, 13)
    portion = 0.4
    fresh = jnp.clip(jax.random.normal(key, (D, KV_HEADS * HD), jnp.float32), -6.0, 6.0)
    return blend_weights(common, fresh, portion).astype(jnp.bfloat16)


def draw_tokens(key, part):
    key = jax.random.fold_in(key, 5)
    noise_key = jax.random.fold_in(key, 0)
    sign_key = jax.random.fold_in(key, 1)
    amp_key = jax.random.fold_in(key, 2)
    pair_key = jax.random.fold_in(key, 3)
    top_key = jax.random.fold_in(key, 5)
    rough = jnp.clip(jax.random.normal(noise_key, (TOKENS, D), jnp.float32), -6.0, 6.0)
    amp_low = 4.0
    amp_high = 8.0
    pair_count = 3
    signs = jnp.where(jax.random.bernoulli(sign_key, 0.5, (pair_count, D)), 1.0, -1.0).astype(jnp.float32)
    strength = jax.random.uniform(amp_key, (pair_count,), jnp.float32, amp_low, amp_high)
    top = amp_high * jax.random.uniform(top_key, (), jnp.float32, 0.97, 1.0)
    strength = jnp.where(jnp.arange(pair_count) == 0, top, strength)
    second = strength * jax.random.uniform(pair_key, (pair_count,), jnp.float32, 0.99, 1.0)
    rows = jnp.arange(TOKENS, dtype=jnp.int32)
    back = (TOKENS - 1 - rows).astype(jnp.int32)
    planted = back < 2 * pair_count
    pair = jnp.minimum(back // 2, pair_count - 1).astype(jnp.int32)
    later = back % 2 == 0
    amplitude = jnp.where(later, second[pair], strength[pair])
    direction = signs[pair]
    result = jnp.where(planted[:, None], amplitude[:, None] * direction + 0.5 * rough, rough)
    return result.astype(jnp.bfloat16)


def draw_out_grad(key, part):
    key = jax.random.fold_in(key, 17)
    values = jnp.clip(jax.random.normal(key, (TOKENS, D), jnp.float32), -6.0, 6.0)
    rows = jnp.arange(TOKENS, dtype=jnp.int32)
    factor = jnp.where(rows >= TOKENS - 6, 0.1, 1.0).astype(jnp.float32)
    return (values * factor[:, None]).astype(jnp.bfloat16)


def draw_kv_first(key, part):
    key = jax.random.fold_in(key, 7)
    raw = jax.random.randint(key, (QBLOCKS,), 0, 1 << 20, dtype=jnp.int32)
    indices = jnp.arange(QBLOCKS, dtype=jnp.int32)
    middle = QBLOCKS // 2
    early = (raw % (indices + 1)).astype(jnp.int32)
    late = (raw % jnp.maximum(indices - middle + 1, 1)).astype(jnp.int32)
    firsts = jnp.where(indices >= middle, late, early)
    return jnp.where(indices == middle - 1, indices, firsts).astype(jnp.int32)


def block_scale(key, extent, shards, low, high):
    loudness = 1.0
    for position, blocks in shards:
        steps = jax.random.uniform(jax.random.fold_in(jax.random.fold_in(key, 6), position), (blocks,), jnp.float32, low / len(shards), high / len(shards))
        loudness = loudness * jnp.repeat(jnp.exp(steps), extent[position] // blocks).reshape((-1,) + (1,) * (len(extent) - 1 - position))
    return loudness


def profile(amount, total, reach, skew):
    weights = [(1 << 20) // math.isqrt(rank ** skew) + 1 for rank in range(2, amount + 1)]
    spare, given = total - reach - (amount - 1), [1] * (amount - 1)
    while spare > 0:
        candidates = [i for i in range(amount - 1) if given[i] < reach]
        whole, budget = sum([weights[i] for i in candidates]), spare
        for i in candidates:
            addition = min(reach - given[i], max(1, budget * weights[i] // whole), spare)
            given[i] = given[i] + addition
            spare = spare - addition
    return np.array([reach] + given)


def ragged_sizes(key, count, total, limit, skew):
    if count == 2:
        one = jax.random.randint(key, (), max(1, total - limit), min(limit, total - 1) + 1)
        return jnp.stack([one, total - one])
    sizes = jnp.asarray(profile(count, total, limit, skew), jnp.int32)
    twos = (count - 1) // 2
    giver, taker = sizes[1:1 + 2 * twos:2], sizes[2:2 + 2 * twos:2]
    room = jnp.minimum(giver - 1, limit - taker)
    passed = jax.random.randint(jax.random.fold_in(key, 1), (twos,), 0, 1 << 20) % (room + 1)
    sizes = sizes.at[1:1 + 2 * twos:2].set(giver - passed).at[2:2 + 2 * twos:2].set(taker + passed)
    return sizes[jax.random.permutation(jax.random.fold_in(key, 2), count)]


def noise(rng, shape, scale, bound, cuts=(), held_as=jnp.bfloat16):
    drawn = jax.random.normal(rng, shape, jnp.float32) * scale
    if len(cuts) > 0:
        drawn = block_scale(rng, shape, cuts, -0.22, 0.18) * drawn
    return jnp.clip(drawn, min=-bound, max=bound).astype(held_as)


def setup_inputs(seed: int = 0) -> dict:
    key_list = jax.random.split(jax.random.key(seed), 9)
    tokens = draw_tokens(jax.random.fold_in(key_list[8], 71), 0)
    w_query = draw_w_query(jax.random.fold_in(key_list[8], 71), 0)
    w_key = draw_w_key(jax.random.fold_in(key_list[8], 71), 0)
    w_value = noise(key_list[3], (D, KV_HEADS * HD), D ** -0.5, 0.09375, ((1, 16),))
    w_out = noise(key_list[4], (HEADS * HD, D), (HEADS * HD) ** -0.5, 0.09375, ((0, 16),))
    out_grad = draw_out_grad(jax.random.fold_in(key_list[8], 71), 0)
    lengths = ragged_sizes(key_list[6], DOCS, TOKENS, DOC_MAX, 0).astype(jnp.int32)
    kv_first = draw_kv_first(jax.random.fold_in(key_list[8], 71), 0)
    return dict(tokens=tokens, w_query=w_query, w_key=w_key, w_value=w_value, w_out=w_out, out_grad=out_grad, lengths=lengths, kv_first=kv_first)


def reference(tokens, w_query, w_key, w_value, w_out, out_grad, lengths, kv_first):
    scale = HD ** -0.5
    share = HEADS // KV_HEADS
    queries = jnp.dot(tokens, w_query, preferred_element_type=jnp.float32).astype(jnp.bfloat16).reshape(TOKENS, HEADS, HD)
    keys = jnp.dot(tokens, w_key, preferred_element_type=jnp.float32).astype(jnp.bfloat16).reshape(TOKENS, KV_HEADS, HD)
    values = jnp.dot(tokens, w_value, preferred_element_type=jnp.float32).astype(jnp.bfloat16).reshape(TOKENS, KV_HEADS, HD)
    keys_rep = jnp.repeat(keys, share, axis=1).astype(jnp.float32)
    values_rep = jnp.repeat(values, share, axis=1).astype(jnp.float32)
    positions = jnp.arange(TOKENS, dtype=jnp.int32)
    ends = jnp.cumsum(lengths).astype(jnp.int32)
    segments = jnp.sum((positions[:, None] >= ends[None, :]).astype(jnp.int32), axis=1).astype(jnp.int32)

    def block_parts(block):
        start = (block * QB).astype(jnp.int32)
        query_blk = lax.dynamic_slice_in_dim(queries, start, QB, 0)
        pos_query = start + jnp.arange(QB, dtype=jnp.int32)
        seg_query = lax.dynamic_slice_in_dim(segments, start, QB, 0)
        visible = (seg_query[:, None] == segments[None, :]) & (positions[None, :] <= pos_query[:, None])
        visible = visible & (positions[None, :] >= (kv_first[block] * QB).astype(jnp.int32))
        logits = jnp.einsum('qhd,khd->hqk', query_blk.astype(jnp.float32), keys_rep) * scale
        shown = visible[None, :, :]
        peak = jnp.max(jnp.where(shown, logits, -1e30), axis=-1)
        total = jnp.sum(jnp.where(shown, jnp.exp(logits - peak[..., None]), 0.0), axis=-1)
        lse = peak + jnp.log(total)
        prob = jnp.where(shown, jnp.exp(logits - lse[..., None]), 0.0)
        return query_blk, prob

    def forward(block):
        query_blk, prob = block_parts(block)
        weights = prob.astype(jnp.bfloat16)
        return jnp.einsum('hqk,khd->qhd', weights.astype(jnp.float32), values_rep).astype(jnp.bfloat16)

    blocks = jnp.arange(QBLOCKS, dtype=jnp.int32)
    attended = lax.map(forward, blocks).reshape(TOKENS, HEADS * HD)
    mixed = jnp.dot(attended, w_out, preferred_element_type=jnp.float32).astype(jnp.bfloat16)
    head_grad = jnp.dot(out_grad, w_out.T, preferred_element_type=jnp.float32).astype(jnp.bfloat16).reshape(TOKENS, HEADS, HD)
    attended_heads = attended.reshape(TOKENS, HEADS, HD)

    def backward(carry, block):
        key_acc, value_acc = carry
        query_blk, prob = block_parts(block)
        start = (block * QB).astype(jnp.int32)
        grad_blk = lax.dynamic_slice_in_dim(head_grad, start, QB, 0).astype(jnp.float32)
        out_blk = lax.dynamic_slice_in_dim(attended_heads, start, QB, 0).astype(jnp.float32)
        delta = jnp.sum(grad_blk * out_blk, axis=-1).T
        dprob = jnp.einsum('qhd,khd->hqk', grad_blk, values_rep)
        score_grad = ((prob * (dprob - delta[..., None])) * scale).astype(jnp.bfloat16).astype(jnp.float32)
        weights = prob.astype(jnp.bfloat16).astype(jnp.float32)
        query_grad = jnp.einsum('hqk,khd->qhd', score_grad, keys_rep)
        key_part = jnp.einsum('hqk,qhd->khd', score_grad, query_blk.astype(jnp.float32))
        value_part = jnp.einsum('hqk,qhd->khd', weights, grad_blk)
        key_part = key_part.reshape(TOKENS, KV_HEADS, share, HD).sum(axis=2)
        value_part = value_part.reshape(TOKENS, KV_HEADS, share, HD).sum(axis=2)
        return (key_acc + key_part, value_acc + value_part), query_grad.astype(jnp.bfloat16)

    empty = jnp.zeros((TOKENS, KV_HEADS, HD), jnp.float32)
    (key_acc, value_acc), query_grads = lax.scan(backward, (empty, empty), blocks)
    query_grad = query_grads.reshape(TOKENS, HEADS * HD)
    key_grad = key_acc.reshape(TOKENS, KV_HEADS * HD).astype(jnp.bfloat16)
    value_grad = value_acc.reshape(TOKENS, KV_HEADS * HD).astype(jnp.bfloat16)
    summed = jnp.dot(query_grad, w_query.T, preferred_element_type=jnp.float32)
    summed = summed + jnp.dot(key_grad, w_key.T, preferred_element_type=jnp.float32)
    summed = summed + jnp.dot(value_grad, w_value.T, preferred_element_type=jnp.float32)
    return mixed, summed.astype(jnp.bfloat16)
```

```python
import jax
import jax.numpy as jnp
from jax import lax
from jax.experimental import pallas as pl
from jax.experimental.pallas import tpu as pltpu
from jax.sharding import PartitionSpec as P

HD = 128
MESH = pl.DeviceIdType.MESH
F32 = jnp.float32
BF16 = jnp.bfloat16


def dot(a, b, ca=1, cb=0):
    return lax.dot_general(a, b, (((ca,), (cb,)), ((), ())), preferred_element_type=F32)


class Place:
    def __init__(self):
        self.g = lax.axis_index("group")
        self.t = lax.axis_index("tensor")
        self.y, self.core = self.g // 2, self.g % 2
        self.z, self.x = self.t // 4, self.t % 4

    def tensor(self, dz, dx):
        return (self.z + dz) % 4 * 4 + (self.x + dx) % 4

    def at(self, dz=0, dx=0, dy=0, dcore=0):
        return (
            (self.y + dy) % 4 * 2 + (self.core + dcore) % 2,
            self.tensor(dz, dx),
        )


def greet(place):
    barrier = pltpu.get_barrier_semaphore()
    others = [place.at(dx=1), place.at(dx=3), place.at(dz=1), place.at(dz=3)]
    others += [place.at(dy=1), place.at(dy=3), place.at(dcore=1)]
    for other in others:
        pl.semaphore_signal(barrier, inc=1, device_id=other, device_id_type=MESH)
    pl.semaphore_wait(barrier, len(others))


class Gather:
    def __init__(self, place, own, buf, send, recv):
        self.place, self.own, self.buf, self.send_sems, self.recv_sems = place, own, buf, send, recv
        self.sent = []

    @staticmethod
    def slot(h, du, dv):
        return (dv % 4) * 4 + du % 4 if h == 0 else (du % 4) * 4 + dv % 4

    @staticmethod
    def rows(h, part):
        return pl.ds(h * 256, 256) if part is None else pl.ds(h * 256 + part * 128, 128)

    def ref(self, h, du, dv, part):
        rows = self.rows(h, part)
        if du % 4 == 0 and dv % 4 == 0:
            return self.own.at[rows, :]
        return self.buf.at[self.slot(h, du, dv), rows, :]

    def push(self, h, axis, sign, du, dv, part=None):
        if axis == 0:
            tu, tv = du - sign, dv
        else:
            tu, tv = du, dv - sign
        along_x = (axis == 0) == (h == 0)
        target = self.place.at(dx=sign) if along_x else self.place.at(dz=sign)
        copy = pltpu.make_async_remote_copy(
            src_ref=self.ref(h, du, dv, part),
            dst_ref=self.buf.at[self.slot(h, tu, tv), self.rows(h, part), :],
            send_sem=self.send_sems.at[len(self.sent)],
            recv_sem=self.recv_sems.at[h, self.slot(h, tu, tv), part or 0],
            device_id=target,
            device_id_type=MESH,
        )
        copy.start()
        self.sent.append(copy)

    def arrive(self, h, du, dv, part=None):
        ref = self.buf.at[self.slot(h, du, dv), self.rows(h, part), :]
        pltpu.make_async_remote_copy(
            src_ref=ref,
            dst_ref=ref,
            send_sem=self.send_sems.at[0],
            recv_sem=self.recv_sems.at[h, self.slot(h, du, dv), part or 0],
            device_id=self.place.at(dx=1),
            device_id_type=MESH,
        ).wait_recv()

    def far(self, h, axis, du, dv, sign):
        self.push(h, axis, sign, du, dv, 0 if sign == 1 else 1)

    def stage0(self):
        for h in (0, 1):
            for s in (1, -1):
                self.push(h, 0, s, 0, 0)
        for h in (0, 1):
            for s in (1, -1):
                self.push(h, 1, s, 0, 0)

    def stage1(self):
        for s in (1, -1):
            for h in (0, 1):
                self.arrive(h, -s, 0)
                self.far(h, 0, -s, 0, s)
                for w in (1, -1):
                    self.push(h, 1, w, -s, 0)
        for s in (1, -1):
            for h in (0, 1):
                self.arrive(h, 0, -s)
                self.far(h, 1, 0, -s, s)

    def stage2(self):
        for h in (0, 1):
            for part in (0, 1):
                self.arrive(h, 2, 0, part)
            for w in (1, -1):
                self.push(h, 1, w, 2, 0)
        for s in (1, -1):
            for w in (1, -1):
                for h in (0, 1):
                    self.arrive(h, -s, -w)
                    self.far(h, 1, -s, -w, w)

    def stage3(self):
        for w in (1, -1):
            for h in (0, 1):
                self.arrive(h, 2, -w)
                self.far(h, 1, 2, -w, w)

    def stage4(self, du):
        for h in (0, 1):
            for part in (0, 1):
                self.arrive(h, du, 2, part)

    def finish(self):
        for copy in self.sent:
            copy.wait_send()


GATHER_SEMS = [pltpu.SemaphoreType.DMA((40,)), pltpu.SemaphoreType.DMA((2, 16, 2))]

READY = [
    [(0, 0)],
    [(1, 0), (3, 0), (0, 1), (0, 3)],
    [(2, 0), (1, 1), (1, 3), (3, 1), (3, 3)],
    [(2, 1), (2, 3)],
    [(0, 2), (1, 2), (2, 2), (3, 2)],
]


def kernel_one(
    tok, wq, wk, wv, wo, og, q_out, kv_out, hg_out,
    xbuf, gbuf, wall, wkt, wvt, wot, acc, hacc, xs, xr, gs, gr, lsem,
):
    place = Place()
    loads = [
        pltpu.make_async_copy(tok, xbuf.at[0], lsem.at[0]),
        pltpu.make_async_copy(wk, wkt, lsem.at[1]),
        pltpu.make_async_copy(wv, wvt, lsem.at[2]),
        pltpu.make_async_copy(wq, wall.at[:, pl.ds(0, 256)], lsem.at[3]),
        pltpu.make_async_copy(og, gbuf.at[0], lsem.at[4]),
        pltpu.make_async_copy(wo, wot, lsem.at[5]),
    ]
    for load in loads:
        load.start()
    greet(place)
    xg = Gather(place, tok, xbuf, xs, xr)
    gg = Gather(place, og, gbuf, gs, gr)
    xg.stage0()
    loads[1].wait()
    loads[2].wait()

    def join(i, _):
        rows = pl.ds(pl.multiple_of(i * 256, 256), 256)
        wall[rows, 256:384] = jnp.concatenate([wkt[rows, :], wvt[rows, :]], axis=1)
        return 0

    lax.fori_loop(0, 16, join, 0)
    loads[0].wait()
    loads[3].wait()

    def project(pairs, first=False):
        for h in (0, 1):
            rows = pl.ds(h * 256, 256)
            total = None
            for du, dv in pairs:
                slot = Gather.slot(h, du, dv)
                chunk = place.tensor(slot // 4, slot % 4)
                depth = pl.ds(pl.multiple_of(chunk * 256, 256), 256)
                part = dot(xbuf[slot, rows, :], wall[depth, :])
                total = part if total is None else total + part
            acc[rows, :] = total if first else acc[rows, :] + total

    def cotangent(pairs, first=False):
        for h in (0, 1):
            rows = pl.ds(h * 256, 256)
            total = None
            for du, dv in pairs:
                slot = Gather.slot(h, du, dv)
                chunk = place.tensor(slot // 4, slot % 4)
                depth = pl.ds(pl.multiple_of(chunk * 256, 256), 256)
                part = dot(gbuf[slot, rows, :], wot[:, depth], 1, 1)
                total = part if total is None else total + part
            hacc[rows, :] = total if first else hacc[rows, :] + total

    project(READY[0], True)
    xg.stage1()
    project(READY[1])
    xg.stage2()
    gg.stage0()
    project(READY[2])
    xg.stage3()
    project(READY[3])
    loads[4].wait()
    loads[5].wait()
    cotangent(READY[0], True)
    for du in range(4):
        xg.stage4(du)
    project(READY[4])
    gg.stage1()
    q_out[...] = acc[:, 0:256].astype(BF16)
    kv_out[...] = acc[:, 256:384].astype(BF16)
    cotangent(READY[1])
    gg.stage2()
    cotangent(READY[2])
    gg.stage3()
    cotangent(READY[3])
    for du in range(4):
        gg.stage4(du)
    cotangent(READY[4])
    hg_out[...] = hacc[...].astype(BF16)
    xg.finish()
    gg.finish()


def gather_project(tokens, w_query, w_key, w_value, w_out, out_grad):
    return pl.pallas_call(
        kernel_one,
        out_shape=(
            jax.ShapeDtypeStruct((512, 256), BF16),
            jax.ShapeDtypeStruct((512, 128), BF16),
            jax.ShapeDtypeStruct((512, 256), BF16),
        ),
        in_specs=[pl.BlockSpec(memory_space=pl.ANY)] * 6,
        out_specs=[pl.BlockSpec(memory_space=pltpu.VMEM)] * 3,
        scratch_shapes=[
            pltpu.VMEM((16, 512, 256), BF16),
            pltpu.VMEM((16, 512, 256), BF16),
            pltpu.VMEM((4096, 384), BF16),
            pltpu.VMEM((4096, 64), BF16),
            pltpu.VMEM((4096, 64), BF16),
            pltpu.VMEM((256, 4096), BF16),
            pltpu.VMEM((512, 384), F32),
            pltpu.VMEM((512, 256), F32),
            *GATHER_SEMS,
            *GATHER_SEMS,
            pltpu.SemaphoreType.DMA((6,)),
        ],
        compiler_params=pltpu.CompilerParams(
            collective_id=0, has_side_effects=True, vmem_limit_bytes=40 * 1024 * 1024
        ),
        name="gather_project",
    )(tokens, w_query, w_key, w_value, w_out, out_grad)


def from_partner(value, axis, bit):
    return lax.ppermute(value, axis, [(i, i ^ 1 << bit) for i in range(lax.axis_size(axis))])


def scores_at(query_blk, key_blk, seg_query, seg_key, pos_query, pos_key):
    factor = query_blk.shape[-1] ** (-0.5)
    logits = (
        jnp.einsum("qhd,kd->hqk", query_blk, key_blk, preferred_element_type=jnp.float32) * factor
    )
    visible = (seg_query[:, None] == seg_key[None, :]) & (pos_key[None, :] <= pos_query[:, None])
    return (logits, visible[None, :, :])


def load_block(column, width, keys_all, values_all, segments):
    start = (column * width).astype(jnp.int32)
    key_blk = lax.dynamic_slice_in_dim(keys_all, start, width, 0)
    value_blk = lax.dynamic_slice_in_dim(values_all, start, width, 0)
    seg_key = lax.dynamic_slice_in_dim(segments, start, width, 0)
    return (key_blk, value_blk, seg_key, start + jnp.arange(width, dtype=jnp.int32))


def query_meta(block, width, segments):
    start = block * width
    return (
        lax.dynamic_slice_in_dim(segments, start, width, 0),
        start + jnp.arange(width, dtype=jnp.int32),
    )


def forward_block(query_blk, block, first, keys_all, values_all, segments):
    width = query_blk.shape[0]
    seg_query, pos_query = query_meta(block, width, segments)
    key_blk, value_blk, seg_key, pos_key = load_block(block, width, keys_all, values_all, segments)
    logits, visible = scores_at(query_blk, key_blk, seg_query, seg_key, pos_query, pos_key)
    running = jnp.max(jnp.where(visible, logits, -1e30), axis=-1)

    def first_pass(column, carry):
        peak, total = carry
        key_blk, value_blk, seg_key, pos_key = load_block(
            column, width, keys_all, values_all, segments
        )
        logits, visible = scores_at(query_blk, key_blk, seg_query, seg_key, pos_query, pos_key)
        newpeak = jnp.maximum(peak, jnp.max(jnp.where(visible, logits, -1e30), axis=-1))
        terms = jnp.where(visible, jnp.exp(logits - newpeak[..., None]), 0.0)
        return (newpeak, total * jnp.exp(peak - newpeak) + jnp.sum(terms, axis=-1))

    peak, total = lax.fori_loop(first, block + 1, first_pass, (running, jnp.zeros_like(running)))
    lse = peak + jnp.log(total)

    def second_pass(column, accum):
        key_blk, value_blk, seg_key, pos_key = load_block(
            column, width, keys_all, values_all, segments
        )
        logits, visible = scores_at(query_blk, key_blk, seg_query, seg_key, pos_query, pos_key)
        weights = jnp.where(visible, jnp.exp(logits - lse[..., None]), 0.0).astype(jnp.bfloat16)
        return accum + jnp.einsum(
            "hqk,kd->qhd", weights, value_blk, preferred_element_type=jnp.float32
        )

    start_acc = jnp.zeros(query_blk.shape, jnp.float32)
    accum = lax.fori_loop(first, block + 1, second_pass, start_acc)
    return (accum.astype(jnp.bfloat16), lse)


def backward_block(
    query_blk,
    grad_blk,
    out_blk,
    lse,
    block,
    first,
    keys_all,
    values_all,
    segments,
    key_acc,
    value_acc,
):
    width = query_blk.shape[0]
    factor = query_blk.shape[-1] ** (-0.5)
    seg_query, pos_query = query_meta(block, width, segments)
    delta = jnp.sum(grad_blk.astype(jnp.float32) * out_blk.astype(jnp.float32), axis=-1).T

    def step(column, carry):
        query_grad, key_acc, value_acc = carry
        key_blk, value_blk, seg_key, pos_key = load_block(
            column, width, keys_all, values_all, segments
        )
        logits, visible = scores_at(query_blk, key_blk, seg_query, seg_key, pos_query, pos_key)
        prob = jnp.where(visible, jnp.exp(logits - lse[..., None]), 0.0)
        weights = prob.astype(jnp.bfloat16)
        dprob = jnp.einsum("qhd,kd->hqk", grad_blk, value_blk, preferred_element_type=jnp.float32)
        score_grad = (prob * (dprob - delta[..., None]) * factor).astype(jnp.bfloat16)
        query_grad = query_grad + jnp.einsum(
            "hqk,kd->qhd", score_grad, key_blk, preferred_element_type=jnp.float32
        )
        key_part = jnp.einsum(
            "hqk,qhd->kd", score_grad, query_blk, preferred_element_type=jnp.float32
        )
        value_part = jnp.einsum(
            "hqk,qhd->kd", weights, grad_blk, preferred_element_type=jnp.float32
        )
        start = (column * width).astype(jnp.int32)
        old_key = lax.dynamic_slice_in_dim(key_acc, start, width, 0)
        old_value = lax.dynamic_slice_in_dim(value_acc, start, width, 0)
        key_acc = lax.dynamic_update_slice_in_dim(key_acc, old_key + key_part, start, 0)
        value_acc = lax.dynamic_update_slice_in_dim(value_acc, old_value + value_part, start, 0)
        return (query_grad, key_acc, value_acc)

    start_grad = jnp.zeros(query_blk.shape, jnp.float32)
    return lax.fori_loop(first, block + 1, step, (start_grad, key_acc, value_acc))


def local(tokens, w_query, w_key, w_value, w_out, out_grad, lengths, kv_first):
    tok_rows = tokens.shape[0]
    half = tok_rows // 2
    query_cols = w_query.shape[1]
    pair_cols = w_key.shape[1]
    local_heads = query_cols // HD
    w_inputs = jnp.concatenate([w_query, w_key, w_value], axis=1)
    queries, kv_half, head_grad = gather_project(tokens, w_query, w_key, w_value, w_out, out_grad)
    key_part = kv_half[:, :pair_cols]
    value_part = kv_half[:, pair_cols:]
    lower = lax.axis_index("tensor") % 2 == 0
    other_key, other_value = from_partner((key_part, value_part), "tensor", 0)
    key_head = jnp.where(
        lower, jnp.concatenate([key_part, other_key], 1), jnp.concatenate([other_key, key_part], 1)
    )
    value_head = jnp.where(
        lower,
        jnp.concatenate([value_part, other_value], 1),
        jnp.concatenate([other_value, value_part], 1),
    )
    keys_all, values_all = (
        lax.all_gather(key_head, "group", axis=0, tiled=True),
        lax.all_gather(value_head, "group", axis=0, tiled=True),
    )
    tokens_all = keys_all.shape[0]
    positions = jnp.arange(tokens_all, dtype=jnp.int32)
    ends = jnp.cumsum(lengths)
    segments = jnp.sum((positions[:, None] >= ends[None, :]).astype(jnp.int32), axis=1)
    group_index = lax.axis_index("group")
    query_heads = queries.reshape(tok_rows, local_heads, HD)
    first_block = 2 * group_index
    moved = query_heads[half:]
    second_block = 2 * group_index + 1
    out_first, lse_first = forward_block(
        query_heads[:half], first_block, kv_first[first_block], keys_all, values_all, segments
    )
    out_second, lse_second = forward_block(
        moved, second_block, kv_first[second_block], keys_all, values_all, segments
    )
    attended = jnp.concatenate([out_first, out_second], 0).reshape(tok_rows, query_cols)
    w_slice = w_out
    mixed = (
        lax.psum_scatter(
            lax.dot_general(
                w_slice, attended, (((0,), (1,)), ((), ())), preferred_element_type=jnp.float32
            ).astype(jnp.bfloat16),
            "tensor",
            scatter_dimension=0,
            tiled=True,
        )
        .astype(jnp.float32)
        .T.astype(jnp.bfloat16)
    )
    grad_heads = head_grad.reshape(tok_rows, local_heads, HD)
    grad_second = grad_heads[half:]
    empty_keys = jnp.zeros((tokens_all, HD), jnp.float32)
    dq_first, key_acc, value_acc = backward_block(
        query_heads[:half],
        grad_heads[:half],
        out_first,
        lse_first,
        first_block,
        kv_first[first_block],
        keys_all,
        values_all,
        segments,
        empty_keys,
        empty_keys,
    )
    dq_second, key_acc, value_acc = backward_block(
        moved,
        grad_second,
        out_second,
        lse_second,
        second_block,
        kv_first[second_block],
        keys_all,
        values_all,
        segments,
        key_acc,
        value_acc,
    )
    dq_back = dq_second.astype(jnp.bfloat16)
    query_grad = jnp.concatenate([dq_first.astype(jnp.bfloat16), dq_back], 0).reshape(
        tok_rows, query_cols
    )
    own_key, own_value = (
        lax.psum_scatter(
            key_acc.astype(jnp.bfloat16), "group", scatter_dimension=0, tiled=True
        ).astype(jnp.float32),
        lax.psum_scatter(
            value_acc.astype(jnp.bfloat16), "group", scatter_dimension=0, tiled=True
        ).astype(jnp.float32),
    )
    mine_key = jnp.where(lower, own_key[:, :pair_cols], own_key[:, pair_cols:])
    mine_value = jnp.where(lower, own_value[:, :pair_cols], own_value[:, pair_cols:])
    give_key = jnp.where(lower, own_key[:, pair_cols:], own_key[:, :pair_cols])
    give_value = jnp.where(lower, own_value[:, pair_cols:], own_value[:, :pair_cols])
    got_key, got_value = (
        from_partner(give_key.astype(jnp.bfloat16), "tensor", 0).astype(give_key.dtype),
        from_partner(give_value.astype(jnp.bfloat16), "tensor", 0).astype(give_value.dtype),
    )
    key_grad = mine_key + got_key
    value_grad = mine_value + got_value
    grads_all = jnp.concatenate(
        [query_grad, key_grad.astype(jnp.bfloat16), value_grad.astype(jnp.bfloat16)], 1
    )
    w_slice = w_inputs
    tokens_grad = (
        lax.psum_scatter(
            lax.dot_general(
                w_slice, grads_all, (((1,), (1,)), ((), ())), preferred_element_type=jnp.float32
            ).astype(jnp.bfloat16),
            "tensor",
            scatter_dimension=0,
            tiled=True,
        )
        .astype(jnp.float32)
        .T.astype(jnp.bfloat16)
    )
    return (mixed, tokens_grad)


def solution(mesh):
    return jax.shard_map(
        local,
        mesh=mesh,
        in_specs=(
            P("group", "tensor"),
            P(None, "tensor"),
            P(None, "tensor"),
            P(None, "tensor"),
            P("tensor", None),
            P("group", "tensor"),
            P(),
            P(),
        ),
        out_specs=(P("group", "tensor"), P("group", "tensor")),
        check_vma=False,
    )
```

```python
import jax
import jax.numpy as jnp
from jax import lax
from jax.experimental import pallas as pl
from jax.experimental.pallas import tpu as pltpu
from jax.sharding import PartitionSpec as P

HD = 128
LOG2E = 1.4426950408889634
SCALE = HD**-0.5
MESH = pl.DeviceIdType.MESH
F32 = jnp.float32
BF16 = jnp.bfloat16


def dot(a, b, ca=1, cb=0):
    return lax.dot_general(a, b, (((ca,), (cb,)), ((), ())), preferred_element_type=F32)


class Place:
    def __init__(self):
        self.g = lax.axis_index("group")
        self.t = lax.axis_index("tensor")
        self.y, self.core = self.g // 2, self.g % 2
        self.z, self.x = self.t // 4, self.t % 4

    def tensor(self, dz, dx):
        return (self.z + dz) % 4 * 4 + (self.x + dx) % 4

    def at(self, dz=0, dx=0, dy=0, dcore=0):
        return (
            (self.y + dy) % 4 * 2 + (self.core + dcore) % 2,
            self.tensor(dz, dx),
        )


def greet(place):
    barrier = pltpu.get_barrier_semaphore()
    others = [place.at(dx=1), place.at(dx=3), place.at(dz=1), place.at(dz=3)]
    others += [place.at(dy=1), place.at(dy=3), place.at(dcore=1)]
    for other in others:
        pl.semaphore_signal(barrier, inc=1, device_id=other, device_id_type=MESH)
    pl.semaphore_wait(barrier, len(others))


class Gather:
    def __init__(self, place, own, buf, send, recv):
        self.place, self.own, self.buf, self.send_sems, self.recv_sems = place, own, buf, send, recv
        self.sent = []

    @staticmethod
    def slot(h, du, dv):
        return (dv % 4) * 4 + du % 4 if h == 0 else (du % 4) * 4 + dv % 4

    @staticmethod
    def rows(h, part):
        return pl.ds(h * 256, 256) if part is None else pl.ds(h * 256 + part * 128, 128)

    def ref(self, h, du, dv, part):
        rows = self.rows(h, part)
        if du % 4 == 0 and dv % 4 == 0:
            return self.own.at[rows, :]
        return self.buf.at[self.slot(h, du, dv), rows, :]

    def push(self, h, axis, sign, du, dv, part=None):
        if axis == 0:
            tu, tv = du - sign, dv
        else:
            tu, tv = du, dv - sign
        along_x = (axis == 0) == (h == 0)
        target = self.place.at(dx=sign) if along_x else self.place.at(dz=sign)
        copy = pltpu.make_async_remote_copy(
            src_ref=self.ref(h, du, dv, part),
            dst_ref=self.buf.at[self.slot(h, tu, tv), self.rows(h, part), :],
            send_sem=self.send_sems.at[len(self.sent)],
            recv_sem=self.recv_sems.at[h, self.slot(h, tu, tv), part or 0],
            device_id=target,
            device_id_type=MESH,
        )
        copy.start()
        self.sent.append(copy)

    def arrive(self, h, du, dv, part=None):
        ref = self.buf.at[self.slot(h, du, dv), self.rows(h, part), :]
        pltpu.make_async_remote_copy(
            src_ref=ref,
            dst_ref=ref,
            send_sem=self.send_sems.at[0],
            recv_sem=self.recv_sems.at[h, self.slot(h, du, dv), part or 0],
            device_id=self.place.at(dx=1),
            device_id_type=MESH,
        ).wait_recv()

    def far(self, h, axis, du, dv, sign):
        self.push(h, axis, sign, du, dv, 0 if sign == 1 else 1)

    def stage0(self):
        for h in (0, 1):
            for s in (1, -1):
                self.push(h, 0, s, 0, 0)
        for h in (0, 1):
            for s in (1, -1):
                self.push(h, 1, s, 0, 0)

    def stage1(self):
        for s in (1, -1):
            for h in (0, 1):
                self.arrive(h, -s, 0)
                self.far(h, 0, -s, 0, s)
                for w in (1, -1):
                    self.push(h, 1, w, -s, 0)
        for s in (1, -1):
            for h in (0, 1):
                self.arrive(h, 0, -s)
                self.far(h, 1, 0, -s, s)

    def stage2(self):
        for h in (0, 1):
            for part in (0, 1):
                self.arrive(h, 2, 0, part)
            for w in (1, -1):
                self.push(h, 1, w, 2, 0)
        for s in (1, -1):
            for w in (1, -1):
                for h in (0, 1):
                    self.arrive(h, -s, -w)
                    self.far(h, 1, -s, -w, w)

    def stage3(self):
        for w in (1, -1):
            for h in (0, 1):
                self.arrive(h, 2, -w)
                self.far(h, 1, 2, -w, w)

    def stage4(self):
        for du in range(4):
            for h in (0, 1):
                for part in (0, 1):
                    self.arrive(h, du, 2, part)

    def finish(self):
        for copy in self.sent:
            copy.wait_send()


GATHER_SEMS = [pltpu.SemaphoreType.DMA((40,)), pltpu.SemaphoreType.DMA((2, 16, 2))]

READY = [
    [(0, 0)],
    [(1, 0), (3, 0), (0, 1), (0, 3)],
    [(2, 0), (1, 1), (1, 3), (3, 1), (3, 3)],
    [(2, 1), (2, 3)],
    [(0, 2), (1, 2), (2, 2), (3, 2)],
]


class Scatter:
    def __init__(self, place, buf, far, near, send, far_sems, near_sems):
        self.place, self.buf, self.far, self.near = place, buf, far, near
        self.send_sems, self.far_sems, self.near_sems = send, far_sems, near_sems
        self.sent = []

    def where(self, h, line, offset):
        return Gather.slot(h, line, offset) if line < 4 else Gather.slot(h, offset, 0)

    def push(self, h, line, sign, src, dst, sem):
        along_x = (line == 4) == (h == 0)
        target = self.place.at(dx=sign) if along_x else self.place.at(dz=sign)
        copy = pltpu.make_async_remote_copy(
            src_ref=src,
            dst_ref=dst,
            send_sem=self.send_sems.at[len(self.sent)],
            recv_sem=sem,
            device_id=target,
            device_id_type=MESH,
        )
        copy.start()
        self.sent.append(copy)

    def arrive(self, ref, sem):
        pltpu.make_async_remote_copy(
            src_ref=ref,
            dst_ref=ref,
            send_sem=self.send_sems.at[0],
            recv_sem=sem,
            device_id=self.place.at(dx=1),
            device_id_type=MESH,
        ).wait_recv()

    def start(self, h, line):
        slot = self.where(h, line, 2)
        for part, sign in ((0, -1), (1, 1)):
            self.push(
                h, line, sign,
                self.buf.at[slot, Gather.rows(h, part), :],
                self.far.at[h, line, part],
                self.far_sems.at[h, line, part],
            )

    def pass_on(self, h, line):
        for part, sign in ((0, -1), (1, 1)):
            slot = self.where(h, line, sign)
            rows = Gather.rows(h, part)
            self.arrive(self.far.at[h, line, part], self.far_sems.at[h, line, part])
            self.buf[slot, rows, :] = (
                self.buf[slot, rows, :].astype(F32) + self.far[h, line, part].astype(F32)
            ).astype(BF16)
            self.push(
                h, line, sign,
                self.buf.at[slot, Gather.rows(h, None), :],
                self.near.at[h, line, part],
                self.near_sems.at[h, line, part],
            )

    def total(self, h, line):
        for part in (0, 1):
            self.arrive(self.near.at[h, line, part], self.near_sems.at[h, line, part])
        slot = self.where(h, line, 0)
        rows = Gather.rows(h, None)
        value = (
            self.buf[slot, rows, :].astype(F32)
            + self.near[h, line, 0].astype(F32)
            + self.near[h, line, 1].astype(F32)
        ).astype(BF16)
        return slot, rows, value

    def stage0(self):
        for line in (2, 1, 3, 0):
            for h in (0, 1):
                self.start(h, line)

    def stage1(self):
        for line in (2, 1, 3, 0):
            for h in (0, 1):
                self.pass_on(h, line)

    def stage2(self):
        for line in (2, 1, 3, 0):
            for h in (0, 1):
                slot, rows, value = self.total(h, line)
                self.buf[slot, rows, :] = value
                if line == 2:
                    self.start(h, 4)

    def stage3(self):
        for h in (0, 1):
            self.pass_on(h, 4)

    def stage4(self, out):
        for h in (0, 1):
            _, rows, value = self.total(h, 4)
            out[rows, :] = value

    def finish(self):
        for copy in self.sent:
            copy.wait_send()


SCATTER_BUFS = [pltpu.VMEM((2, 5, 2, 128, 256), BF16), pltpu.VMEM((2, 5, 2, 256, 256), BF16)]
SCATTER_SEMS = [
    pltpu.SemaphoreType.DMA((40,)),
    pltpu.SemaphoreType.DMA((2, 5, 2)),
    pltpu.SemaphoreType.DMA((2, 5, 2)),
]


class Links:
    def __init__(self, send, recv):
        self.send_sems, self.recv_sems, self.sent = send, recv, []

    def push(self, index, src, dst, target):
        copy = pltpu.make_async_remote_copy(
            src_ref=src,
            dst_ref=dst,
            send_sem=self.send_sems.at[index],
            recv_sem=self.recv_sems.at[index],
            device_id=target,
            device_id_type=MESH,
        )
        copy.start()
        self.sent.append(copy)

    def arrive(self, index, ref, source):
        pltpu.make_async_remote_copy(
            src_ref=ref,
            dst_ref=ref,
            send_sem=self.send_sems.at[index],
            recv_sem=self.recv_sems.at[index],
            device_id=source,
            device_id_type=MESH,
        ).wait_recv()

    def finish(self):
        for copy in self.sent:
            copy.wait_send()


LINK_SEMS = [pltpu.SemaphoreType.DMA((16,)), pltpu.SemaphoreType.DMA((16,))]


def layer(
    tok, wq, wk, wv, wo, og, lens, firsts, mixed_out, grad_out,
    xbuf, gbuf, wall, wkt, wvt, wot, acc, hacc,
    qs, half_own, half_got, kvall, logits, probs, att, attended_t, linv, dos, dlt, dqt, dkv, dkv16, core_in,
    yfar, ynear, give_buf, got_buf, grads, mfar, mnear, tfar, tnear,
    xs, xr, gs, gr, ms, mfs, mns, ts, tfs, tns, ks, kr, ds_, dr, lsem,
):
    place = Place()
    g, y, core = place.g, place.y, place.core
    loads = [
        pltpu.make_async_copy(tok, xbuf.at[0], lsem.at[0]),
        pltpu.make_async_copy(wk, wkt, lsem.at[1]),
        pltpu.make_async_copy(wv, wvt, lsem.at[2]),
        pltpu.make_async_copy(wq, wall.at[:, pl.ds(0, 256)], lsem.at[3]),
        pltpu.make_async_copy(og, gbuf.at[0], lsem.at[4]),
        pltpu.make_async_copy(wo, wot, lsem.at[5]),
    ]
    for load in loads:
        load.start()
    greet(place)
    xg = Gather(place, tok, xbuf, xs, xr)
    gg = Gather(place, og, gbuf, gs, gr)
    xg.stage0()
    loads[1].wait()
    loads[2].wait()

    def join(i, _):
        rows = pl.ds(pl.multiple_of(i * 256, 256), 256)
        wall[rows, 256:384] = jnp.concatenate([wkt[rows, :], wvt[rows, :]], axis=1)
        dkv[rows, :] = jnp.zeros((256, 256), F32)
        return 0

    lax.fori_loop(0, 16, join, 0)
    loads[0].wait()
    loads[3].wait()

    def span(slot):
        chunk = place.tensor(slot // 4, slot % 4)
        return pl.ds(pl.multiple_of(chunk * 256, 256), 256)

    def project(pairs, first=False):
        for h in (0, 1):
            rows = pl.ds(h * 256, 256)
            total = None
            for du, dv in pairs:
                slot = Gather.slot(h, du, dv)
                part = dot(xbuf[slot, rows, :], wall[span(slot), :])
                total = part if total is None else total + part
            acc[rows, :] = total if first else acc[rows, :] + total

    def cotangent(pairs, first=False):
        for h in (0, 1):
            rows = pl.ds(h * 256, 256)
            total = None
            for du, dv in pairs:
                slot = Gather.slot(h, du, dv)
                part = dot(gbuf[slot, rows, :], wot[:, span(slot)], 1, 1)
                total = part if total is None else total + part
            hacc[rows, :] = total if first else hacc[rows, :] + total

    project(READY[0], True)
    xg.stage1()
    project(READY[1])
    xg.stage2()
    project(READY[2])
    xg.stage3()
    project(READY[3])
    xg.stage4()
    project(READY[4])

    lower = place.t % 2 == 0
    partner = (g, place.t + 1 - 2 * (place.t % 2))
    kv = Links(ks, kr)
    own_half = acc[:, 256:384].astype(BF16)
    half_own[...] = own_half
    kv.push(0, half_own, half_got, partner)
    gg.stage0()
    qs[0] = acc[:, 0:128].astype(BF16)
    qs[1] = acc[:, 128:256].astype(BF16)
    loads[4].wait()
    loads[5].wait()
    cotangent(READY[0], True)
    kv.arrive(0, half_got, partner)
    other_half = half_got[...]
    low = jnp.where(lower, own_half, other_half)
    high = jnp.where(lower, other_half, own_half)
    kvall[g] = jnp.concatenate([low[:, 0:64], high[:, 0:64], low[:, 64:128], high[:, 64:128]], axis=1)

    def group_at(dy, dcore=0):
        return place.at(dy=dy, dcore=dcore)[0]

    sibling = place.at(dcore=1)
    up, down = place.at(dy=1), place.at(dy=3)
    first_rows, last_rows = pl.ds(0, 256), pl.ds(256, 256)
    kv.push(1, kvall.at[g], kvall.at[g], up)
    kv.push(2, kvall.at[g], kvall.at[g], down)
    kv.push(8, kvall.at[g], kvall.at[g], sibling)
    gg.stage1()
    below, above, across = group_at(3), group_at(1), group_at(2)
    kv.arrive(1, kvall.at[below], down)
    kv.push(3, kvall.at[below, first_rows, :], kvall.at[below, first_rows, :], up)
    kv.push(9, kvall.at[below], kvall.at[below], sibling)
    kv.arrive(2, kvall.at[above], up)
    kv.push(4, kvall.at[above, last_rows, :], kvall.at[above, last_rows, :], down)
    kv.push(10, kvall.at[above], kvall.at[above], sibling)
    cotangent(READY[1])
    kv.arrive(3, kvall.at[across, first_rows, :], down)
    kv.arrive(4, kvall.at[across, last_rows, :], up)
    kv.push(11, kvall.at[across], kvall.at[across], sibling)
    for index, dy in ((8, 0), (9, 3), (10, 1), (11, 2)):
        kv.arrive(index, kvall.at[group_at(dy, 1)], sibling)

    lane = lax.broadcasted_iota(jnp.int32, (1, 512), 1)
    position = lane + g * 512
    low_key = jnp.where(lane < 256, firsts[2 * g], firsts[2 * g + 1]) * 256
    end = lens[0]
    for i in range(1, 5):
        low_key = jnp.maximum(low_key, jnp.where(position >= end, end, 0))
        if i < 4:
            end = end + lens[i]
    blocks = 2 * g + 2

    def key_block(c):
        return kvall[c // 2, pl.ds(pl.multiple_of(c % 2 * 256, 256), 256), 0:128]

    def value_block(c):
        return kvall[c // 2, pl.ds(pl.multiple_of(c % 2 * 256, 256), 256), 128:256]

    def forward(h):
        def score(c, peak):
            raw = dot(key_block(c), qs[h], 1, 1) * (SCALE * LOG2E)
            key = lax.broadcasted_iota(jnp.int32, (256, 512), 0) + c * 256
            raw = jnp.where((key >= low_key) & (key <= position), raw, -1e30)
            logits[c] = raw
            return jnp.maximum(peak, jnp.max(raw, axis=0, keepdims=True))

        peak = lax.fori_loop(0, blocks, score, jnp.full((1, 512), -1e30, F32))

        def weigh(c, carry):
            total, out = carry
            prob = jnp.exp2(logits[c] - peak)
            rounded = prob.astype(BF16)
            probs[c, h] = rounded
            return (
                total + jnp.sum(prob, axis=0, keepdims=True),
                out + dot(value_block(c), rounded, 0, 0),
            )

        total, out = lax.fori_loop(
            0, blocks, weigh, (jnp.zeros((1, 512), F32), jnp.zeros((128, 512), F32))
        )
        inverse = 1.0 / total
        linv[h] = inverse
        rounded = (out * inverse).T.astype(BF16)
        attended_t[h] = (out * inverse).astype(BF16)
        att[:, h * 128 : (h + 1) * 128] = rounded

    forward(0)
    gg.stage2()
    cotangent(READY[2])
    forward(1)
    gg.stage3()
    cotangent(READY[3])

    xg.finish()
    early = [s for s in range(16) if s // 4 == 2 or s % 4 == 2]
    late = [s for s in range(16) if s not in early]
    mixed = Scatter(place, xbuf, mfar, mnear, ms, mfs, mns)

    def mix(slots):
        for slot in slots:
            xbuf[slot] = dot(att[...], wot[:, span(slot)]).astype(BF16)

    mix(early)
    gg.stage4()
    mixed.stage0()
    cotangent(READY[4])
    mix(late)

    for h in (0, 1):
        grad_t = hacc[:, h * 128 : (h + 1) * 128].T * linv[h]
        dlt[h] = jnp.sum(grad_t * attended_t[h].astype(F32), axis=0, keepdims=True)
        dos[h] = grad_t.T.astype(BF16)
        dqt[h] = jnp.zeros((128, 512), F32)

    def backward(c, _):
        keys, values = key_block(c), value_block(c)
        rows = pl.ds(pl.multiple_of(c * 256, 256), 256)
        key_part, value_part = None, None
        for h in (0, 1):
            prob = probs[c, h]
            dprob = dot(values, dos[h], 1, 1)
            score = (prob.astype(F32) * (dprob - dlt[h])).astype(BF16)
            dqt[h] += dot(keys, score, 0, 0)
            one, two = dot(score, qs[h]), dot(prob, dos[h])
            key_part = one if h == 0 else key_part + one
            value_part = two if h == 0 else value_part + two
        dkv[rows, 0:128] = key_part * SCALE
        dkv[rows, 128:256] = value_part
        return 0

    def section(i, n):
        lax.fori_loop(blocks * i // n, blocks * (i + 1) // n, backward, 0)

    section(0, 4)
    mixed.stage1()
    section(1, 4)
    section(2, 4)
    mixed.stage2()
    section(3, 4)

    kvg = Links(ds_, dr)

    def narrow(dy, dcore):
        group = group_at(dy, dcore)
        rows = pl.ds(pl.multiple_of(group * 512, 512), 512)
        dkv16[group] = dkv[rows, :].astype(BF16)
        return group

    for dy in (2, 1, 3, 0):
        group = narrow(dy, 1)
        kvg.push(dy, dkv16.at[group], core_in.at[dy], sibling)

    def join_cores(dy):
        group = group_at(dy)
        rows = pl.ds(pl.multiple_of(group * 512, 512), 512)
        kvg.arrive(dy, core_in.at[dy], sibling)
        dkv16[group] = (dkv[rows, :] + core_in[dy].astype(F32)).astype(BF16)
        return group

    group = join_cores(2)
    kvg.push(4, dkv16.at[group, first_rows, :], yfar.at[0], down)
    kvg.push(5, dkv16.at[group, last_rows, :], yfar.at[1], up)
    mixed.stage3()
    group = join_cores(3)
    kvg.arrive(4, yfar.at[0], up)
    dkv16[group, first_rows, :] = (dkv16[group, first_rows, :].astype(F32) + yfar[0].astype(F32)).astype(BF16)
    kvg.push(6, dkv16.at[group], ynear.at[0], down)
    group = join_cores(1)
    kvg.arrive(5, yfar.at[1], down)
    dkv16[group, last_rows, :] = (dkv16[group, last_rows, :].astype(F32) + yfar[1].astype(F32)).astype(BF16)
    kvg.push(7, dkv16.at[group], ynear.at[1], up)
    for h in (0, 1):
        grads[:, h * 128 : (h + 1) * 128] = (dqt[h] * SCALE).T.astype(BF16)
    group = join_cores(0)
    kvg.arrive(6, ynear.at[0], up)
    kvg.arrive(7, ynear.at[1], down)
    summed = dkv16[group].astype(F32) + ynear[0].astype(F32) + ynear[1].astype(F32)
    low = jnp.concatenate([summed[:, 0:64], summed[:, 128:192]], axis=1)
    high = jnp.concatenate([summed[:, 64:128], summed[:, 192:256]], axis=1)
    give_buf[...] = jnp.where(lower, high, low).astype(BF16)
    kvg.push(8, give_buf, got_buf, partner)
    gg.finish()
    mixed.stage4(mixed_out)
    kvg.arrive(8, got_buf, partner)
    grads[:, 256:384] = (jnp.where(lower, low, high) + got_buf[...].astype(F32)).astype(BF16)

    final = Scatter(place, gbuf, tfar, tnear, ts, tfs, tns)

    def spread(slots):
        for slot in slots:
            gbuf[slot] = dot(grads[...], wall[span(slot), :], 1, 1).astype(BF16)

    spread(early)
    final.stage0()
    spread(late)
    final.stage1()
    final.stage2()
    final.stage3()
    final.stage4(grad_out)
    kv.finish()
    kvg.finish()
    mixed.finish()
    final.finish()


def local(*args):
    return tuple(
        pl.pallas_call(
            layer,
            out_shape=(
                jax.ShapeDtypeStruct((512, 256), BF16),
                jax.ShapeDtypeStruct((512, 256), BF16),
            ),
            in_specs=[pl.BlockSpec(memory_space=pl.ANY)] * 6
            + [pl.BlockSpec(memory_space=pltpu.SMEM)] * 2,
            out_specs=[pl.BlockSpec(memory_space=pltpu.VMEM)] * 2,
            scratch_shapes=[
                pltpu.VMEM((16, 512, 256), BF16),
                pltpu.VMEM((16, 512, 256), BF16),
                pltpu.VMEM((4096, 384), BF16),
                pltpu.VMEM((4096, 64), BF16),
                pltpu.VMEM((4096, 64), BF16),
                pltpu.VMEM((256, 4096), BF16),
                pltpu.VMEM((512, 384), F32),
                pltpu.VMEM((512, 256), F32),
                pltpu.VMEM((2, 512, 128), BF16),
                pltpu.VMEM((512, 128), BF16),
                pltpu.VMEM((512, 128), BF16),
                pltpu.VMEM((8, 512, 256), BF16),
                pltpu.VMEM((16, 256, 512), F32),
                pltpu.VMEM((16, 2, 256, 512), BF16),
                pltpu.VMEM((512, 256), BF16),
                pltpu.VMEM((2, 128, 512), BF16),
                pltpu.VMEM((2, 1, 512), F32),
                pltpu.VMEM((2, 512, 128), BF16),
                pltpu.VMEM((2, 1, 512), F32),
                pltpu.VMEM((2, 128, 512), F32),
                pltpu.VMEM((4096, 256), F32),
                pltpu.VMEM((8, 512, 256), BF16),
                pltpu.VMEM((4, 512, 256), BF16),
                pltpu.VMEM((2, 256, 256), BF16),
                pltpu.VMEM((2, 512, 256), BF16),
                pltpu.VMEM((512, 128), BF16),
                pltpu.VMEM((512, 128), BF16),
                pltpu.VMEM((512, 384), BF16),
                *SCATTER_BUFS,
                *SCATTER_BUFS,
                *GATHER_SEMS,
                *GATHER_SEMS,
                *SCATTER_SEMS,
                *SCATTER_SEMS,
                *LINK_SEMS,
                *LINK_SEMS,
                pltpu.SemaphoreType.DMA((6,)),
            ],
            compiler_params=pltpu.CompilerParams(
                collective_id=0, has_side_effects=True, vmem_limit_bytes=60 * 1024 * 1024
            ),
            name="layer",
        )(*args)
    )


def solution(mesh):
    return jax.shard_map(
        local,
        mesh=mesh,
        in_specs=(
            P("group", "tensor"),
            P(None, "tensor"),
            P(None, "tensor"),
            P(None, "tensor"),
            P("tensor", None),
            P("group", "tensor"),
            P(),
            P(),
        ),
        out_specs=(P("group", "tensor"), P("group", "tensor")),
        check_vma=False,
    )
```

```python
import jax
import jax.numpy as jnp
from jax import lax
from jax.experimental import pallas as pl
from jax.experimental.pallas import tpu as pltpu
from jax.sharding import PartitionSpec as P

HD = 128
LOG2E = 1.4426950408889634
SCALE = HD**-0.5
MESH = pl.DeviceIdType.MESH
F32 = jnp.float32
BF16 = jnp.bfloat16


def dot(a, b, ca=1, cb=0):
    return lax.dot_general(a, b, (((ca,), (cb,)), ((), ())), preferred_element_type=F32)


class Place:
    def __init__(self):
        self.g = lax.axis_index("group")
        self.t = lax.axis_index("tensor")
        self.y, self.core = self.g // 2, self.g % 2
        self.z, self.x = self.t // 4, self.t % 4

    def tensor(self, dz, dx):
        return (self.z + dz) % 4 * 4 + (self.x + dx) % 4

    def at(self, dz=0, dx=0, dy=0, dcore=0):
        return (
            (self.y + dy) % 4 * 2 + (self.core + dcore) % 2,
            self.tensor(dz, dx),
        )


def greet(place):
    barrier = pltpu.get_barrier_semaphore()
    others = [place.at(dx=1), place.at(dx=3), place.at(dz=1), place.at(dz=3)]
    others += [place.at(dy=1), place.at(dy=3), place.at(dcore=1)]
    for other in others:
        pl.semaphore_signal(barrier, inc=1, device_id=other, device_id_type=MESH)
    pl.semaphore_wait(barrier, len(others))


class Gather:
    def __init__(self, place, own, buf, send, recv):
        self.place, self.own, self.buf, self.send_sems, self.recv_sems = place, own, buf, send, recv
        self.sent = []

    @staticmethod
    def slot(h, du, dv):
        return (dv % 4) * 4 + du % 4 if h == 0 else (du % 4) * 4 + dv % 4

    @staticmethod
    def rows(h, part):
        return pl.ds(h * 256, 256) if part is None else pl.ds(h * 256 + part * 128, 128)

    def ref(self, h, du, dv, part):
        rows = self.rows(h, part)
        if du % 4 == 0 and dv % 4 == 0:
            return self.own.at[rows, :]
        return self.buf.at[self.slot(h, du, dv), rows, :]

    def push(self, h, axis, sign, du, dv, part=None):
        if axis == 0:
            tu, tv = du - sign, dv
        else:
            tu, tv = du, dv - sign
        along_x = (axis == 0) == (h == 0)
        target = self.place.at(dx=sign) if along_x else self.place.at(dz=sign)
        copy = pltpu.make_async_remote_copy(
            src_ref=self.ref(h, du, dv, part),
            dst_ref=self.buf.at[self.slot(h, tu, tv), self.rows(h, part), :],
            send_sem=self.send_sems.at[len(self.sent)],
            recv_sem=self.recv_sems.at[h, self.slot(h, tu, tv), part or 0],
            device_id=target,
            device_id_type=MESH,
        )
        copy.start()
        self.sent.append(copy)

    def arrive(self, h, du, dv, part=None):
        ref = self.buf.at[self.slot(h, du, dv), self.rows(h, part), :]
        pltpu.make_async_remote_copy(
            src_ref=ref,
            dst_ref=ref,
            send_sem=self.send_sems.at[0],
            recv_sem=self.recv_sems.at[h, self.slot(h, du, dv), part or 0],
            device_id=self.place.at(dx=1),
            device_id_type=MESH,
        ).wait_recv()

    def far(self, h, axis, du, dv, sign):
        self.push(h, axis, sign, du, dv, 0 if sign == 1 else 1)

    def stage0(self):
        for h in (0, 1):
            for s in (1, -1):
                self.push(h, 0, s, 0, 0)
        for h in (0, 1):
            for s in (1, -1):
                self.push(h, 1, s, 0, 0)

    def stage1(self):
        for s in (1, -1):
            for h in (0, 1):
                self.arrive(h, -s, 0)
                self.far(h, 0, -s, 0, s)
                for w in (1, -1):
                    self.push(h, 1, w, -s, 0)
        for s in (1, -1):
            for h in (0, 1):
                self.arrive(h, 0, -s)
                self.far(h, 1, 0, -s, s)

    def stage2(self):
        for h in (0, 1):
            for part in (0, 1):
                self.arrive(h, 2, 0, part)
            for w in (1, -1):
                self.push(h, 1, w, 2, 0)
        for s in (1, -1):
            for w in (1, -1):
                for h in (0, 1):
                    self.arrive(h, -s, -w)
                    self.far(h, 1, -s, -w, w)

    def stage3(self):
        for w in (1, -1):
            for h in (0, 1):
                self.arrive(h, 2, -w)
                self.far(h, 1, 2, -w, w)

    def stage4(self):
        for du in range(4):
            for h in (0, 1):
                for part in (0, 1):
                    self.arrive(h, du, 2, part)

    def finish(self):
        for copy in self.sent:
            copy.wait_send()


GATHER_SEMS = [pltpu.SemaphoreType.DMA((40,)), pltpu.SemaphoreType.DMA((2, 16, 2))]

READY = [
    [(0, 0)],
    [(1, 0), (3, 0), (0, 1), (0, 3)],
    [(2, 0), (1, 1), (1, 3), (3, 1), (3, 3)],
    [(2, 1), (2, 3)],
    [(0, 2), (1, 2), (2, 2), (3, 2)],
]


class Scatter:
    def __init__(self, place, buf, far, near, send, far_sems, near_sems):
        self.place, self.buf, self.far, self.near = place, buf, far, near
        self.send_sems, self.far_sems, self.near_sems = send, far_sems, near_sems
        self.sent = []

    def where(self, h, line, offset):
        return Gather.slot(h, line, offset) if line < 4 else Gather.slot(h, offset, 0)

    def push(self, h, line, sign, src, dst, sem):
        along_x = (line == 4) == (h == 0)
        target = self.place.at(dx=sign) if along_x else self.place.at(dz=sign)
        copy = pltpu.make_async_remote_copy(
            src_ref=src,
            dst_ref=dst,
            send_sem=self.send_sems.at[len(self.sent)],
            recv_sem=sem,
            device_id=target,
            device_id_type=MESH,
        )
        copy.start()
        self.sent.append(copy)

    def arrive(self, ref, sem):
        pltpu.make_async_remote_copy(
            src_ref=ref,
            dst_ref=ref,
            send_sem=self.send_sems.at[0],
            recv_sem=sem,
            device_id=self.place.at(dx=1),
            device_id_type=MESH,
        ).wait_recv()

    def start(self, h, line):
        slot = self.where(h, line, 2)
        for part, sign in ((0, -1), (1, 1)):
            self.push(
                h, line, sign,
                self.buf.at[slot, Gather.rows(h, part), :],
                self.far.at[h, line, part],
                self.far_sems.at[h, line, part],
            )

    def pass_on(self, h, line):
        for part, sign in ((0, -1), (1, 1)):
            slot = self.where(h, line, sign)
            rows = Gather.rows(h, part)
            self.arrive(self.far.at[h, line, part], self.far_sems.at[h, line, part])
            self.buf[slot, rows, :] = (
                self.buf[slot, rows, :].astype(F32) + self.far[h, line, part].astype(F32)
            ).astype(BF16)
            self.push(
                h, line, sign,
                self.buf.at[slot, Gather.rows(h, None), :],
                self.near.at[h, line, part],
                self.near_sems.at[h, line, part],
            )

    def total(self, h, line):
        for part in (0, 1):
            self.arrive(self.near.at[h, line, part], self.near_sems.at[h, line, part])
        slot = self.where(h, line, 0)
        rows = Gather.rows(h, None)
        value = (
            self.buf[slot, rows, :].astype(F32)
            + self.near[h, line, 0].astype(F32)
            + self.near[h, line, 1].astype(F32)
        ).astype(BF16)
        return slot, rows, value

    def stage0(self):
        for line in (2, 1, 3, 0):
            for h in (0, 1):
                self.start(h, line)

    def stage1(self):
        for line in (2, 1, 3, 0):
            for h in (0, 1):
                self.pass_on(h, line)

    def stage2(self):
        for line in (2, 1, 3, 0):
            for h in (0, 1):
                slot, rows, value = self.total(h, line)
                self.buf[slot, rows, :] = value
                if line == 2:
                    self.start(h, 4)

    def stage3(self):
        for h in (0, 1):
            self.pass_on(h, 4)

    def stage4(self, out):
        for h in (0, 1):
            _, rows, value = self.total(h, 4)
            out[rows, :] = value

    def finish(self):
        for copy in self.sent:
            copy.wait_send()


SCATTER_BUFS = [pltpu.VMEM((2, 5, 2, 128, 256), BF16), pltpu.VMEM((2, 5, 2, 256, 256), BF16)]
SCATTER_SEMS = [
    pltpu.SemaphoreType.DMA((40,)),
    pltpu.SemaphoreType.DMA((2, 5, 2)),
    pltpu.SemaphoreType.DMA((2, 5, 2)),
]


class Links:
    def __init__(self, send, recv):
        self.send_sems, self.recv_sems, self.sent = send, recv, []

    def push(self, index, src, dst, target):
        copy = pltpu.make_async_remote_copy(
            src_ref=src,
            dst_ref=dst,
            send_sem=self.send_sems.at[index],
            recv_sem=self.recv_sems.at[index],
            device_id=target,
            device_id_type=MESH,
        )
        copy.start()
        self.sent.append(copy)

    def arrive(self, index, ref, source):
        pltpu.make_async_remote_copy(
            src_ref=ref,
            dst_ref=ref,
            send_sem=self.send_sems.at[index],
            recv_sem=self.recv_sems.at[index],
            device_id=source,
            device_id_type=MESH,
        ).wait_recv()

    def finish(self):
        for copy in self.sent:
            copy.wait_send()


LINK_SEMS = [pltpu.SemaphoreType.DMA((16,)), pltpu.SemaphoreType.DMA((16,))]


def each(items, body):
    def step(i, _):
        item = items[0]
        for j in range(1, len(items)):
            item = jnp.where(i == j, items[j], item)
        body(item)
        return 0

    lax.fori_loop(0, len(items), step, 0)


def layer(
    tok, wq, wk, wv, wo, og, lens, firsts, mixed_out, grad_out,
    xbuf, gbuf, wqt, wkv, wot, acc, kacc, hacc,
    qs, kvall, logits, probs, peak, sums, outs, att, dos, dlt, dqt, dkv16, core_in,
    yfar, ynear, grads, mfar, mnear, tfar, tnear,
    xs, xr, gs, gr, ms, mfs, mns, ts, tfs, tns, ws, wr, ks, kr, ds_, dr, lsem,
):
    place = Place()
    g = place.g
    half = place.t % 2
    own_rows = pl.ds(pl.multiple_of(half * 64, 64), 64)
    other_rows = pl.ds(pl.multiple_of((1 - half) * 64, 64), 64)
    loads = [
        pltpu.make_async_copy(wk, wkv.at[0, own_rows, :], lsem.at[1]),
        pltpu.make_async_copy(wv, wkv.at[1, own_rows, :], lsem.at[2]),
        pltpu.make_async_copy(tok, xbuf.at[0], lsem.at[0]),
        pltpu.make_async_copy(wq, wqt, lsem.at[3]),
        pltpu.make_async_copy(og, gbuf.at[0], lsem.at[4]),
        pltpu.make_async_copy(wo, wot, lsem.at[5]),
    ]
    for load in loads:
        load.start()
    greet(place)
    xg = Gather(place, tok, xbuf, xs, xr)
    gg = Gather(place, og, gbuf, gs, gr)
    xg.stage0()

    def group_at(dy, dcore=0):
        return place.at(dy=dy, dcore=dcore)[0]

    partner = (g, place.t + 1 - 2 * half)
    sibling = place.at(dcore=1)
    up, down = place.at(dy=1), place.at(dy=3)
    below, above, across = group_at(3), group_at(1), group_at(2)
    sib_own, sib_below, sib_above, sib_across = (group_at(dy, 1) for dy in (0, 3, 1, 2))
    first_rows, last_rows = pl.ds(0, 256), pl.ds(256, 256)

    def slice_of(rows, group, kind=None):
        columns = pl.ds(pl.multiple_of(group * 512, 512), 512)
        return wkv.at[pl.ds(0, 2) if kind is None else kind, rows, columns]

    wl = Links(ws, wr)
    loads[0].wait()
    loads[1].wait()
    wl.push(0, slice_of(own_rows, g), slice_of(own_rows, g), partner)

    def weights_one():
        ref = slice_of(other_rows, g)
        wl.arrive(0, ref, partner)
        wl.push(1, ref, ref, up)
        wl.push(2, ref, ref, down)
        wl.push(8, ref, ref, sibling)

    def weights_two():
        ref = slice_of(other_rows, below)
        wl.arrive(1, ref, down)
        wl.push(3, slice_of(other_rows, below, 0), slice_of(other_rows, below, 0), up)
        wl.push(9, ref, ref, sibling)
        ref = slice_of(other_rows, above)
        wl.arrive(2, ref, up)
        wl.push(4, slice_of(other_rows, above, 1), slice_of(other_rows, above, 1), down)
        wl.push(10, ref, ref, sibling)

    def weights_three():
        wl.arrive(3, slice_of(other_rows, across, 0), down)
        wl.arrive(4, slice_of(other_rows, across, 1), up)
        ref = slice_of(other_rows, across)
        wl.push(11, ref, ref, sibling)

    def weights_four():
        for index, group in ((8, sib_own), (9, sib_below), (10, sib_above), (11, sib_across)):
            wl.arrive(index, slice_of(other_rows, group), sibling)

    def clear(i, _):
        dkv16[i] = jnp.zeros((512, 256), BF16)
        return 0

    lax.fori_loop(0, 8, clear, 0)
    loads[2].wait()
    loads[3].wait()

    def span(slot):
        chunk = place.tensor(slot // 4, slot % 4)
        return pl.ds(pl.multiple_of(chunk * 256, 256), 256)

    def head_weights(slot):
        return wkv[:, :, span(slot)].reshape(256, 256)

    def gathered(total_ref, buf, weight, cb, pairs, first=False):
        for h in (0, 1):
            rows = pl.ds(h * 256, 256)
            total = None
            for du, dv in pairs:
                slot = Gather.slot(h, du, dv)
                part = dot(buf[slot, rows, :], weight(slot), 1, cb)
                total = part if total is None else total + part
            total_ref[rows, :] = total if first else total_ref[rows, :] + total

    def project(pairs, first=False):
        gathered(acc, xbuf, lambda slot: wqt[span(slot), :], 0, pairs, first)

    def project_kv(pairs, first=False):
        gathered(kacc, xbuf, head_weights, 1, pairs, first)

    def cotangent(pairs, first=False):
        gathered(hacc, gbuf, lambda slot: wot[:, span(slot)], 1, pairs, first)

    project(READY[0], True)
    xg.stage1()
    weights_one()
    project(READY[1])
    xg.stage2()
    weights_two()
    gg.stage0()
    project(READY[2])
    xg.stage3()
    weights_three()
    project(READY[3])
    weights_four()
    project_kv(READY[0], True)
    project_kv(READY[1])
    project_kv(READY[2])
    project_kv(READY[3])
    xg.stage4()
    project_kv(READY[4])

    kv = Links(ks, kr)
    kvall[g] = kacc[...].astype(BF16)
    kv.push(1, kvall.at[g], kvall.at[g], up)
    kv.push(2, kvall.at[g], kvall.at[g], down)
    kv.push(8, kvall.at[g], kvall.at[g], sibling)
    project(READY[4])
    qs[0] = acc[:, 0:128].astype(BF16)
    qs[1] = acc[:, 128:256].astype(BF16)
    loads[4].wait()
    loads[5].wait()

    lane = lax.broadcasted_iota(jnp.int32, (1, 512), 1)
    position = lane + g * 512
    low_key = jnp.where(lane < 256, firsts[2 * g], firsts[2 * g + 1]) * 256
    end = lens[0]
    for i in range(1, 5):
        low_key = jnp.maximum(low_key, jnp.where(position >= end, end, 0))
        if i < 4:
            end = end + lens[i]
    for h in (0, 1):
        peak[h] = jnp.full((1, 512), -1e30, F32)
        sums[h] = jnp.zeros((1, 512), F32)
        outs[h] = jnp.zeros((128, 512), F32)
        dqt[h] = jnp.zeros((128, 512), F32)

    def score(k):
        @pl.when(k <= g)
        def _():
            key = lax.broadcasted_iota(jnp.int32, (512, 512), 0) + k * 512
            visible = (key >= low_key) & (key <= position)
            for h in (0, 1):
                raw = dot(kvall[k, :, 0:128], qs[h], 1, 1) * (SCALE * LOG2E)
                raw = jnp.where(visible, raw, -1e30)
                logits[k, h] = raw
                peak[h] = jnp.maximum(peak[h], jnp.max(raw, axis=0, keepdims=True))

    def weigh(k, _):
        for h in (0, 1):
            prob = jnp.exp2(logits[k, h] - peak[h])
            rounded = prob.astype(BF16)
            probs[k, h] = rounded
            sums[h] += jnp.sum(prob, axis=0, keepdims=True)
            outs[h] += dot(kvall[k, :, 128:256], rounded, 0, 0)
        return 0

    each([g], score)
    gg.stage1()
    kv.arrive(1, kvall.at[below], down)
    kv.push(3, kvall.at[below, first_rows, :], kvall.at[below, first_rows, :], up)
    kv.push(9, kvall.at[below], kvall.at[below], sibling)
    kv.arrive(2, kvall.at[above], up)
    kv.push(4, kvall.at[above, last_rows, :], kvall.at[above, last_rows, :], down)
    kv.push(10, kvall.at[above], kvall.at[above], sibling)
    kv.arrive(8, kvall.at[sib_own], sibling)
    each([sib_own, below, above], score)
    cotangent(READY[0], True)
    cotangent(READY[1])
    kv.arrive(3, kvall.at[across, first_rows, :], down)
    kv.arrive(4, kvall.at[across, last_rows, :], up)
    kv.push(11, kvall.at[across], kvall.at[across], sibling)
    kv.arrive(9, kvall.at[sib_below], sibling)
    kv.arrive(10, kvall.at[sib_above], sibling)
    gg.stage2()
    each([sib_below, sib_above, across], score)
    cotangent(READY[2])
    kv.arrive(11, kvall.at[sib_across], sibling)
    each([sib_across], score)
    gg.stage3()
    lax.fori_loop(0, g + 1, weigh, 0)

    for h in (0, 1):
        inverse = 1.0 / sums[h]
        sums[h] = inverse
        outs[h] = outs[h] * inverse
        att[:, h * 128 : (h + 1) * 128] = outs[h].T.astype(BF16)

    xg.finish()
    early = [s for s in range(16) if s // 4 == 2 or s % 4 == 2]
    late = [s for s in range(16) if s not in early]
    mixed = Scatter(place, xbuf, mfar, mnear, ms, mfs, mns)

    def mix(slots):
        for slot in slots:
            xbuf[slot] = dot(att[...], wot[:, span(slot)]).astype(BF16)

    mix(early)
    gg.stage4()
    mixed.stage0()
    cotangent(READY[3])
    cotangent(READY[4])
    mix(late)

    for h in (0, 1):
        grad_t = hacc[:, h * 128 : (h + 1) * 128].T * sums[h]
        out_t = outs[h].astype(BF16).astype(F32)
        dlt[h] = jnp.sum(grad_t * out_t, axis=0, keepdims=True)
        dos[h] = grad_t.T.astype(BF16)

    def backward(k):
        @pl.when(k <= g)
        def _():
            keys, values = kvall[k, :, 0:128], kvall[k, :, 128:256]
            key_part, value_part = None, None
            for h in (0, 1):
                prob = probs[k, h]
                dprob = dot(values, dos[h], 1, 1)
                grad = (prob.astype(F32) * (dprob - dlt[h])).astype(BF16)
                dqt[h] += dot(keys, grad, 0, 0)
                one, two = dot(grad, qs[h]), dot(prob, dos[h])
                key_part = one if h == 0 else key_part + one
                value_part = two if h == 0 else value_part + two
            dkv16[k, :, 0:128] = (key_part * SCALE).astype(BF16)
            dkv16[k, :, 128:256] = value_part.astype(BF16)

    kvg = Links(ds_, dr)

    def to_sibling(dy, group):
        kvg.push(dy, dkv16.at[group], core_in.at[dy], sibling)

    def join_cores(dy, group):
        kvg.arrive(dy, core_in.at[dy], sibling)
        dkv16[group] = (dkv16[group].astype(F32) + core_in[dy].astype(F32)).astype(BF16)

    def add_far(part, group, rows, source):
        kvg.arrive(4 + part, yfar.at[part], source)
        dkv16[group, rows, :] = (dkv16[group, rows, :].astype(F32) + yfar[part].astype(F32)).astype(BF16)

    each([sib_across, across], backward)
    to_sibling(2, sib_across)
    join_cores(2, across)
    kvg.push(4, dkv16.at[across, first_rows, :], yfar.at[0], down)
    kvg.push(5, dkv16.at[across, last_rows, :], yfar.at[1], up)
    mixed.stage1()
    each([sib_below, sib_above, sib_own], backward)
    to_sibling(3, sib_below)
    to_sibling(1, sib_above)
    to_sibling(0, sib_own)
    mixed.stage2()
    each([below, above], backward)
    mixed.stage3()
    join_cores(3, below)
    add_far(0, below, first_rows, up)
    kvg.push(6, dkv16.at[below], ynear.at[0], down)
    join_cores(1, above)
    add_far(1, above, last_rows, down)
    kvg.push(7, dkv16.at[above], ynear.at[1], up)
    each([g], backward)
    for h in (0, 1):
        grads[:, h * 128 : (h + 1) * 128] = (dqt[h] * SCALE).T.astype(BF16)
    gg.finish()
    join_cores(0, g)
    mixed.stage4(mixed_out)
    kvg.arrive(6, ynear.at[0], up)
    kvg.arrive(7, ynear.at[1], down)
    grads[:, 256:512] = (
        dkv16[g].astype(F32) + ynear[0].astype(F32) + ynear[1].astype(F32)
    ).astype(BF16)

    final = Scatter(place, gbuf, tfar, tnear, ts, tfs, tns)

    def spread(slots):
        for slot in slots:
            gbuf[slot] = (
                dot(grads[:, 0:256], wqt[span(slot), :], 1, 1)
                + dot(grads[:, 256:512], head_weights(slot), 1, 0)
            ).astype(BF16)

    spread(early)
    final.stage0()
    spread(late)
    final.stage1()
    final.stage2()
    final.stage3()
    final.stage4(grad_out)
    wl.finish()
    kv.finish()
    kvg.finish()
    mixed.finish()
    final.finish()


def local(tokens, w_query, w_key, w_value, w_out, out_grad, lengths, kv_first):
    return tuple(
        pl.pallas_call(
            layer,
            out_shape=(
                jax.ShapeDtypeStruct((512, 256), BF16),
                jax.ShapeDtypeStruct((512, 256), BF16),
            ),
            in_specs=[pl.BlockSpec(memory_space=pl.ANY)] * 6
            + [pl.BlockSpec(memory_space=pltpu.SMEM)] * 2,
            out_specs=[pl.BlockSpec(memory_space=pltpu.VMEM)] * 2,
            scratch_shapes=[
                pltpu.VMEM((16, 512, 256), BF16),
                pltpu.VMEM((16, 512, 256), BF16),
                pltpu.VMEM((4096, 256), BF16),
                pltpu.VMEM((2, 128, 4096), BF16),
                pltpu.VMEM((256, 4096), BF16),
                pltpu.VMEM((512, 256), F32),
                pltpu.VMEM((512, 256), F32),
                pltpu.VMEM((512, 256), F32),
                pltpu.VMEM((2, 512, 128), BF16),
                pltpu.VMEM((8, 512, 256), BF16),
                pltpu.VMEM((8, 2, 512, 512), F32),
                pltpu.VMEM((8, 2, 512, 512), BF16),
                pltpu.VMEM((2, 1, 512), F32),
                pltpu.VMEM((2, 1, 512), F32),
                pltpu.VMEM((2, 128, 512), F32),
                pltpu.VMEM((512, 256), BF16),
                pltpu.VMEM((2, 512, 128), BF16),
                pltpu.VMEM((2, 1, 512), F32),
                pltpu.VMEM((2, 128, 512), F32),
                pltpu.VMEM((8, 512, 256), BF16),
                pltpu.VMEM((4, 512, 256), BF16),
                pltpu.VMEM((2, 256, 256), BF16),
                pltpu.VMEM((2, 512, 256), BF16),
                pltpu.VMEM((512, 512), BF16),
                *SCATTER_BUFS,
                *SCATTER_BUFS,
                *GATHER_SEMS,
                *GATHER_SEMS,
                *SCATTER_SEMS,
                *SCATTER_SEMS,
                *LINK_SEMS,
                *LINK_SEMS,
                *LINK_SEMS,
                pltpu.SemaphoreType.DMA((6,)),
            ],
            compiler_params=pltpu.CompilerParams(
                collective_id=0, has_side_effects=True, vmem_limit_bytes=62 * 1024 * 1024
            ),
            name="layer",
        )(tokens, w_query, w_key.T, w_value.T, w_out, out_grad, lengths, kv_first)
    )


def solution(mesh):
    return jax.shard_map(
        local,
        mesh=mesh,
        in_specs=(
            P("group", "tensor"),
            P(None, "tensor"),
            P(None, "tensor"),
            P(None, "tensor"),
            P("tensor", None),
            P("group", "tensor"),
            P(),
            P(),
        ),
        out_specs=(P("group", "tensor"), P("group", "tensor")),
        check_vma=False,
    )
```

```python
import jax
import jax.numpy as jnp
from jax import lax
from jax.experimental import pallas as pl
from jax.experimental.pallas import tpu as pltpu
from jax.sharding import PartitionSpec as P

HD = 128
LOG2E = 1.4426950408889634
SCALE = HD**-0.5
MESH = pl.DeviceIdType.MESH
F32 = jnp.float32
BF16 = jnp.bfloat16


def dot(a, b, ca=1, cb=0):
    return lax.dot_general(a, b, (((ca,), (cb,)), ((), ())), preferred_element_type=F32)


class Place:
    def __init__(self):
        self.g = lax.axis_index("group")
        self.t = lax.axis_index("tensor")
        self.y, self.core = self.g // 2, self.g % 2
        self.z, self.x = self.t // 4, self.t % 4

    def tensor(self, dz, dx):
        return (self.z + dz) % 4 * 4 + (self.x + dx) % 4

    def at(self, dz=0, dx=0, dy=0, dcore=0):
        return (
            (self.y + dy) % 4 * 2 + (self.core + dcore) % 2,
            self.tensor(dz, dx),
        )


def greet(place):
    barrier = pltpu.get_barrier_semaphore()
    others = [place.at(dx=1), place.at(dx=3), place.at(dz=1), place.at(dz=3)]
    others += [place.at(dy=1), place.at(dy=3), place.at(dcore=1)]
    for other in others:
        pl.semaphore_signal(barrier, inc=1, device_id=other, device_id_type=MESH)
    pl.semaphore_wait(barrier, len(others))


class Gather:
    def __init__(self, place, own, buf, send, recv):
        self.place, self.own, self.buf, self.send_sems, self.recv_sems = place, own, buf, send, recv
        self.sent = []

    @staticmethod
    def slot(h, du, dv):
        return (dv % 4) * 4 + du % 4 if h == 0 else (du % 4) * 4 + dv % 4

    @staticmethod
    def rows(h, part):
        return pl.ds(h * 256, 256) if part is None else pl.ds(h * 256 + part * 128, 128)

    def ref(self, h, du, dv, part):
        rows = self.rows(h, part)
        if du % 4 == 0 and dv % 4 == 0:
            return self.own.at[rows, :]
        return self.buf.at[self.slot(h, du, dv), rows, :]

    def push(self, h, axis, sign, du, dv, part=None):
        if axis == 0:
            tu, tv = du - sign, dv
        else:
            tu, tv = du, dv - sign
        along_x = (axis == 0) == (h == 0)
        target = self.place.at(dx=sign) if along_x else self.place.at(dz=sign)
        copy = pltpu.make_async_remote_copy(
            src_ref=self.ref(h, du, dv, part),
            dst_ref=self.buf.at[self.slot(h, tu, tv), self.rows(h, part), :],
            send_sem=self.send_sems.at[len(self.sent)],
            recv_sem=self.recv_sems.at[h, self.slot(h, tu, tv), part or 0],
            device_id=target,
            device_id_type=MESH,
        )
        copy.start()
        self.sent.append(copy)

    def arrive(self, h, du, dv, part=None):
        ref = self.buf.at[self.slot(h, du, dv), self.rows(h, part), :]
        pltpu.make_async_remote_copy(
            src_ref=ref,
            dst_ref=ref,
            send_sem=self.send_sems.at[0],
            recv_sem=self.recv_sems.at[h, self.slot(h, du, dv), part or 0],
            device_id=self.place.at(dx=1),
            device_id_type=MESH,
        ).wait_recv()

    def far(self, h, axis, du, dv, sign):
        self.push(h, axis, sign, du, dv, 0 if sign == 1 else 1)

    def stage0(self):
        for h in (0, 1):
            for s in (1, -1):
                self.push(h, 0, s, 0, 0)
        for h in (0, 1):
            for s in (1, -1):
                self.push(h, 1, s, 0, 0)

    def stage1(self):
        for s in (1, -1):
            for h in (0, 1):
                self.arrive(h, -s, 0)
                self.far(h, 0, -s, 0, s)
                for w in (1, -1):
                    self.push(h, 1, w, -s, 0)
        for s in (1, -1):
            for h in (0, 1):
                self.arrive(h, 0, -s)
                self.far(h, 1, 0, -s, s)

    def stage2a(self):
        for h in (0, 1):
            for part in (0, 1):
                self.arrive(h, 2, 0, part)
            for w in (1, -1):
                self.push(h, 1, w, 2, 0)

    def stage2b(self):
        for s in (1, -1):
            for w in (1, -1):
                for h in (0, 1):
                    self.arrive(h, -s, -w)
                    self.far(h, 1, -s, -w, w)

    def stage3(self):
        for w in (1, -1):
            for h in (0, 1):
                self.arrive(h, 2, -w)
                self.far(h, 1, 2, -w, w)

    def stage4(self):
        for du in range(4):
            for h in (0, 1):
                for part in (0, 1):
                    self.arrive(h, du, 2, part)

    def finish(self):
        for copy in self.sent:
            copy.wait_send()


GATHER_SEMS = [pltpu.SemaphoreType.DMA((40,)), pltpu.SemaphoreType.DMA((2, 16, 2))]

READY = [
    [(0, 0)],
    [(1, 0), (3, 0), (0, 1), (0, 3)],
    [(2, 0), (1, 1), (1, 3), (3, 1), (3, 3)],
    [(2, 1), (2, 3)],
    [(0, 2), (1, 2), (2, 2), (3, 2)],
]


class Scatter:
    def __init__(self, place, buf, far, near, send, far_sems, near_sems):
        self.place, self.buf, self.far, self.near = place, buf, far, near
        self.send_sems, self.far_sems, self.near_sems = send, far_sems, near_sems
        self.sent = []

    def where(self, h, line, offset):
        return Gather.slot(h, line, offset) if line < 4 else Gather.slot(h, offset, 0)

    def push(self, h, line, sign, src, dst, sem):
        along_x = (line == 4) == (h == 0)
        target = self.place.at(dx=sign) if along_x else self.place.at(dz=sign)
        copy = pltpu.make_async_remote_copy(
            src_ref=src,
            dst_ref=dst,
            send_sem=self.send_sems.at[len(self.sent)],
            recv_sem=sem,
            device_id=target,
            device_id_type=MESH,
        )
        copy.start()
        self.sent.append(copy)

    def arrive(self, ref, sem):
        pltpu.make_async_remote_copy(
            src_ref=ref,
            dst_ref=ref,
            send_sem=self.send_sems.at[0],
            recv_sem=sem,
            device_id=self.place.at(dx=1),
            device_id_type=MESH,
        ).wait_recv()

    def start(self, h, line):
        slot = self.where(h, line, 2)
        for part, sign in ((0, -1), (1, 1)):
            self.push(
                h, line, sign,
                self.buf.at[slot, Gather.rows(h, part), :],
                self.far.at[h, line, part],
                self.far_sems.at[h, line, part],
            )

    def pass_on(self, h, line):
        for part, sign in ((0, -1), (1, 1)):
            slot = self.where(h, line, sign)
            rows = Gather.rows(h, part)
            self.arrive(self.far.at[h, line, part], self.far_sems.at[h, line, part])
            self.buf[slot, rows, :] = (
                self.buf[slot, rows, :].astype(F32) + self.far[h, line, part].astype(F32)
            ).astype(BF16)
            self.push(
                h, line, sign,
                self.buf.at[slot, Gather.rows(h, None), :],
                self.near.at[h, line, part],
                self.near_sems.at[h, line, part],
            )

    def total(self, h, line):
        for part in (0, 1):
            self.arrive(self.near.at[h, line, part], self.near_sems.at[h, line, part])
        slot = self.where(h, line, 0)
        rows = Gather.rows(h, None)
        value = (
            self.buf[slot, rows, :].astype(F32)
            + self.near[h, line, 0].astype(F32)
            + self.near[h, line, 1].astype(F32)
        ).astype(BF16)
        return slot, rows, value

    def stage0(self, fill):
        done = []
        for line in (2, 1, 3, 0):
            for h in (0, 1):
                slot = self.where(h, line, 2)
                if slot not in done:
                    fill(slot)
                    done.append(slot)
                self.start(h, line)
        for slot in range(16):
            if slot not in done:
                fill(slot)

    def stage1(self):
        for line in (2, 1, 3, 0):
            for h in (0, 1):
                self.pass_on(h, line)

    def settle(self, line):
        for h in (0, 1):
            slot, rows, value = self.total(h, line)
            self.buf[slot, rows, :] = value

    def stage2(self):
        self.settle(2)
        for h in (0, 1):
            self.start(h, 4)

    def stage3(self):
        self.settle(1)
        self.settle(3)
        for h in (0, 1):
            self.pass_on(h, 4)

    def stage4(self, out):
        self.settle(0)
        for h in (0, 1):
            _, rows, value = self.total(h, 4)
            out[rows, :] = value

    def finish(self):
        for copy in self.sent:
            copy.wait_send()


SCATTER_BUFS = [pltpu.VMEM((2, 5, 2, 128, 256), BF16), pltpu.VMEM((2, 5, 2, 256, 256), BF16)]
SCATTER_SEMS = [
    pltpu.SemaphoreType.DMA((40,)),
    pltpu.SemaphoreType.DMA((2, 5, 2)),
    pltpu.SemaphoreType.DMA((2, 5, 2)),
]


class Links:
    def __init__(self, send, recv):
        self.send_sems, self.recv_sems, self.sent = send, recv, []

    def push(self, index, src, dst, target):
        copy = pltpu.make_async_remote_copy(
            src_ref=src,
            dst_ref=dst,
            send_sem=self.send_sems.at[index],
            recv_sem=self.recv_sems.at[index],
            device_id=target,
            device_id_type=MESH,
        )
        copy.start()
        self.sent.append(copy)

    def arrive(self, index, ref, source):
        pltpu.make_async_remote_copy(
            src_ref=ref,
            dst_ref=ref,
            send_sem=self.send_sems.at[index],
            recv_sem=self.recv_sems.at[index],
            device_id=source,
            device_id_type=MESH,
        ).wait_recv()

    def finish(self):
        for copy in self.sent:
            copy.wait_send()


LINK_SEMS = [pltpu.SemaphoreType.DMA((16,)), pltpu.SemaphoreType.DMA((16,))]


def each(items, body):
    def step(i, _):
        item = items[0]
        for j in range(1, len(items)):
            item = jnp.where(i == j, items[j], item)
        body(item)
        return 0

    lax.fori_loop(0, len(items), step, 0)


def layer(
    tok, wq, wk, wv, wo, og, lens, firsts, mixed_out, grad_out,
    xbuf, gbuf, wqt, wkv, wot, acc, kacc, hacc,
    qs, kvall, logits, probs, peak, sums, outs, att, dos, dlt, dqt, dkv16, core_in,
    yfar, ynear, grads, mfar, mnear, tfar, tnear,
    xs, xr, gs, gr, ms, mfs, mns, ts, tfs, tns, ws, wr, ks, kr, ds_, dr, lsem,
):
    place = Place()
    g = place.g
    half = place.t % 2
    own_rows = pl.ds(pl.multiple_of(half * 64, 64), 64)
    other_rows = pl.ds(pl.multiple_of((1 - half) * 64, 64), 64)
    loads = [
        pltpu.make_async_copy(wk, wkv.at[0, own_rows, :], lsem.at[1]),
        pltpu.make_async_copy(wv, wkv.at[1, own_rows, :], lsem.at[2]),
        pltpu.make_async_copy(tok, xbuf.at[0], lsem.at[0]),
        pltpu.make_async_copy(wq, wqt, lsem.at[3]),
        pltpu.make_async_copy(og, gbuf.at[0], lsem.at[4]),
        pltpu.make_async_copy(wo, wot, lsem.at[5]),
    ]
    for load in loads:
        load.start()
    greet(place)
    xg = Gather(place, tok, xbuf, xs, xr)
    gg = Gather(place, og, gbuf, gs, gr)
    xg.stage0()

    def group_at(dy, dcore=0):
        return place.at(dy=dy, dcore=dcore)[0]

    partner = (g, place.t + 1 - 2 * half)
    sibling = place.at(dcore=1)
    up, down = place.at(dy=1), place.at(dy=3)
    below, above, across = group_at(3), group_at(1), group_at(2)
    sib_own, sib_below, sib_above, sib_across = (group_at(dy, 1) for dy in (0, 3, 1, 2))
    first_rows, last_rows = pl.ds(0, 256), pl.ds(256, 256)

    def slice_of(rows, group, kind=None):
        columns = pl.ds(pl.multiple_of(group * 512, 512), 512)
        return wkv.at[pl.ds(0, 2) if kind is None else kind, rows, columns]

    wl = Links(ws, wr)
    loads[0].wait()
    loads[1].wait()
    wl.push(0, slice_of(own_rows, g), slice_of(own_rows, g), partner)

    def weights_one():
        ref = slice_of(other_rows, g)
        wl.arrive(0, ref, partner)
        wl.push(1, ref, ref, up)
        wl.push(2, ref, ref, down)
        wl.push(8, ref, ref, sibling)

    def weights_two():
        ref = slice_of(other_rows, below)
        wl.arrive(1, ref, down)
        wl.push(3, slice_of(other_rows, below, 0), slice_of(other_rows, below, 0), up)
        wl.push(9, ref, ref, sibling)
        ref = slice_of(other_rows, above)
        wl.arrive(2, ref, up)
        wl.push(4, slice_of(other_rows, above, 1), slice_of(other_rows, above, 1), down)
        wl.push(10, ref, ref, sibling)

    def weights_three():
        wl.arrive(3, slice_of(other_rows, across, 0), down)
        wl.arrive(4, slice_of(other_rows, across, 1), up)
        ref = slice_of(other_rows, across)
        wl.push(11, ref, ref, sibling)

    def weights_four():
        for index, group in ((8, sib_own), (9, sib_below), (10, sib_above), (11, sib_across)):
            wl.arrive(index, slice_of(other_rows, group), sibling)

    def clear(i, _):
        dkv16[i] = jnp.zeros((512, 256), BF16)
        return 0

    lax.fori_loop(0, 8, clear, 0)
    loads[2].wait()
    loads[3].wait()

    def span(slot):
        chunk = place.tensor(slot // 4, slot % 4)
        return pl.ds(pl.multiple_of(chunk * 256, 256), 256)

    def head_weights(slot):
        return wkv[:, :, span(slot)].reshape(256, 256)

    def gathered(total_ref, buf, weight, cb, pairs, first=False):
        for h in (0, 1):
            rows = pl.ds(h * 256, 256)
            total = None
            for du, dv in pairs:
                slot = Gather.slot(h, du, dv)
                part = dot(buf[slot, rows, :], weight(slot), 1, cb)
                total = part if total is None else total + part
            total_ref[rows, :] = total if first else total_ref[rows, :] + total

    def project(pairs, first=False):
        gathered(acc, xbuf, lambda slot: wqt[span(slot), :], 0, pairs, first)

    def project_kv(pairs, first=False):
        gathered(kacc, xbuf, head_weights, 1, pairs, first)

    def cotangent(pairs, first=False):
        gathered(hacc, gbuf, lambda slot: wot[:, span(slot)], 1, pairs, first)

    project(READY[0], True)
    xg.stage1()
    weights_one()
    project(READY[1])
    xg.stage2a()
    xg.stage2b()
    weights_two()
    project(READY[2])
    xg.stage3()
    gg.stage0()
    weights_three()
    project(READY[3])
    weights_four()
    project_kv(READY[0], True)
    project_kv(READY[1])
    project_kv(READY[2])
    project_kv(READY[3])
    xg.stage4()
    project_kv(READY[4])

    kv = Links(ks, kr)
    kvall[g] = kacc[...].astype(BF16)
    kv.push(1, kvall.at[g], kvall.at[g], up)
    kv.push(2, kvall.at[g], kvall.at[g], down)
    kv.push(8, kvall.at[g], kvall.at[g], sibling)
    project(READY[4])
    qs[0] = acc[:, 0:128].astype(BF16)
    qs[1] = acc[:, 128:256].astype(BF16)
    loads[4].wait()
    loads[5].wait()

    lane = lax.broadcasted_iota(jnp.int32, (1, 512), 1)
    position = lane + g * 512
    low_key = jnp.where(lane < 256, firsts[2 * g], firsts[2 * g + 1]) * 256
    end = lens[0]
    for i in range(1, 5):
        low_key = jnp.maximum(low_key, jnp.where(position >= end, end, 0))
        if i < 4:
            end = end + lens[i]
    for h in (0, 1):
        peak[h] = jnp.full((1, 512), -1e30, F32)
        sums[h] = jnp.zeros((1, 512), F32)
        outs[h] = jnp.zeros((128, 512), F32)
        dqt[h] = jnp.zeros((128, 512), F32)

    def score(k):
        @pl.when(k <= g)
        def _():
            key = lax.broadcasted_iota(jnp.int32, (512, 512), 0) + k * 512
            visible = (key >= low_key) & (key <= position)
            for h in (0, 1):
                raw = dot(kvall[k, :, 0:128], qs[h], 1, 1) * (SCALE * LOG2E)
                raw = jnp.where(visible, raw, -1e30)
                logits[k, h] = raw
                peak[h] = jnp.maximum(peak[h], jnp.max(raw, axis=0, keepdims=True))

    def weigh(k, _):
        for h in (0, 1):
            prob = jnp.exp2(logits[k, h] - peak[h])
            rounded = prob.astype(BF16)
            probs[k, h] = rounded
            sums[h] += jnp.sum(prob, axis=0, keepdims=True)
            outs[h] += dot(kvall[k, :, 128:256], rounded, 0, 0)
        return 0

    each([g], score)
    gg.stage1()
    cotangent(READY[0], True)
    gg.stage2a()
    cotangent(READY[1])
    kv.arrive(1, kvall.at[below], down)
    kv.push(3, kvall.at[below, first_rows, :], kvall.at[below, first_rows, :], up)
    kv.push(9, kvall.at[below], kvall.at[below], sibling)
    kv.arrive(2, kvall.at[above], up)
    kv.push(4, kvall.at[above, last_rows, :], kvall.at[above, last_rows, :], down)
    kv.push(10, kvall.at[above], kvall.at[above], sibling)
    kv.arrive(8, kvall.at[sib_own], sibling)
    each([sib_own, below, above], score)
    gg.stage2b()
    kv.arrive(3, kvall.at[across, first_rows, :], down)
    kv.arrive(4, kvall.at[across, last_rows, :], up)
    kv.push(11, kvall.at[across], kvall.at[across], sibling)
    kv.arrive(9, kvall.at[sib_below], sibling)
    kv.arrive(10, kvall.at[sib_above], sibling)
    each([sib_below, sib_above, across], score)
    gg.stage3()
    kv.arrive(11, kvall.at[sib_across], sibling)
    each([sib_across], score)
    lax.fori_loop(0, g + 1, weigh, 0)

    for h in (0, 1):
        inverse = 1.0 / sums[h]
        sums[h] = inverse
        outs[h] = outs[h] * inverse
        att[:, h * 128 : (h + 1) * 128] = outs[h].T.astype(BF16)

    xg.finish()
    mixed = Scatter(place, xbuf, mfar, mnear, ms, mfs, mns)

    def mix(slot):
        xbuf[slot] = dot(att[...], wot[:, span(slot)]).astype(BF16)

    mixed.stage0(mix)
    cotangent(READY[2])
    cotangent(READY[3])
    gg.stage4()
    cotangent(READY[4])

    for h in (0, 1):
        grad_t = hacc[:, h * 128 : (h + 1) * 128].T * sums[h]
        out_t = outs[h].astype(BF16).astype(F32)
        dlt[h] = jnp.sum(grad_t * out_t, axis=0, keepdims=True)
        dos[h] = grad_t.T.astype(BF16)

    def backward(k):
        @pl.when(k <= g)
        def _():
            keys, values = kvall[k, :, 0:128], kvall[k, :, 128:256]
            key_part, value_part = None, None
            for h in (0, 1):
                prob = probs[k, h]
                dprob = dot(values, dos[h], 1, 1)
                grad = (prob.astype(F32) * (dprob - dlt[h])).astype(BF16)
                dqt[h] += dot(keys, grad, 0, 0)
                one, two = dot(grad, qs[h]), dot(prob, dos[h])
                key_part = one if h == 0 else key_part + one
                value_part = two if h == 0 else value_part + two
            dkv16[k, :, 0:128] = (key_part * SCALE).astype(BF16)
            dkv16[k, :, 128:256] = value_part.astype(BF16)

    kvg = Links(ds_, dr)

    def to_sibling(dy, group):
        kvg.push(dy, dkv16.at[group], core_in.at[dy], sibling)

    def join_cores(dy, group):
        kvg.arrive(dy, core_in.at[dy], sibling)
        dkv16[group] = (dkv16[group].astype(F32) + core_in[dy].astype(F32)).astype(BF16)

    def add_far(part, group, rows, source):
        kvg.arrive(4 + part, yfar.at[part], source)
        dkv16[group, rows, :] = (dkv16[group, rows, :].astype(F32) + yfar[part].astype(F32)).astype(BF16)

    each([sib_across, across], backward)
    to_sibling(2, sib_across)
    mixed.stage1()
    join_cores(2, across)
    kvg.push(4, dkv16.at[across, first_rows, :], yfar.at[0], down)
    kvg.push(5, dkv16.at[across, last_rows, :], yfar.at[1], up)
    each([sib_below, sib_above, sib_own], backward)
    to_sibling(3, sib_below)
    to_sibling(1, sib_above)
    to_sibling(0, sib_own)
    mixed.stage2()
    each([below, above], backward)
    join_cores(3, below)
    add_far(0, below, first_rows, up)
    kvg.push(6, dkv16.at[below], ynear.at[0], down)
    join_cores(1, above)
    add_far(1, above, last_rows, down)
    kvg.push(7, dkv16.at[above], ynear.at[1], up)
    each([g], backward)
    gg.finish()
    mixed.stage3()
    for h in (0, 1):
        grads[:, h * 128 : (h + 1) * 128] = (dqt[h] * SCALE).T.astype(BF16)
    join_cores(0, g)
    kvg.arrive(6, ynear.at[0], up)
    kvg.arrive(7, ynear.at[1], down)
    grads[:, 256:512] = (
        dkv16[g].astype(F32) + ynear[0].astype(F32) + ynear[1].astype(F32)
    ).astype(BF16)

    final = Scatter(place, gbuf, tfar, tnear, ts, tfs, tns)

    def spread(slot):
        gbuf[slot] = (
            dot(grads[:, 0:256], wqt[span(slot), :], 1, 1)
            + dot(grads[:, 256:512], head_weights(slot), 1, 0)
        ).astype(BF16)

    final.stage0(spread)
    mixed.stage4(mixed_out)
    final.stage1()
    final.stage2()
    final.stage3()
    final.stage4(grad_out)
    wl.finish()
    kv.finish()
    kvg.finish()
    mixed.finish()
    final.finish()


def local(tokens, w_query, w_key, w_value, w_out, out_grad, lengths, kv_first):
    return tuple(
        pl.pallas_call(
            layer,
            out_shape=(
                jax.ShapeDtypeStruct((512, 256), BF16),
                jax.ShapeDtypeStruct((512, 256), BF16),
            ),
            in_specs=[pl.BlockSpec(memory_space=pl.ANY)] * 6
            + [pl.BlockSpec(memory_space=pltpu.SMEM)] * 2,
            out_specs=[pl.BlockSpec(memory_space=pltpu.VMEM)] * 2,
            scratch_shapes=[
                pltpu.VMEM((16, 512, 256), BF16),
                pltpu.VMEM((16, 512, 256), BF16),
                pltpu.VMEM((4096, 256), BF16),
                pltpu.VMEM((2, 128, 4096), BF16),
                pltpu.VMEM((256, 4096), BF16),
                pltpu.VMEM((512, 256), F32),
                pltpu.VMEM((512, 256), F32),
                pltpu.VMEM((512, 256), F32),
                pltpu.VMEM((2, 512, 128), BF16),
                pltpu.VMEM((8, 512, 256), BF16),
                pltpu.VMEM((8, 2, 512, 512), F32),
                pltpu.VMEM((8, 2, 512, 512), BF16),
                pltpu.VMEM((2, 1, 512), F32),
                pltpu.VMEM((2, 1, 512), F32),
                pltpu.VMEM((2, 128, 512), F32),
                pltpu.VMEM((512, 256), BF16),
                pltpu.VMEM((2, 512, 128), BF16),
                pltpu.VMEM((2, 1, 512), F32),
                pltpu.VMEM((2, 128, 512), F32),
                pltpu.VMEM((8, 512, 256), BF16),
                pltpu.VMEM((4, 512, 256), BF16),
                pltpu.VMEM((2, 256, 256), BF16),
                pltpu.VMEM((2, 512, 256), BF16),
                pltpu.VMEM((512, 512), BF16),
                *SCATTER_BUFS,
                *SCATTER_BUFS,
                *GATHER_SEMS,
                *GATHER_SEMS,
                *SCATTER_SEMS,
                *SCATTER_SEMS,
                *LINK_SEMS,
                *LINK_SEMS,
                *LINK_SEMS,
                pltpu.SemaphoreType.DMA((6,)),
            ],
            compiler_params=pltpu.CompilerParams(
                collective_id=0, has_side_effects=True, vmem_limit_bytes=62 * 1024 * 1024
            ),
            name="layer",
        )(tokens, w_query, w_key.T, w_value.T, w_out, out_grad, lengths, kv_first)
    )


def solution(mesh):
    return jax.shard_map(
        local,
        mesh=mesh,
        in_specs=(
            P("group", "tensor"),
            P(None, "tensor"),
            P(None, "tensor"),
            P(None, "tensor"),
            P("tensor", None),
            P("group", "tensor"),
            P(),
            P(),
        ),
        out_specs=(P("group", "tensor"), P("group", "tensor")),
        check_vma=False,
    )
```

```python
import jax
import jax.numpy as jnp
from jax import lax
from jax.experimental import pallas as pl
from jax.experimental.pallas import tpu as pltpu
from jax.sharding import PartitionSpec as P

HD = 128
LOG2E = 1.4426950408889634
SCALE = HD**-0.5
MESH = pl.DeviceIdType.MESH
F32 = jnp.float32
BF16 = jnp.bfloat16


def dot(a, b, ca=1, cb=0):
    return lax.dot_general(a, b, (((ca,), (cb,)), ((), ())), preferred_element_type=F32)


class Place:
    def __init__(self):
        self.g = lax.axis_index("group")
        self.t = lax.axis_index("tensor")
        self.y, self.core = self.g // 2, self.g % 2
        self.z, self.x = self.t // 4, self.t % 4

    def tensor(self, dz, dx):
        return (self.z + dz) % 4 * 4 + (self.x + dx) % 4

    def at(self, dz=0, dx=0, dy=0, dcore=0):
        return (
            (self.y + dy) % 4 * 2 + (self.core + dcore) % 2,
            self.tensor(dz, dx),
        )


def greet(place):
    barrier = pltpu.get_barrier_semaphore()
    others = [place.at(dx=1), place.at(dx=2), place.at(dx=3), place.at(dz=1), place.at(dz=3)]
    others += [place.at(dy=1), place.at(dy=3), place.at(dcore=1)]
    for other in others:
        pl.semaphore_signal(barrier, inc=1, device_id=other, device_id_type=MESH)
    pl.semaphore_wait(barrier, len(others))


class Gather:
    def __init__(self, place, own, buf, send, recv):
        self.place, self.own, self.buf, self.send_sems, self.recv_sems = place, own, buf, send, recv
        self.sent = []

    @staticmethod
    def slot(h, du, dv):
        return (dv % 4) * 4 + du % 4 if h == 0 else (du % 4) * 4 + dv % 4

    @staticmethod
    def rows(h, part):
        return pl.ds(h * 256, 256) if part is None else pl.ds(h * 256 + part * 128, 128)

    def ref(self, h, du, dv, part):
        rows = self.rows(h, part)
        if du % 4 == 0 and dv % 4 == 0:
            return self.own.at[rows, :]
        return self.buf.at[self.slot(h, du, dv), rows, :]

    def push(self, h, axis, sign, du, dv, part=None):
        if axis == 0:
            tu, tv = du - sign, dv
        else:
            tu, tv = du, dv - sign
        along_x = (axis == 0) == (h == 0)
        target = self.place.at(dx=sign) if along_x else self.place.at(dz=sign)
        copy = pltpu.make_async_remote_copy(
            src_ref=self.ref(h, du, dv, part),
            dst_ref=self.buf.at[self.slot(h, tu, tv), self.rows(h, part), :],
            send_sem=self.send_sems.at[len(self.sent)],
            recv_sem=self.recv_sems.at[h, self.slot(h, tu, tv), part or 0],
            device_id=target,
            device_id_type=MESH,
        )
        copy.start()
        self.sent.append(copy)

    def arrive(self, h, du, dv, part=None):
        ref = self.buf.at[self.slot(h, du, dv), self.rows(h, part), :]
        pltpu.make_async_remote_copy(
            src_ref=ref,
            dst_ref=ref,
            send_sem=self.send_sems.at[0],
            recv_sem=self.recv_sems.at[h, self.slot(h, du, dv), part or 0],
            device_id=self.place.at(dx=1),
            device_id_type=MESH,
        ).wait_recv()

    def far(self, h, axis, du, dv, sign):
        self.push(h, axis, sign, du, dv, 0 if sign == 1 else 1)

    def stage0(self):
        for h in (0, 1):
            for s in (1, -1):
                self.push(h, 0, s, 0, 0)
        for h in (0, 1):
            for s in (1, -1):
                self.push(h, 1, s, 0, 0)

    def stage1(self):
        for s in (1, -1):
            for h in (0, 1):
                self.arrive(h, -s, 0)
                self.far(h, 0, -s, 0, s)
                for w in (1, -1):
                    self.push(h, 1, w, -s, 0)
        for s in (1, -1):
            for h in (0, 1):
                self.arrive(h, 0, -s)
                self.far(h, 1, 0, -s, s)

    def stage2a(self):
        for h in (0, 1):
            for part in (0, 1):
                self.arrive(h, 2, 0, part)
            for w in (1, -1):
                self.push(h, 1, w, 2, 0)

    def stage2b(self):
        for s in (1, -1):
            for w in (1, -1):
                for h in (0, 1):
                    self.arrive(h, -s, -w)
                    self.far(h, 1, -s, -w, w)

    def stage3(self):
        for w in (1, -1):
            for h in (0, 1):
                self.arrive(h, 2, -w)
                self.far(h, 1, 2, -w, w)

    def stage4(self):
        for du in range(4):
            for h in (0, 1):
                for part in (0, 1):
                    self.arrive(h, du, 2, part)

    def finish(self):
        for copy in self.sent:
            copy.wait_send()


GATHER_SEMS = [pltpu.SemaphoreType.DMA((40,)), pltpu.SemaphoreType.DMA((2, 16, 2))]

READY = [
    [(0, 0)],
    [(1, 0), (3, 0), (0, 1), (0, 3)],
    [(2, 0), (1, 1), (1, 3), (3, 1), (3, 3)],
    [(2, 1), (2, 3)],
    [(0, 2), (1, 2), (2, 2), (3, 2)],
]


class Scatter:
    def __init__(self, place, buf, far, near, send, far_sems, near_sems):
        self.place, self.buf, self.far, self.near = place, buf, far, near
        self.send_sems, self.far_sems, self.near_sems = send, far_sems, near_sems
        self.sent = []

    def where(self, h, line, offset):
        return Gather.slot(h, line, offset) if line < 4 else Gather.slot(h, offset, 0)

    def push(self, h, line, sign, src, dst, sem):
        along_x = (line == 4) == (h == 0)
        target = self.place.at(dx=sign) if along_x else self.place.at(dz=sign)
        copy = pltpu.make_async_remote_copy(
            src_ref=src,
            dst_ref=dst,
            send_sem=self.send_sems.at[len(self.sent)],
            recv_sem=sem,
            device_id=target,
            device_id_type=MESH,
        )
        copy.start()
        self.sent.append(copy)

    def arrive(self, ref, sem):
        pltpu.make_async_remote_copy(
            src_ref=ref,
            dst_ref=ref,
            send_sem=self.send_sems.at[0],
            recv_sem=sem,
            device_id=self.place.at(dx=1),
            device_id_type=MESH,
        ).wait_recv()

    def start(self, h, line):
        slot = self.where(h, line, 2)
        for part, sign in ((0, -1), (1, 1)):
            self.push(
                h, line, sign,
                self.buf.at[slot, Gather.rows(h, part), :],
                self.far.at[h, line, part],
                self.far_sems.at[h, line, part],
            )

    def pass_on(self, h, line):
        for part, sign in ((0, -1), (1, 1)):
            slot = self.where(h, line, sign)
            rows = Gather.rows(h, part)
            self.arrive(self.far.at[h, line, part], self.far_sems.at[h, line, part])
            self.buf[slot, rows, :] = (
                self.buf[slot, rows, :].astype(F32) + self.far[h, line, part].astype(F32)
            ).astype(BF16)
            self.push(
                h, line, sign,
                self.buf.at[slot, Gather.rows(h, None), :],
                self.near.at[h, line, part],
                self.near_sems.at[h, line, part],
            )

    def total(self, h, line):
        for part in (0, 1):
            self.arrive(self.near.at[h, line, part], self.near_sems.at[h, line, part])
        slot = self.where(h, line, 0)
        rows = Gather.rows(h, None)
        value = (
            self.buf[slot, rows, :].astype(F32)
            + self.near[h, line, 0].astype(F32)
            + self.near[h, line, 1].astype(F32)
        ).astype(BF16)
        return slot, rows, value

    def stage0(self, fill):
        done = []
        for line in (2, 1, 3, 0):
            for h in (0, 1):
                slot = self.where(h, line, 2)
                if slot not in done:
                    fill(slot)
                    done.append(slot)
                self.start(h, line)
        for slot in range(16):
            if slot not in done:
                fill(slot)

    def stage1(self):
        for line in (2, 1, 3, 0):
            for h in (0, 1):
                self.pass_on(h, line)

    def settle(self, line):
        for h in (0, 1):
            slot, rows, value = self.total(h, line)
            self.buf[slot, rows, :] = value

    def stage2(self):
        self.settle(2)
        for h in (0, 1):
            self.start(h, 4)

    def stage3(self):
        self.settle(1)
        self.settle(3)
        for h in (0, 1):
            self.pass_on(h, 4)

    def stage4(self, out):
        self.settle(0)
        for h in (0, 1):
            _, rows, value = self.total(h, 4)
            out[rows, :] = value

    def finish(self):
        for copy in self.sent:
            copy.wait_send()


SCATTER_BUFS = [pltpu.VMEM((2, 5, 2, 128, 256), BF16), pltpu.VMEM((2, 5, 2, 256, 256), BF16)]
SCATTER_SEMS = [
    pltpu.SemaphoreType.DMA((40,)),
    pltpu.SemaphoreType.DMA((2, 5, 2)),
    pltpu.SemaphoreType.DMA((2, 5, 2)),
]


class Links:
    def __init__(self, send, recv):
        self.send_sems, self.recv_sems, self.sent = send, recv, []

    def push(self, index, src, dst, target):
        copy = pltpu.make_async_remote_copy(
            src_ref=src,
            dst_ref=dst,
            send_sem=self.send_sems.at[index],
            recv_sem=self.recv_sems.at[index],
            device_id=target,
            device_id_type=MESH,
        )
        copy.start()
        self.sent.append(copy)

    def arrive(self, index, ref, source):
        pltpu.make_async_remote_copy(
            src_ref=ref,
            dst_ref=ref,
            send_sem=self.send_sems.at[index],
            recv_sem=self.recv_sems.at[index],
            device_id=source,
            device_id_type=MESH,
        ).wait_recv()

    def finish(self):
        for copy in self.sent:
            copy.wait_send()


class LineGather:
    def __init__(self, place, along_x, own, buf, send, recv):
        self.links, self.own, self.buf = Links(send, recv), own, buf
        self.next = lambda sign: place.at(dx=sign) if along_x else place.at(dz=sign)

    def stage0(self):
        for r in (0, 1):
            for s in (1, -1):
                rows = Gather.rows(r, None)
                self.links.push(
                    r * 4 + (s < 0), self.own.at[rows, :], self.buf.at[-s % 4, rows, :], self.next(s)
                )

    def stage1(self):
        for r in (0, 1):
            for part, s in ((0, 1), (1, -1)):
                whole, rows = Gather.rows(r, None), Gather.rows(r, part)
                self.links.arrive(r * 4 + (s < 0), self.buf.at[-s % 4, whole, :], self.next(-s))
                self.links.push(
                    r * 4 + 2 + part, self.buf.at[-s % 4, rows, :], self.buf.at[2, rows, :], self.next(s)
                )

    def stage2(self):
        for r in (0, 1):
            for part, s in ((0, 1), (1, -1)):
                self.links.arrive(r * 4 + 2 + part, self.buf.at[2, Gather.rows(r, part), :], self.next(-s))


class LineScatter:
    def __init__(self, place, along_x, buf, far, near, send, recv):
        self.links, self.buf, self.far, self.near = Links(send, recv), buf, far, near
        self.next = lambda sign: place.at(dx=sign) if along_x else place.at(dz=sign)

    def start(self):
        for r in (0, 1):
            for part, s in ((0, -1), (1, 1)):
                self.links.push(
                    r * 4 + part, self.buf.at[2, Gather.rows(r, part), :], self.far.at[r, part], self.next(s)
                )

    def pass_on(self):
        for r in (0, 1):
            for part, s in ((0, -1), (1, 1)):
                whole, rows = Gather.rows(r, None), Gather.rows(r, part)
                self.links.arrive(r * 4 + part, self.far.at[r, part], self.next(-s))
                self.buf[s % 4, rows, :] = (
                    self.buf[s % 4, rows, :].astype(F32) + self.far[r, part].astype(F32)
                ).astype(BF16)
                self.links.push(
                    r * 4 + 2 + part, self.buf.at[s % 4, whole, :], self.near.at[r, part], self.next(s)
                )

    def total(self, out):
        for r in (0, 1):
            rows = Gather.rows(r, None)
            for part, s in ((0, -1), (1, 1)):
                self.links.arrive(r * 4 + 2 + part, self.near.at[r, part], self.next(-s))
            out[rows, :] = (
                self.buf[0, rows, :].astype(F32)
                + self.near[r, 0].astype(F32)
                + self.near[r, 1].astype(F32)
            ).astype(out.dtype)


LINE_BUFS = [
    pltpu.VMEM((4, 512, 256), BF16),
    pltpu.VMEM((2, 2, 128, 256), BF16),
    pltpu.VMEM((2, 2, 256, 256), BF16),
]
LINE_SEMS = [pltpu.SemaphoreType.DMA((8,))] * 4

LINK_SEMS = [pltpu.SemaphoreType.DMA((16,)), pltpu.SemaphoreType.DMA((16,))]


def each(items, body):
    def step(i, _):
        item = items[0]
        for j in range(1, len(items)):
            item = jnp.where(i == j, items[j], item)
        body(item)
        return 0

    lax.fori_loop(0, len(items), step, 0)


def layer(
    tok, wq, wk, wv, wo, og, lens, firsts, mixed_out, grad_out,
    xbuf, wqt, wkv, wob, acc, kacc, hacc,
    qs, kvall, logits, probs, peak, sums, outs, dos, dlt, dqt, dkv16, core_in,
    yfar, ynear, grads, tfar, tnear,
    gz, hp, hfar, hnear, ax, mp, mfar, mnear,
    xs, xr, ts, tfs, tns, ws, wr, ks, kr, ds_, dr, os_, or_,
    gs, gr, hs, hr, as_, ar, ms, mr, lsem,
):
    place = Place()
    g = place.g
    half = place.t % 2
    own_rows = pl.ds(pl.multiple_of(half * 64, 64), 64)
    other_rows = pl.ds(pl.multiple_of((1 - half) * 64, 64), 64)
    loads = [
        pltpu.make_async_copy(wk, wkv.at[0, own_rows, :], lsem.at[1]),
        pltpu.make_async_copy(wv, wkv.at[1, own_rows, :], lsem.at[2]),
        pltpu.make_async_copy(tok, xbuf.at[0], lsem.at[0]),
        pltpu.make_async_copy(wq, wqt, lsem.at[3]),
        pltpu.make_async_copy(og, gz.at[0], lsem.at[4]),
    ]

    def columns_of(dz, dx):
        return pl.ds(pl.multiple_of(place.tensor(dz, dx) * 256, 256), 256)

    for dz in range(4):
        loads.append(pltpu.make_async_copy(wo.at[:, columns_of(dz, 0)], wob.at[0, dz], lsem.at[5 + dz]))
    for load in loads:
        load.start()
    greet(place)
    xg = Gather(place, tok, xbuf, xs, xr)
    gg = LineGather(place, False, og, gz, gs, gr)
    head_sum = LineScatter(place, True, hp, hfar, hnear, hs, hr)
    ag = LineGather(place, True, ax.at[0], ax, as_, ar)
    mixed = LineScatter(place, False, mp, mfar, mnear, ms, mr)
    xg.stage0()

    def group_at(dy, dcore=0):
        return place.at(dy=dy, dcore=dcore)[0]

    partner = (g, place.t + 1 - 2 * half)
    sibling = place.at(dcore=1)
    up, down = place.at(dy=1), place.at(dy=3)
    below, above, across = group_at(3), group_at(1), group_at(2)
    sib_own, sib_below, sib_above, sib_across = (group_at(dy, 1) for dy in (0, 3, 1, 2))
    first_rows, last_rows = pl.ds(0, 256), pl.ds(256, 256)

    def slice_of(rows, group, kind=None):
        columns = pl.ds(pl.multiple_of(group * 512, 512), 512)
        return wkv.at[pl.ds(0, 2) if kind is None else kind, rows, columns]

    wl = Links(ws, wr)
    loads[0].wait()
    loads[1].wait()
    wl.push(0, slice_of(own_rows, g), slice_of(own_rows, g), partner)

    ol = Links(os_, or_)
    own_slice = pl.ds(pl.multiple_of(g * 32, 32), 32)
    for d in (1, 3, 2):
        for dz in range(4):
            ol.push(
                (d - 1) * 4 + dz,
                wo.at[own_slice, columns_of(dz, d)],
                wob.at[4 - d, dz, own_slice, :],
                place.at(dx=d),
            )

    def out_slice(group, part=None):
        if part is None:
            rows = pl.ds(pl.multiple_of(group * 32, 32), 32)
        else:
            rows = pl.ds(pl.multiple_of(group * 32 + part * 16, 16), 16)
        return wob.at[pl.ds(1, 3), pl.ds(0, 4), rows, :]

    def out_one():
        for d in (1, 3, 2):
            for dz in range(4):
                ol.arrive((d - 1) * 4 + dz, wob.at[4 - d, dz, own_slice, :], place.at(dx=4 - d))
        ref = out_slice(g)
        ol.push(12, ref, ref, up)
        ol.push(13, ref, ref, down)
        ol.push(20, ref, ref, sibling)

    def out_two():
        ref = out_slice(below)
        ol.arrive(12, ref, down)
        ol.push(14, out_slice(below, 0), out_slice(below, 0), up)
        ol.push(21, ref, ref, sibling)
        ref = out_slice(above)
        ol.arrive(13, ref, up)
        ol.push(15, out_slice(above, 1), out_slice(above, 1), down)
        ol.push(22, ref, ref, sibling)

    def out_three():
        ol.arrive(14, out_slice(across, 0), down)
        ol.arrive(15, out_slice(across, 1), up)
        ref = out_slice(across)
        ol.push(23, ref, ref, sibling)

    def out_four():
        for index, group in ((20, sib_own), (21, sib_below), (22, sib_above), (23, sib_across)):
            ol.arrive(index, out_slice(group), sibling)

    def weights_one():
        ref = slice_of(other_rows, g)
        wl.arrive(0, ref, partner)
        wl.push(1, ref, ref, up)
        wl.push(2, ref, ref, down)
        wl.push(8, ref, ref, sibling)

    def weights_two():
        ref = slice_of(other_rows, below)
        wl.arrive(1, ref, down)
        wl.push(3, slice_of(other_rows, below, 0), slice_of(other_rows, below, 0), up)
        wl.push(9, ref, ref, sibling)
        ref = slice_of(other_rows, above)
        wl.arrive(2, ref, up)
        wl.push(4, slice_of(other_rows, above, 1), slice_of(other_rows, above, 1), down)
        wl.push(10, ref, ref, sibling)

    def weights_three():
        wl.arrive(3, slice_of(other_rows, across, 0), down)
        wl.arrive(4, slice_of(other_rows, across, 1), up)
        ref = slice_of(other_rows, across)
        wl.push(11, ref, ref, sibling)

    def weights_four():
        for index, group in ((8, sib_own), (9, sib_below), (10, sib_above), (11, sib_across)):
            wl.arrive(index, slice_of(other_rows, group), sibling)

    def clear(i, _):
        dkv16[i] = jnp.zeros((512, 256), BF16)
        return 0

    lax.fori_loop(0, 8, clear, 0)
    loads[2].wait()
    loads[3].wait()

    def span(slot):
        chunk = place.tensor(slot // 4, slot % 4)
        return pl.ds(pl.multiple_of(chunk * 256, 256), 256)

    def head_weights(slot):
        return wkv[:, :, span(slot)].reshape(256, 256)

    def gathered(total_ref, buf, weight, cb, pairs, first=False):
        for h in (0, 1):
            rows = pl.ds(h * 256, 256)
            total = None
            for du, dv in pairs:
                slot = Gather.slot(h, du, dv)
                part = dot(buf[slot, rows, :], weight(slot), 1, cb)
                total = part if total is None else total + part
            total_ref[rows, :] = total if first else total_ref[rows, :] + total

    def project(pairs, first=False):
        gathered(acc, xbuf, lambda slot: wqt[span(slot), :], 0, pairs, first)

    def project_kv(pairs, first=False):
        gathered(kacc, xbuf, head_weights, 1, pairs, first)

    def head_part(dx):
        total = dot(gz[0], wob[dx, 0], 1, 1)
        for dz in (1, 2, 3):
            total = total + dot(gz[dz], wob[dx, dz], 1, 1)
        hp[dx] = total.astype(BF16)

    def mixed_part(dz):
        total = dot(ax[0], wob[0, dz])
        for dx in (1, 2, 3):
            total = total + dot(ax[dx], wob[dx, dz])
        mp[dz] = total.astype(BF16)

    project(READY[0], True)
    xg.stage1()
    gg.stage0()
    weights_one()
    out_one()
    project(READY[1])
    xg.stage2a()
    xg.stage2b()
    weights_two()
    out_two()
    project(READY[2])
    xg.stage3()
    gg.stage1()
    weights_three()
    out_three()
    project(READY[3])
    weights_four()
    project_kv(READY[0], True)
    project_kv(READY[1])
    project_kv(READY[2])
    project_kv(READY[3])
    xg.stage4()
    project_kv(READY[4])

    kv = Links(ks, kr)
    kvall[g] = kacc[...].astype(BF16)
    kv.push(1, kvall.at[g], kvall.at[g], up)
    kv.push(2, kvall.at[g], kvall.at[g], down)
    kv.push(8, kvall.at[g], kvall.at[g], sibling)
    project(READY[4])
    qs[0] = acc[:, 0:128].astype(BF16)
    qs[1] = acc[:, 128:256].astype(BF16)
    for load in loads[4:]:
        load.wait()

    lane = lax.broadcasted_iota(jnp.int32, (1, 512), 1)
    position = lane + g * 512
    low_key = jnp.where(lane < 256, firsts[2 * g], firsts[2 * g + 1]) * 256
    end = lens[0]
    for i in range(1, 5):
        low_key = jnp.maximum(low_key, jnp.where(position >= end, end, 0))
        if i < 4:
            end = end + lens[i]
    for h in (0, 1):
        peak[h] = jnp.full((1, 512), -1e30, F32)
        sums[h] = jnp.zeros((1, 512), F32)
        outs[h] = jnp.zeros((128, 512), F32)
        dqt[h] = jnp.zeros((128, 512), F32)

    def score(k):
        @pl.when(k <= g)
        def _():
            key = lax.broadcasted_iota(jnp.int32, (512, 512), 0) + k * 512
            visible = (key >= low_key) & (key <= position)
            for h in (0, 1):
                raw = dot(kvall[k, :, 0:128], qs[h], 1, 1) * (SCALE * LOG2E)
                raw = jnp.where(visible, raw, -1e30)
                logits[k, h] = raw
                peak[h] = jnp.maximum(peak[h], jnp.max(raw, axis=0, keepdims=True))

    def weigh(k, _):
        for h in (0, 1):
            prob = jnp.exp2(logits[k, h] - peak[h])
            rounded = prob.astype(BF16)
            probs[k, h] = rounded
            sums[h] += jnp.sum(prob, axis=0, keepdims=True)
            outs[h] += dot(kvall[k, :, 128:256], rounded, 0, 0)
        return 0

    each([g], score)
    out_four()
    gg.stage2()
    head_part(2)
    head_sum.start()
    for dx in (1, 3, 0):
        head_part(dx)
    kv.arrive(1, kvall.at[below], down)
    kv.push(3, kvall.at[below, first_rows, :], kvall.at[below, first_rows, :], up)
    kv.push(9, kvall.at[below], kvall.at[below], sibling)
    kv.arrive(2, kvall.at[above], up)
    kv.push(4, kvall.at[above, last_rows, :], kvall.at[above, last_rows, :], down)
    kv.push(10, kvall.at[above], kvall.at[above], sibling)
    kv.arrive(8, kvall.at[sib_own], sibling)
    each([sib_own, below, above], score)
    head_sum.pass_on()
    kv.arrive(3, kvall.at[across, first_rows, :], down)
    kv.arrive(4, kvall.at[across, last_rows, :], up)
    kv.push(11, kvall.at[across], kvall.at[across], sibling)
    kv.arrive(9, kvall.at[sib_below], sibling)
    kv.arrive(10, kvall.at[sib_above], sibling)
    each([sib_below, sib_above, across], score)
    kv.arrive(11, kvall.at[sib_across], sibling)
    each([sib_across], score)
    lax.fori_loop(0, g + 1, weigh, 0)

    for h in (0, 1):
        inverse = 1.0 / sums[h]
        sums[h] = inverse
        outs[h] = outs[h] * inverse
        ax[0, :, h * 128 : (h + 1) * 128] = outs[h].T.astype(BF16)

    ag.stage0()
    head_sum.total(hacc)
    for h in (0, 1):
        grad_t = hacc[:, h * 128 : (h + 1) * 128].T * sums[h]
        out_t = outs[h].astype(BF16).astype(F32)
        dlt[h] = jnp.sum(grad_t * out_t, axis=0, keepdims=True)
        dos[h] = grad_t.T.astype(BF16)

    def backward(k):
        @pl.when(k <= g)
        def _():
            keys, values = kvall[k, :, 0:128], kvall[k, :, 128:256]
            key_part, value_part = None, None
            for h in (0, 1):
                prob = probs[k, h]
                dprob = dot(values, dos[h], 1, 1)
                grad = (prob.astype(F32) * (dprob - dlt[h])).astype(BF16)
                dqt[h] += dot(keys, grad, 0, 0)
                one, two = dot(grad, qs[h]), dot(prob, dos[h])
                key_part = one if h == 0 else key_part + one
                value_part = two if h == 0 else value_part + two
            dkv16[k, :, 0:128] = (key_part * SCALE).astype(BF16)
            dkv16[k, :, 128:256] = value_part.astype(BF16)

    kvg = Links(ds_, dr)

    def to_sibling(dy, group):
        kvg.push(dy, dkv16.at[group], core_in.at[dy], sibling)

    def join_cores(dy, group):
        kvg.arrive(dy, core_in.at[dy], sibling)
        dkv16[group] = (dkv16[group].astype(F32) + core_in[dy].astype(F32)).astype(BF16)

    def add_far(part, group, rows, source):
        kvg.arrive(4 + part, yfar.at[part], source)
        dkv16[group, rows, :] = (dkv16[group, rows, :].astype(F32) + yfar[part].astype(F32)).astype(BF16)

    each([sib_across, across], backward)
    to_sibling(2, sib_across)
    join_cores(2, across)
    kvg.push(4, dkv16.at[across, first_rows, :], yfar.at[0], down)
    kvg.push(5, dkv16.at[across, last_rows, :], yfar.at[1], up)
    ag.stage1()
    each([sib_below, sib_above], backward)
    to_sibling(3, sib_below)
    to_sibling(1, sib_above)
    each([below, above], backward)
    join_cores(3, below)
    add_far(0, below, first_rows, up)
    kvg.push(6, dkv16.at[below], ynear.at[0], down)
    join_cores(1, above)
    add_far(1, above, last_rows, down)
    kvg.push(7, dkv16.at[above], ynear.at[1], up)
    ag.stage2()
    mixed_part(2)
    mixed.start()
    each([sib_own], backward)
    to_sibling(0, sib_own)
    each([g], backward)
    for dz in (1, 3, 0):
        mixed_part(dz)
    mixed.pass_on()
    xg.finish()
    for h in (0, 1):
        grads[:, h * 128 : (h + 1) * 128] = (dqt[h] * SCALE).T.astype(BF16)
    join_cores(0, g)
    kvg.arrive(6, ynear.at[0], up)
    kvg.arrive(7, ynear.at[1], down)
    grads[:, 256:512] = (
        dkv16[g].astype(F32) + ynear[0].astype(F32) + ynear[1].astype(F32)
    ).astype(BF16)

    final = Scatter(place, xbuf, tfar, tnear, ts, tfs, tns)

    def spread(slot):
        xbuf[slot] = (
            dot(grads[:, 0:256], wqt[span(slot), :], 1, 1)
            + dot(grads[:, 256:512], head_weights(slot), 1, 0)
        ).astype(BF16)

    final.stage0(spread)
    mixed.total(mixed_out)
    final.stage1()
    final.stage2()
    final.stage3()
    final.stage4(grad_out)
    for links in (wl, ol, kv, kvg, gg.links, head_sum.links, ag.links, mixed.links, final):
        links.finish()


def local(tokens, w_query, w_key, w_value, w_out, out_grad, lengths, kv_first):
    return tuple(
        pl.pallas_call(
            layer,
            out_shape=(
                jax.ShapeDtypeStruct((512, 256), BF16),
                jax.ShapeDtypeStruct((512, 256), BF16),
            ),
            in_specs=[pl.BlockSpec(memory_space=pl.ANY)] * 6
            + [pl.BlockSpec(memory_space=pltpu.SMEM)] * 2,
            out_specs=[pl.BlockSpec(memory_space=pltpu.VMEM)] * 2,
            scratch_shapes=[
                pltpu.VMEM((16, 512, 256), BF16),
                pltpu.VMEM((4096, 256), BF16),
                pltpu.VMEM((2, 128, 4096), BF16),
                pltpu.VMEM((4, 4, 256, 256), BF16),
                pltpu.VMEM((512, 256), F32),
                pltpu.VMEM((512, 256), F32),
                pltpu.VMEM((512, 256), F32),
                pltpu.VMEM((2, 512, 128), BF16),
                pltpu.VMEM((8, 512, 256), BF16),
                pltpu.VMEM((8, 2, 512, 512), F32),
                pltpu.VMEM((8, 2, 512, 512), BF16),
                pltpu.VMEM((2, 1, 512), F32),
                pltpu.VMEM((2, 1, 512), F32),
                pltpu.VMEM((2, 128, 512), F32),
                pltpu.VMEM((2, 512, 128), BF16),
                pltpu.VMEM((2, 1, 512), F32),
                pltpu.VMEM((2, 128, 512), F32),
                pltpu.VMEM((8, 512, 256), BF16),
                pltpu.VMEM((4, 512, 256), BF16),
                pltpu.VMEM((2, 256, 256), BF16),
                pltpu.VMEM((2, 512, 256), BF16),
                pltpu.VMEM((512, 512), BF16),
                *SCATTER_BUFS,
                pltpu.VMEM((4, 512, 256), BF16),
                *LINE_BUFS,
                pltpu.VMEM((4, 512, 256), BF16),
                *LINE_BUFS,
                *GATHER_SEMS,
                *SCATTER_SEMS,
                *LINK_SEMS,
                *LINK_SEMS,
                *LINK_SEMS,
                pltpu.SemaphoreType.DMA((24,)),
                pltpu.SemaphoreType.DMA((24,)),
                *LINE_SEMS,
                *LINE_SEMS,
                pltpu.SemaphoreType.DMA((9,)),
            ],
            compiler_params=pltpu.CompilerParams(
                collective_id=0, has_side_effects=True, vmem_limit_bytes=62 * 1024 * 1024
            ),
            name="layer",
        )(tokens, w_query, w_key.T, w_value.T, w_out, out_grad, lengths, kv_first)
    )


def solution(mesh):
    return jax.shard_map(
        local,
        mesh=mesh,
        in_specs=(
            P("group", "tensor"),
            P(None, "tensor"),
            P(None, "tensor"),
            P(None, "tensor"),
            P("tensor", None),
            P("group", "tensor"),
            P(),
            P(),
        ),
        out_specs=(P("group", "tensor"), P("group", "tensor")),
        check_vma=False,
    )
```

```python
import jax
import jax.numpy as jnp
from jax import lax
from jax.experimental import pallas as pl
from jax.experimental.pallas import tpu as pltpu
from jax.sharding import PartitionSpec as P

HD = 128
LOG2E = 1.4426950408889634
SCALE = HD**-0.5
MESH = pl.DeviceIdType.MESH
F32 = jnp.float32
BF16 = jnp.bfloat16


def dot(a, b, ca=1, cb=0):
    return lax.dot_general(a, b, (((ca,), (cb,)), ((), ())), preferred_element_type=F32)


class Place:
    def __init__(self):
        self.g = lax.axis_index("group")
        self.t = lax.axis_index("tensor")
        self.y, self.core = self.g // 2, self.g % 2
        self.z, self.x = self.t // 4, self.t % 4

    def tensor(self, dz, dx):
        return (self.z + dz) % 4 * 4 + (self.x + dx) % 4

    def at(self, dz=0, dx=0, dy=0, dcore=0):
        return (
            (self.y + dy) % 4 * 2 + (self.core + dcore) % 2,
            self.tensor(dz, dx),
        )


def greet(place):
    barrier = pltpu.get_barrier_semaphore()
    others = [place.at(dx=1), place.at(dx=2), place.at(dx=3), place.at(dz=1), place.at(dz=3)]
    others += [place.at(dy=1), place.at(dy=3), place.at(dcore=1)]
    for other in others:
        pl.semaphore_signal(barrier, inc=1, device_id=other, device_id_type=MESH)
    pl.semaphore_wait(barrier, len(others))


class Gather:
    def __init__(self, place, own, buf, send, recv):
        self.place, self.own, self.buf, self.send_sems, self.recv_sems = place, own, buf, send, recv
        self.sent = []

    @staticmethod
    def slot(h, du, dv):
        return (dv % 4) * 4 + du % 4 if h == 0 else (du % 4) * 4 + dv % 4

    @staticmethod
    def rows(h, part):
        return pl.ds(h * 256, 256) if part is None else pl.ds(h * 256 + part * 128, 128)

    def ref(self, h, du, dv, part):
        rows = self.rows(h, part)
        if du % 4 == 0 and dv % 4 == 0:
            return self.own.at[rows, :]
        return self.buf.at[self.slot(h, du, dv), rows, :]

    def push(self, h, axis, sign, du, dv, part=None):
        if axis == 0:
            tu, tv = du - sign, dv
        else:
            tu, tv = du, dv - sign
        along_x = (axis == 0) == (h == 0)
        target = self.place.at(dx=sign) if along_x else self.place.at(dz=sign)
        copy = pltpu.make_async_remote_copy(
            src_ref=self.ref(h, du, dv, part),
            dst_ref=self.buf.at[self.slot(h, tu, tv), self.rows(h, part), :],
            send_sem=self.send_sems.at[len(self.sent)],
            recv_sem=self.recv_sems.at[h, self.slot(h, tu, tv), part or 0],
            device_id=target,
            device_id_type=MESH,
        )
        copy.start()
        self.sent.append(copy)

    def arrive(self, h, du, dv, part=None):
        ref = self.buf.at[self.slot(h, du, dv), self.rows(h, part), :]
        pltpu.make_async_remote_copy(
            src_ref=ref,
            dst_ref=ref,
            send_sem=self.send_sems.at[0],
            recv_sem=self.recv_sems.at[h, self.slot(h, du, dv), part or 0],
            device_id=self.place.at(dx=1),
            device_id_type=MESH,
        ).wait_recv()

    def far(self, h, axis, du, dv, sign):
        self.push(h, axis, sign, du, dv, 0 if sign == 1 else 1)

    def stage0(self):
        for h in (0, 1):
            for s in (1, -1):
                self.push(h, 0, s, 0, 0)
        for h in (0, 1):
            for s in (1, -1):
                self.push(h, 1, s, 0, 0)

    def stage1(self):
        for s in (1, -1):
            for h in (0, 1):
                self.arrive(h, -s, 0)
                self.far(h, 0, -s, 0, s)
                for w in (1, -1):
                    self.push(h, 1, w, -s, 0)
        for s in (1, -1):
            for h in (0, 1):
                self.arrive(h, 0, -s)
                self.far(h, 1, 0, -s, s)

    def stage2a(self):
        for h in (0, 1):
            for part in (0, 1):
                self.arrive(h, 2, 0, part)
            for w in (1, -1):
                self.push(h, 1, w, 2, 0)

    def stage2b(self):
        for s in (1, -1):
            for w in (1, -1):
                for h in (0, 1):
                    self.arrive(h, -s, -w)
                    self.far(h, 1, -s, -w, w)

    def stage3(self):
        for w in (1, -1):
            for h in (0, 1):
                self.arrive(h, 2, -w)
                self.far(h, 1, 2, -w, w)

    def stage4(self):
        for du in range(4):
            for h in (0, 1):
                for part in (0, 1):
                    self.arrive(h, du, 2, part)

    def finish(self):
        for copy in self.sent:
            copy.wait_send()


GATHER_SEMS = [pltpu.SemaphoreType.DMA((40,)), pltpu.SemaphoreType.DMA((2, 16, 2))]

READY = [
    [(0, 0)],
    [(1, 0), (3, 0), (0, 1), (0, 3)],
    [(2, 0), (1, 1), (1, 3), (3, 1), (3, 3)],
    [(2, 1), (2, 3)],
    [(0, 2), (1, 2), (2, 2), (3, 2)],
]


class Scatter:
    def __init__(self, place, buf, far, near, send, far_sems, near_sems):
        self.place, self.buf, self.far, self.near = place, buf, far, near
        self.send_sems, self.far_sems, self.near_sems = send, far_sems, near_sems
        self.sent = []

    def where(self, h, line, offset):
        return Gather.slot(h, line, offset) if line < 4 else Gather.slot(h, offset, 0)

    def push(self, h, line, sign, src, dst, sem):
        along_x = (line == 4) == (h == 0)
        target = self.place.at(dx=sign) if along_x else self.place.at(dz=sign)
        copy = pltpu.make_async_remote_copy(
            src_ref=src,
            dst_ref=dst,
            send_sem=self.send_sems.at[len(self.sent)],
            recv_sem=sem,
            device_id=target,
            device_id_type=MESH,
        )
        copy.start()
        self.sent.append(copy)

    def arrive(self, ref, sem):
        pltpu.make_async_remote_copy(
            src_ref=ref,
            dst_ref=ref,
            send_sem=self.send_sems.at[0],
            recv_sem=sem,
            device_id=self.place.at(dx=1),
            device_id_type=MESH,
        ).wait_recv()

    def start(self, h, line):
        slot = self.where(h, line, 2)
        for part, sign in ((0, -1), (1, 1)):
            self.push(
                h, line, sign,
                self.buf.at[slot, Gather.rows(h, part), :],
                self.far.at[h, line, part],
                self.far_sems.at[h, line, part],
            )

    def pass_on(self, h, line):
        for part, sign in ((0, -1), (1, 1)):
            slot = self.where(h, line, sign)
            rows = Gather.rows(h, part)
            self.arrive(self.far.at[h, line, part], self.far_sems.at[h, line, part])
            self.buf[slot, rows, :] = (
                self.buf[slot, rows, :].astype(F32) + self.far[h, line, part].astype(F32)
            ).astype(BF16)
            self.push(
                h, line, sign,
                self.buf.at[slot, Gather.rows(h, None), :],
                self.near.at[h, line, part],
                self.near_sems.at[h, line, part],
            )

    def total(self, h, line):
        for part in (0, 1):
            self.arrive(self.near.at[h, line, part], self.near_sems.at[h, line, part])
        slot = self.where(h, line, 0)
        rows = Gather.rows(h, None)
        value = (
            self.buf[slot, rows, :].astype(F32)
            + self.near[h, line, 0].astype(F32)
            + self.near[h, line, 1].astype(F32)
        ).astype(BF16)
        return slot, rows, value

    def stage0(self, fill):
        done = []
        for line in (2, 1, 3, 0):
            for h in (0, 1):
                slot = self.where(h, line, 2)
                if slot not in done:
                    fill(slot)
                    done.append(slot)
                self.start(h, line)
        for slot in range(16):
            if slot not in done:
                fill(slot)

    def stage1(self):
        for line in (2, 1, 3, 0):
            for h in (0, 1):
                self.pass_on(h, line)

    def settle(self, line):
        for h in (0, 1):
            slot, rows, value = self.total(h, line)
            self.buf[slot, rows, :] = value

    def stage2(self):
        self.settle(2)
        for h in (0, 1):
            self.start(h, 4)

    def stage3(self):
        self.settle(1)
        self.settle(3)
        for h in (0, 1):
            self.pass_on(h, 4)

    def stage4(self, out):
        self.settle(0)
        for h in (0, 1):
            _, rows, value = self.total(h, 4)
            out[rows, :] = value

    def finish(self):
        for copy in self.sent:
            copy.wait_send()


SCATTER_BUFS = [pltpu.VMEM((2, 5, 2, 128, 256), BF16), pltpu.VMEM((2, 5, 2, 256, 256), BF16)]
SCATTER_SEMS = [
    pltpu.SemaphoreType.DMA((40,)),
    pltpu.SemaphoreType.DMA((2, 5, 2)),
    pltpu.SemaphoreType.DMA((2, 5, 2)),
]


class Links:
    def __init__(self, send, recv):
        self.send_sems, self.recv_sems, self.sent = send, recv, []

    def push(self, index, src, dst, target):
        copy = pltpu.make_async_remote_copy(
            src_ref=src,
            dst_ref=dst,
            send_sem=self.send_sems.at[index],
            recv_sem=self.recv_sems.at[index],
            device_id=target,
            device_id_type=MESH,
        )
        copy.start()
        self.sent.append(copy)

    def arrive(self, index, ref, source):
        pltpu.make_async_remote_copy(
            src_ref=ref,
            dst_ref=ref,
            send_sem=self.send_sems.at[index],
            recv_sem=self.recv_sems.at[index],
            device_id=source,
            device_id_type=MESH,
        ).wait_recv()

    def finish(self):
        for copy in self.sent:
            copy.wait_send()


class LineGather:
    def __init__(self, place, along_x, own, buf, send, recv):
        self.links, self.own, self.buf = Links(send, recv), own, buf
        self.next = lambda sign: place.at(dx=sign) if along_x else place.at(dz=sign)

    def stage0(self):
        for r in (0, 1):
            for s in (1, -1):
                rows = Gather.rows(r, None)
                self.links.push(
                    r * 4 + (s < 0), self.own.at[rows, :], self.buf.at[-s % 4, rows, :], self.next(s)
                )

    def stage1(self, halves=(0, 1)):
        for r in halves:
            for part, s in ((0, 1), (1, -1)):
                whole, rows = Gather.rows(r, None), Gather.rows(r, part)
                self.links.arrive(r * 4 + (s < 0), self.buf.at[-s % 4, whole, :], self.next(-s))
                self.links.push(
                    r * 4 + 2 + part, self.buf.at[-s % 4, rows, :], self.buf.at[2, rows, :], self.next(s)
                )

    def stage2(self, halves=(0, 1)):
        for r in halves:
            for part, s in ((0, 1), (1, -1)):
                self.links.arrive(r * 4 + 2 + part, self.buf.at[2, Gather.rows(r, part), :], self.next(-s))


class LineScatter:
    def __init__(self, place, along_x, buf, far, near, send, recv):
        self.links, self.buf, self.far, self.near = Links(send, recv), buf, far, near
        self.next = lambda sign: place.at(dx=sign) if along_x else place.at(dz=sign)

    def start(self, halves=(0, 1)):
        for r in halves:
            for part, s in ((0, -1), (1, 1)):
                self.links.push(
                    r * 4 + part, self.buf.at[2, Gather.rows(r, part), :], self.far.at[r, part], self.next(s)
                )

    def pass_on(self, halves=(0, 1)):
        for r in halves:
            for part, s in ((0, -1), (1, 1)):
                whole, rows = Gather.rows(r, None), Gather.rows(r, part)
                self.links.arrive(r * 4 + part, self.far.at[r, part], self.next(-s))
                self.buf[s % 4, rows, :] = (
                    self.buf[s % 4, rows, :].astype(F32) + self.far[r, part].astype(F32)
                ).astype(BF16)
                self.links.push(
                    r * 4 + 2 + part, self.buf.at[s % 4, whole, :], self.near.at[r, part], self.next(s)
                )

    def total(self, out):
        for r in (0, 1):
            rows = Gather.rows(r, None)
            for part, s in ((0, -1), (1, 1)):
                self.links.arrive(r * 4 + 2 + part, self.near.at[r, part], self.next(-s))
            out[rows, :] = (
                self.buf[0, rows, :].astype(F32)
                + self.near[r, 0].astype(F32)
                + self.near[r, 1].astype(F32)
            ).astype(out.dtype)


LINE_BUFS = [
    pltpu.VMEM((4, 512, 256), BF16),
    pltpu.VMEM((2, 2, 128, 256), BF16),
    pltpu.VMEM((2, 2, 256, 256), BF16),
]
LINE_SEMS = [pltpu.SemaphoreType.DMA((8,))] * 4

LINK_SEMS = [pltpu.SemaphoreType.DMA((16,)), pltpu.SemaphoreType.DMA((16,))]


def each(items, body):
    def step(i, _):
        item = items[0]
        for j in range(1, len(items)):
            item = jnp.where(i == j, items[j], item)
        body(item)
        return 0

    lax.fori_loop(0, len(items), step, 0)


def layer(
    tok, wq, wk, wv, wo, og, lens, firsts, mixed_out, grad_out,
    xbuf, wqt, wkv, wob, acc, kacc, hacc,
    qs, kvall, logits, probs, peak, sums, outs, grad_t, dos, dlt, dqt, dkv16, core_in,
    yfar, ynear, grads, tfar, tnear,
    gz, hp, hfar, hnear, ax, mp, mfar, mnear,
    xs, xr, ts, tfs, tns, ws, wr, ks, kr, ds_, dr, os_, or_,
    gs, gr, hs, hr, as_, ar, ms, mr, lsem,
):
    place = Place()
    g = place.g
    half = place.t % 2
    own_rows = pl.ds(pl.multiple_of(half * 64, 64), 64)
    other_rows = pl.ds(pl.multiple_of((1 - half) * 64, 64), 64)
    loads = [
        pltpu.make_async_copy(wk, wkv.at[0, own_rows, :], lsem.at[1]),
        pltpu.make_async_copy(wv, wkv.at[1, own_rows, :], lsem.at[2]),
        pltpu.make_async_copy(tok, xbuf.at[0], lsem.at[0]),
        pltpu.make_async_copy(wq, wqt, lsem.at[3]),
        pltpu.make_async_copy(og, gz.at[0], lsem.at[4]),
    ]

    def columns_of(dz, dx):
        return pl.ds(pl.multiple_of(place.tensor(dz, dx) * 256, 256), 256)

    for dz in range(4):
        loads.append(pltpu.make_async_copy(wo.at[:, columns_of(dz, 0)], wob.at[0, dz], lsem.at[5 + dz]))
    for load in loads:
        load.start()
    greet(place)
    xg = Gather(place, tok, xbuf, xs, xr)
    gg = LineGather(place, False, og, gz, gs, gr)
    head_sum = LineScatter(place, True, hp, hfar, hnear, hs, hr)
    ag = LineGather(place, True, ax.at[0], ax, as_, ar)
    mixed = LineScatter(place, False, mp, mfar, mnear, ms, mr)
    xg.stage0()

    def group_at(dy, dcore=0):
        return place.at(dy=dy, dcore=dcore)[0]

    partner = (g, place.t + 1 - 2 * half)
    sibling = place.at(dcore=1)
    up, down = place.at(dy=1), place.at(dy=3)
    below, above, across = group_at(3), group_at(1), group_at(2)
    sib_own, sib_below, sib_above, sib_across = (group_at(dy, 1) for dy in (0, 3, 1, 2))
    first_rows, last_rows = pl.ds(0, 256), pl.ds(256, 256)

    def slice_of(rows, group, kind=None):
        columns = pl.ds(pl.multiple_of(group * 512, 512), 512)
        return wkv.at[pl.ds(0, 2) if kind is None else kind, rows, columns]

    wl = Links(ws, wr)
    loads[0].wait()
    loads[1].wait()
    wl.push(0, slice_of(own_rows, g), slice_of(own_rows, g), partner)

    ol = Links(os_, or_)
    own_slice = pl.ds(pl.multiple_of(g * 32, 32), 32)
    for d in (1, 3, 2):
        for dz in range(4):
            ol.push(
                (d - 1) * 4 + dz,
                wo.at[own_slice, columns_of(dz, d)],
                wob.at[4 - d, dz, own_slice, :],
                place.at(dx=d),
            )

    def out_slice(group, part=None):
        if part is None:
            rows = pl.ds(pl.multiple_of(group * 32, 32), 32)
        else:
            rows = pl.ds(pl.multiple_of(group * 32 + part * 16, 16), 16)
        return wob.at[pl.ds(1, 3), pl.ds(0, 4), rows, :]

    def out_one():
        for d in (1, 3, 2):
            for dz in range(4):
                ol.arrive((d - 1) * 4 + dz, wob.at[4 - d, dz, own_slice, :], place.at(dx=4 - d))
        ref = out_slice(g)
        ol.push(12, ref, ref, up)
        ol.push(13, ref, ref, down)
        ol.push(20, ref, ref, sibling)

    def out_two():
        ref = out_slice(below)
        ol.arrive(12, ref, down)
        ol.push(14, out_slice(below, 0), out_slice(below, 0), up)
        ol.push(21, ref, ref, sibling)
        ref = out_slice(above)
        ol.arrive(13, ref, up)
        ol.push(15, out_slice(above, 1), out_slice(above, 1), down)
        ol.push(22, ref, ref, sibling)

    def out_three():
        ol.arrive(14, out_slice(across, 0), down)
        ol.arrive(15, out_slice(across, 1), up)
        ref = out_slice(across)
        ol.push(23, ref, ref, sibling)

    def out_four():
        for index, group in ((20, sib_own), (21, sib_below), (22, sib_above), (23, sib_across)):
            ol.arrive(index, out_slice(group), sibling)

    def weights_one():
        ref = slice_of(other_rows, g)
        wl.arrive(0, ref, partner)
        wl.push(1, ref, ref, up)
        wl.push(2, ref, ref, down)
        wl.push(8, ref, ref, sibling)

    def weights_two():
        ref = slice_of(other_rows, below)
        wl.arrive(1, ref, down)
        wl.push(3, slice_of(other_rows, below, 0), slice_of(other_rows, below, 0), up)
        wl.push(9, ref, ref, sibling)
        ref = slice_of(other_rows, above)
        wl.arrive(2, ref, up)
        wl.push(4, slice_of(other_rows, above, 1), slice_of(other_rows, above, 1), down)
        wl.push(10, ref, ref, sibling)

    def weights_three():
        wl.arrive(3, slice_of(other_rows, across, 0), down)
        wl.arrive(4, slice_of(other_rows, across, 1), up)
        ref = slice_of(other_rows, across)
        wl.push(11, ref, ref, sibling)

    def weights_four():
        for index, group in ((8, sib_own), (9, sib_below), (10, sib_above), (11, sib_across)):
            wl.arrive(index, slice_of(other_rows, group), sibling)

    def clear(i, _):
        dkv16[i] = jnp.zeros((512, 256), BF16)
        return 0

    lax.fori_loop(0, 8, clear, 0)
    loads[2].wait()
    loads[3].wait()

    def span(slot):
        chunk = place.tensor(slot // 4, slot % 4)
        return pl.ds(pl.multiple_of(chunk * 256, 256), 256)

    def head_weights(slot):
        return wkv[:, :, span(slot)].reshape(256, 256)

    def gathered(total_ref, buf, weight, cb, pairs, first=False):
        for h in (0, 1):
            rows = pl.ds(h * 256, 256)
            total = None
            for du, dv in pairs:
                slot = Gather.slot(h, du, dv)
                part = dot(buf[slot, rows, :], weight(slot), 1, cb)
                total = part if total is None else total + part
            total_ref[rows, :] = total if first else total_ref[rows, :] + total

    def project(pairs, first=False):
        gathered(acc, xbuf, lambda slot: wqt[span(slot), :], 0, pairs, first)

    def project_kv(pairs, first=False):
        gathered(kacc, xbuf, head_weights, 1, pairs, first)

    def head_part(dx):
        total = dot(gz[0], wob[dx, 0], 1, 1)
        for dz in (1, 2, 3):
            total = total + dot(gz[dz], wob[dx, dz], 1, 1)
        hp[dx] = total.astype(BF16)

    def mixed_part(dz, r):
        rows = pl.ds(r * 256, 256)
        total = dot(ax[0, rows, :], wob[0, dz])
        for dx in (1, 2, 3):
            total = total + dot(ax[dx, rows, :], wob[dx, dz])
        mp[dz, rows, :] = total.astype(BF16)

    project(READY[0], True)
    xg.stage1()
    gg.stage0()
    weights_one()
    out_one()
    project(READY[1])
    xg.stage2a()
    xg.stage2b()
    weights_two()
    out_two()
    project(READY[2])
    xg.stage3()
    gg.stage1()
    weights_three()
    out_three()
    project(READY[3])
    weights_four()
    project_kv(READY[0], True)
    project_kv(READY[1])
    project_kv(READY[2])
    project_kv(READY[3])
    xg.stage4()
    project_kv(READY[4])

    kv = Links(ks, kr)
    kvall[g] = kacc[...].astype(BF16)
    kv.push(1, kvall.at[g], kvall.at[g], up)
    kv.push(2, kvall.at[g], kvall.at[g], down)
    kv.push(8, kvall.at[g], kvall.at[g], sibling)
    project(READY[4])
    qs[0] = acc[:, 0:128].astype(BF16)
    qs[1] = acc[:, 128:256].astype(BF16)
    for load in loads[4:]:
        load.wait()

    lane = lax.broadcasted_iota(jnp.int32, (1, 512), 1)
    position = lane + g * 512
    low_key = jnp.where(lane < 256, firsts[2 * g], firsts[2 * g + 1]) * 256
    end = lens[0]
    for i in range(1, 5):
        low_key = jnp.maximum(low_key, jnp.where(position >= end, end, 0))
        if i < 4:
            end = end + lens[i]
    for h in (0, 1):
        peak[h] = jnp.full((1, 512), -1e30, F32)
        sums[h] = jnp.zeros((1, 512), F32)
        outs[h] = jnp.zeros((128, 512), F32)
        dqt[h] = jnp.zeros((128, 512), F32)

    def score(k):
        @pl.when(k <= g)
        def _():
            key = lax.broadcasted_iota(jnp.int32, (512, 512), 0) + k * 512
            visible = (key >= low_key) & (key <= position)
            for h in (0, 1):
                raw = dot(kvall[k, :, 0:128], qs[h], 1, 1) * (SCALE * LOG2E)
                raw = jnp.where(visible, raw, -1e30)
                logits[k, h] = raw
                peak[h] = jnp.maximum(peak[h], jnp.max(raw, axis=0, keepdims=True))

    def weigh(k, _):
        for h in (0, 1):
            prob = jnp.exp2(logits[k, h] - peak[h])
            rounded = prob.astype(BF16)
            probs[k, h] = rounded
            sums[h] += jnp.sum(prob, axis=0, keepdims=True)
            outs[h] += dot(kvall[k, :, 128:256], rounded, 0, 0)
        return 0

    each([g], score)
    out_four()
    gg.stage2()
    head_part(2)
    head_sum.start()
    for dx in (1, 3, 0):
        head_part(dx)
    kv.arrive(1, kvall.at[below], down)
    kv.push(3, kvall.at[below, first_rows, :], kvall.at[below, first_rows, :], up)
    kv.push(9, kvall.at[below], kvall.at[below], sibling)
    kv.arrive(2, kvall.at[above], up)
    kv.push(4, kvall.at[above, last_rows, :], kvall.at[above, last_rows, :], down)
    kv.push(10, kvall.at[above], kvall.at[above], sibling)
    kv.arrive(8, kvall.at[sib_own], sibling)
    each([sib_own, below, above], score)
    head_sum.pass_on()
    kv.arrive(3, kvall.at[across, first_rows, :], down)
    kv.arrive(4, kvall.at[across, last_rows, :], up)
    kv.push(11, kvall.at[across], kvall.at[across], sibling)
    kv.arrive(9, kvall.at[sib_below], sibling)
    kv.arrive(10, kvall.at[sib_above], sibling)
    each([sib_below, sib_above, across], score)
    kv.arrive(11, kvall.at[sib_across], sibling)
    each([sib_across], score)
    lax.fori_loop(0, (g + 1) // 2, weigh, 0)
    head_sum.total(hacc)
    for h in (0, 1):
        grad_t[h] = hacc[:, h * 128 : (h + 1) * 128].T
    lax.fori_loop((g + 1) // 2, g + 1, weigh, 0)

    for h in (0, 1):
        inverse = 1.0 / sums[h]
        outs[h] = outs[h] * inverse
        out_t = outs[h].astype(BF16).astype(F32)
        dlt[h] = jnp.sum(grad_t[h] * out_t, axis=0, keepdims=True) * inverse
        column = jnp.broadcast_to(inverse, (8, 512)).T[:, 0:1]
        dos[h] = (hacc[:, h * 128 : (h + 1) * 128] * column).astype(BF16)

    def backward(k):
        @pl.when(k <= g)
        def _():
            keys, values = kvall[k, :, 0:128], kvall[k, :, 128:256]
            key_part, value_part = None, None
            for h in (0, 1):
                prob = probs[k, h]
                dprob = dot(values, dos[h], 1, 1)
                grad = (prob.astype(F32) * (dprob - dlt[h])).astype(BF16)
                dqt[h] += dot(keys, grad, 0, 0)
                one, two = dot(grad, qs[h]), dot(prob, dos[h])
                key_part = one if h == 0 else key_part + one
                value_part = two if h == 0 else value_part + two
            dkv16[k, :, 0:128] = (key_part * SCALE).astype(BF16)
            dkv16[k, :, 128:256] = value_part.astype(BF16)

    kvg = Links(ds_, dr)

    def to_sibling(dy, group):
        kvg.push(dy, dkv16.at[group], core_in.at[dy], sibling)

    def join_cores(dy, group):
        kvg.arrive(dy, core_in.at[dy], sibling)
        dkv16[group] = (dkv16[group].astype(F32) + core_in[dy].astype(F32)).astype(BF16)

    def add_far(part, group, rows, source):
        kvg.arrive(4 + part, yfar.at[part], source)
        dkv16[group, rows, :] = (dkv16[group, rows, :].astype(F32) + yfar[part].astype(F32)).astype(BF16)

    for h in (0, 1):
        ax[0, :, h * 128 : (h + 1) * 128] = outs[h].T.astype(BF16)
    ag.stage0()
    each([sib_across], backward)
    to_sibling(2, sib_across)
    each([across, sib_below], backward)
    to_sibling(3, sib_below)
    join_cores(2, across)
    kvg.push(4, dkv16.at[across, first_rows, :], yfar.at[0], down)
    kvg.push(5, dkv16.at[across, last_rows, :], yfar.at[1], up)
    ag.stage1((0,))
    each([sib_above, below], backward)
    to_sibling(1, sib_above)
    ag.stage1((1,))
    join_cores(3, below)
    add_far(0, below, first_rows, up)
    kvg.push(6, dkv16.at[below], ynear.at[0], down)
    each([above], backward)
    join_cores(1, above)
    add_far(1, above, last_rows, down)
    kvg.push(7, dkv16.at[above], ynear.at[1], up)
    ag.stage2((0,))
    mixed_part(2, 0)
    mixed.start((0,))
    each([sib_own], backward)
    to_sibling(0, sib_own)
    ag.stage2((1,))
    mixed_part(2, 1)
    mixed.start((1,))
    for r in (0, 1):
        mixed_part(1, r)
        mixed_part(3, r)
    each([g], backward)
    mixed.pass_on((0,))
    for r in (0, 1):
        mixed_part(0, r)
    mixed.pass_on((1,))
    xg.finish()
    for h in (0, 1):
        grads[:, h * 128 : (h + 1) * 128] = (dqt[h] * SCALE).T.astype(BF16)
    join_cores(0, g)
    kvg.arrive(6, ynear.at[0], up)
    kvg.arrive(7, ynear.at[1], down)
    grads[:, 256:512] = (
        dkv16[g].astype(F32) + ynear[0].astype(F32) + ynear[1].astype(F32)
    ).astype(BF16)

    final = Scatter(place, xbuf, tfar, tnear, ts, tfs, tns)

    def spread(slot):
        xbuf[slot] = (
            dot(grads[:, 0:256], wqt[span(slot), :], 1, 1)
            + dot(grads[:, 256:512], head_weights(slot), 1, 0)
        ).astype(BF16)

    final.stage0(spread)
    mixed.total(mixed_out)
    final.stage1()
    final.stage2()
    final.stage3()
    final.stage4(grad_out)
    for links in (wl, ol, kv, kvg, gg.links, head_sum.links, ag.links, mixed.links, final):
        links.finish()


def hand_on(mixed, grad):
    def body(a, b, c, d):
        c[...] = a[...]
        d[...] = b[...]

    spec = pl.BlockSpec((512, 256), lambda: (0, 0))
    return pl.pallas_call(
        body,
        out_shape=(jax.ShapeDtypeStruct((512, 256), BF16),) * 2,
        in_specs=[spec] * 2,
        out_specs=[spec] * 2,
        name="hand_on",
    )(mixed, grad)


def local(tokens, w_query, w_key, w_value, w_out, out_grad, lengths, kv_first):
    return hand_on(
        *pl.pallas_call(
            layer,
            out_shape=(
                jax.ShapeDtypeStruct((512, 256), BF16),
                jax.ShapeDtypeStruct((512, 256), BF16),
            ),
            in_specs=[pl.BlockSpec(memory_space=pl.ANY)] * 6
            + [pl.BlockSpec(memory_space=pltpu.SMEM)] * 2,
            out_specs=[pl.BlockSpec(memory_space=pltpu.VMEM)] * 2,
            scratch_shapes=[
                pltpu.VMEM((16, 512, 256), BF16),
                pltpu.VMEM((4096, 256), BF16),
                pltpu.VMEM((2, 128, 4096), BF16),
                pltpu.VMEM((4, 4, 256, 256), BF16),
                pltpu.VMEM((512, 256), F32),
                pltpu.VMEM((512, 256), F32),
                pltpu.VMEM((512, 256), F32),
                pltpu.VMEM((2, 512, 128), BF16),
                pltpu.VMEM((8, 512, 256), BF16),
                pltpu.VMEM((8, 2, 512, 512), F32),
                pltpu.VMEM((8, 2, 512, 512), BF16),
                pltpu.VMEM((2, 1, 512), F32),
                pltpu.VMEM((2, 1, 512), F32),
                pltpu.VMEM((2, 128, 512), F32),
                pltpu.VMEM((2, 128, 512), F32),
                pltpu.VMEM((2, 512, 128), BF16),
                pltpu.VMEM((2, 1, 512), F32),
                pltpu.VMEM((2, 128, 512), F32),
                pltpu.VMEM((8, 512, 256), BF16),
                pltpu.VMEM((4, 512, 256), BF16),
                pltpu.VMEM((2, 256, 256), BF16),
                pltpu.VMEM((2, 512, 256), BF16),
                pltpu.VMEM((512, 512), BF16),
                *SCATTER_BUFS,
                pltpu.VMEM((4, 512, 256), BF16),
                *LINE_BUFS,
                pltpu.VMEM((4, 512, 256), BF16),
                *LINE_BUFS,
                *GATHER_SEMS,
                *SCATTER_SEMS,
                *LINK_SEMS,
                *LINK_SEMS,
                *LINK_SEMS,
                pltpu.SemaphoreType.DMA((24,)),
                pltpu.SemaphoreType.DMA((24,)),
                *LINE_SEMS,
                *LINE_SEMS,
                pltpu.SemaphoreType.DMA((9,)),
            ],
            compiler_params=pltpu.CompilerParams(
                collective_id=0, has_side_effects=True, vmem_limit_bytes=62 * 1024 * 1024
            ),
            name="layer",
        )(tokens, w_query, w_key.T, w_value.T, w_out, out_grad, lengths, kv_first)
    )


def solution(mesh):
    return jax.shard_map(
        local,
        mesh=mesh,
        in_specs=(
            P("group", "tensor"),
            P(None, "tensor"),
            P(None, "tensor"),
            P(None, "tensor"),
            P("tensor", None),
            P("group", "tensor"),
            P(),
            P(),
        ),
        out_specs=(P("group", "tensor"), P("group", "tensor")),
        check_vma=False,
    )
```

```python
import jax
import jax.numpy as jnp
from jax import lax
from jax.experimental import pallas as pl
from jax.experimental.pallas import tpu as pltpu
from jax.sharding import PartitionSpec as P

HD = 128
LOG2E = 1.4426950408889634
SCALE = HD**-0.5
MESH = pl.DeviceIdType.MESH
F32 = jnp.float32
BF16 = jnp.bfloat16


def dot(a, b, ca=1, cb=0):
    return lax.dot_general(a, b, (((ca,), (cb,)), ((), ())), preferred_element_type=F32)


class Place:
    def __init__(self):
        self.g = lax.axis_index("group")
        self.t = lax.axis_index("tensor")
        self.y, self.core = self.g // 2, self.g % 2
        self.z, self.x = self.t // 4, self.t % 4

    def tensor(self, dz, dx):
        return (self.z + dz) % 4 * 4 + (self.x + dx) % 4

    def at(self, dz=0, dx=0, dy=0, dcore=0):
        return (
            (self.y + dy) % 4 * 2 + (self.core + dcore) % 2,
            self.tensor(dz, dx),
        )


def greet(place):
    barrier = pltpu.get_barrier_semaphore()
    others = [place.at(dx=1), place.at(dx=2), place.at(dx=3), place.at(dz=1), place.at(dz=3)]
    others += [place.at(dy=1), place.at(dy=3), place.at(dcore=1)]
    for other in others:
        pl.semaphore_signal(barrier, inc=1, device_id=other, device_id_type=MESH)
    pl.semaphore_wait(barrier, len(others))


class Gather:
    def __init__(self, place, own, buf, send, recv):
        self.place, self.own, self.buf, self.send_sems, self.recv_sems = place, own, buf, send, recv
        self.sent = []

    @staticmethod
    def slot(h, du, dv):
        return (dv % 4) * 4 + du % 4 if h == 0 else (du % 4) * 4 + dv % 4

    @staticmethod
    def rows(h, part):
        return pl.ds(h * 256, 256) if part is None else pl.ds(h * 256 + part * 128, 128)

    def ref(self, h, du, dv, part):
        rows = self.rows(h, part)
        if du % 4 == 0 and dv % 4 == 0:
            return self.own.at[rows, :]
        return self.buf.at[self.slot(h, du, dv), rows, :]

    def push(self, h, axis, sign, du, dv, part=None):
        if axis == 0:
            tu, tv = du - sign, dv
        else:
            tu, tv = du, dv - sign
        along_x = (axis == 0) == (h == 0)
        target = self.place.at(dx=sign) if along_x else self.place.at(dz=sign)
        copy = pltpu.make_async_remote_copy(
            src_ref=self.ref(h, du, dv, part),
            dst_ref=self.buf.at[self.slot(h, tu, tv), self.rows(h, part), :],
            send_sem=self.send_sems.at[len(self.sent)],
            recv_sem=self.recv_sems.at[h, self.slot(h, tu, tv), part or 0],
            device_id=target,
            device_id_type=MESH,
        )
        copy.start()
        self.sent.append(copy)

    def arrive(self, h, du, dv, part=None):
        ref = self.buf.at[self.slot(h, du, dv), self.rows(h, part), :]
        pltpu.make_async_remote_copy(
            src_ref=ref,
            dst_ref=ref,
            send_sem=self.send_sems.at[0],
            recv_sem=self.recv_sems.at[h, self.slot(h, du, dv), part or 0],
            device_id=self.place.at(dx=1),
            device_id_type=MESH,
        ).wait_recv()

    def far(self, h, axis, du, dv, sign):
        self.push(h, axis, sign, du, dv, 0 if sign == 1 else 1)

    def stage0(self):
        for h in (0, 1):
            for s in (1, -1):
                self.push(h, 0, s, 0, 0)
        for h in (0, 1):
            for s in (1, -1):
                self.push(h, 1, s, 0, 0)

    def stage1(self):
        for s in (1, -1):
            for h in (0, 1):
                self.arrive(h, -s, 0)
                self.far(h, 0, -s, 0, s)
                for w in (1, -1):
                    self.push(h, 1, w, -s, 0)
        for s in (1, -1):
            for h in (0, 1):
                self.arrive(h, 0, -s)
                self.far(h, 1, 0, -s, s)

    def stage2a(self):
        for h in (0, 1):
            for part in (0, 1):
                self.arrive(h, 2, 0, part)
            for w in (1, -1):
                self.push(h, 1, w, 2, 0)

    def stage2b(self):
        for s in (1, -1):
            for w in (1, -1):
                for h in (0, 1):
                    self.arrive(h, -s, -w)
                    self.far(h, 1, -s, -w, w)

    def stage3(self):
        for w in (1, -1):
            for h in (0, 1):
                self.arrive(h, 2, -w)
                self.far(h, 1, 2, -w, w)

    def stage4(self):
        for du in range(4):
            for h in (0, 1):
                for part in (0, 1):
                    self.arrive(h, du, 2, part)

    def finish(self):
        for copy in self.sent:
            copy.wait_send()


GATHER_SEMS = [pltpu.SemaphoreType.DMA((40,)), pltpu.SemaphoreType.DMA((2, 16, 2))]

READY = [
    [(0, 0)],
    [(1, 0), (3, 0), (0, 1), (0, 3)],
    [(2, 0), (1, 1), (1, 3), (3, 1), (3, 3)],
    [(2, 1), (2, 3)],
    [(0, 2), (1, 2), (2, 2), (3, 2)],
]


class Scatter:
    def __init__(self, place, buf, far, near, send, far_sems, near_sems):
        self.place, self.buf, self.far, self.near = place, buf, far, near
        self.send_sems, self.far_sems, self.near_sems = send, far_sems, near_sems
        self.sent = []

    def where(self, h, line, offset):
        return Gather.slot(h, line, offset) if line < 4 else Gather.slot(h, offset, 0)

    def push(self, h, line, sign, src, dst, sem):
        along_x = (line == 4) == (h == 0)
        target = self.place.at(dx=sign) if along_x else self.place.at(dz=sign)
        copy = pltpu.make_async_remote_copy(
            src_ref=src,
            dst_ref=dst,
            send_sem=self.send_sems.at[len(self.sent)],
            recv_sem=sem,
            device_id=target,
            device_id_type=MESH,
        )
        copy.start()
        self.sent.append(copy)

    def arrive(self, ref, sem):
        pltpu.make_async_remote_copy(
            src_ref=ref,
            dst_ref=ref,
            send_sem=self.send_sems.at[0],
            recv_sem=sem,
            device_id=self.place.at(dx=1),
            device_id_type=MESH,
        ).wait_recv()

    def start(self, h, line):
        slot = self.where(h, line, 2)
        for part, sign in ((0, -1), (1, 1)):
            self.push(
                h, line, sign,
                self.buf.at[slot, Gather.rows(h, part), :],
                self.far.at[h, line, part],
                self.far_sems.at[h, line, part],
            )

    def pass_on(self, h, line):
        for part, sign in ((0, -1), (1, 1)):
            slot = self.where(h, line, sign)
            rows = Gather.rows(h, part)
            self.arrive(self.far.at[h, line, part], self.far_sems.at[h, line, part])
            self.buf[slot, rows, :] = (
                self.buf[slot, rows, :].astype(F32) + self.far[h, line, part].astype(F32)
            ).astype(BF16)
            self.push(
                h, line, sign,
                self.buf.at[slot, Gather.rows(h, None), :],
                self.near.at[h, line, part],
                self.near_sems.at[h, line, part],
            )

    def total(self, h, line):
        for part in (0, 1):
            self.arrive(self.near.at[h, line, part], self.near_sems.at[h, line, part])
        slot = self.where(h, line, 0)
        rows = Gather.rows(h, None)
        value = (
            self.buf[slot, rows, :].astype(F32)
            + self.near[h, line, 0].astype(F32)
            + self.near[h, line, 1].astype(F32)
        ).astype(BF16)
        return slot, rows, value

    def stage0(self, fill):
        done = []
        for line in (2, 1, 3, 0):
            for h in (0, 1):
                slot = self.where(h, line, 2)
                if slot not in done:
                    fill(slot)
                    done.append(slot)
                self.start(h, line)
        for slot in range(16):
            if slot not in done:
                fill(slot)

    def stage1(self):
        for line in (2, 1, 3, 0):
            for h in (0, 1):
                self.pass_on(h, line)

    def settle(self, line):
        for h in (0, 1):
            slot, rows, value = self.total(h, line)
            self.buf[slot, rows, :] = value

    def stage2(self):
        self.settle(2)
        for h in (0, 1):
            self.start(h, 4)

    def stage3(self):
        self.settle(1)
        self.settle(3)
        for h in (0, 1):
            self.pass_on(h, 4)

    def stage4(self, out):
        self.settle(0)
        for h in (0, 1):
            _, rows, value = self.total(h, 4)
            out[rows, :] = value

    def finish(self):
        for copy in self.sent:
            copy.wait_send()


SCATTER_BUFS = [pltpu.VMEM((2, 5, 2, 128, 256), BF16), pltpu.VMEM((2, 5, 2, 256, 256), BF16)]
SCATTER_SEMS = [
    pltpu.SemaphoreType.DMA((40,)),
    pltpu.SemaphoreType.DMA((2, 5, 2)),
    pltpu.SemaphoreType.DMA((2, 5, 2)),
]


class Links:
    def __init__(self, send, recv):
        self.send_sems, self.recv_sems, self.sent = send, recv, []

    def push(self, index, src, dst, target):
        copy = pltpu.make_async_remote_copy(
            src_ref=src,
            dst_ref=dst,
            send_sem=self.send_sems.at[index],
            recv_sem=self.recv_sems.at[index],
            device_id=target,
            device_id_type=MESH,
        )
        copy.start()
        self.sent.append(copy)

    def arrive(self, index, ref, source):
        pltpu.make_async_remote_copy(
            src_ref=ref,
            dst_ref=ref,
            send_sem=self.send_sems.at[index],
            recv_sem=self.recv_sems.at[index],
            device_id=source,
            device_id_type=MESH,
        ).wait_recv()

    def finish(self):
        for copy in self.sent:
            copy.wait_send()


class LineGather:
    def __init__(self, place, along_x, own, buf, send, recv):
        self.links, self.own, self.buf = Links(send, recv), own, buf
        self.next = lambda sign: place.at(dx=sign) if along_x else place.at(dz=sign)

    def stage0(self):
        for r in (0, 1):
            for s in (1, -1):
                rows = Gather.rows(r, None)
                self.links.push(
                    r * 4 + (s < 0), self.own.at[rows, :], self.buf.at[-s % 4, rows, :], self.next(s)
                )

    def stage1(self, halves=(0, 1)):
        for r in halves:
            for part, s in ((0, 1), (1, -1)):
                whole, rows = Gather.rows(r, None), Gather.rows(r, part)
                self.links.arrive(r * 4 + (s < 0), self.buf.at[-s % 4, whole, :], self.next(-s))
                self.links.push(
                    r * 4 + 2 + part, self.buf.at[-s % 4, rows, :], self.buf.at[2, rows, :], self.next(s)
                )

    def stage2(self, halves=(0, 1)):
        for r in halves:
            for part, s in ((0, 1), (1, -1)):
                self.links.arrive(r * 4 + 2 + part, self.buf.at[2, Gather.rows(r, part), :], self.next(-s))


class LineScatter:
    def __init__(self, place, along_x, buf, far, near, send, recv):
        self.links, self.buf, self.far, self.near = Links(send, recv), buf, far, near
        self.next = lambda sign: place.at(dx=sign) if along_x else place.at(dz=sign)

    def start(self, halves=(0, 1)):
        for r in halves:
            for part, s in ((0, -1), (1, 1)):
                self.links.push(
                    r * 4 + part, self.buf.at[2, Gather.rows(r, part), :], self.far.at[r, part], self.next(s)
                )

    def pass_on(self, halves=(0, 1)):
        for r in halves:
            for part, s in ((0, -1), (1, 1)):
                whole, rows = Gather.rows(r, None), Gather.rows(r, part)
                self.links.arrive(r * 4 + part, self.far.at[r, part], self.next(-s))
                self.buf[s % 4, rows, :] = (
                    self.buf[s % 4, rows, :].astype(F32) + self.far[r, part].astype(F32)
                ).astype(BF16)
                self.links.push(
                    r * 4 + 2 + part, self.buf.at[s % 4, whole, :], self.near.at[r, part], self.next(s)
                )

    def total(self, out):
        for r in (0, 1):
            rows = Gather.rows(r, None)
            for part, s in ((0, -1), (1, 1)):
                self.links.arrive(r * 4 + 2 + part, self.near.at[r, part], self.next(-s))
            out[rows, :] = (
                self.buf[0, rows, :].astype(F32)
                + self.near[r, 0].astype(F32)
                + self.near[r, 1].astype(F32)
            ).astype(out.dtype)


LINE_BUFS = [
    pltpu.VMEM((4, 512, 256), BF16),
    pltpu.VMEM((2, 2, 128, 256), BF16),
    pltpu.VMEM((2, 2, 256, 256), BF16),
]
LINE_SEMS = [pltpu.SemaphoreType.DMA((8,))] * 4

LINK_SEMS = [pltpu.SemaphoreType.DMA((16,)), pltpu.SemaphoreType.DMA((16,))]


def each(items, body):
    def step(i, _):
        item = items[0]
        for j in range(1, len(items)):
            item = jnp.where(i == j, items[j], item)
        body(item)
        return 0

    lax.fori_loop(0, len(items), step, 0)


def layer(
    tok, wq, wk, wv, wo, og, lens, firsts, mixed_out, grad_out,
    xbuf, wqt, wkv, wob, acc, kacc, hacc,
    qs, kvall, logits, probs, peak, sums, outs, grad_t, dos, dlt, dqt, dkv16, core_in,
    yfar, ynear, grads, tfar, tnear,
    gz, hp, hfar, hnear, ax, mp, mfar, mnear,
    xs, xr, ts, tfs, tns, ws, wr, ks, kr, ds_, dr, os_, or_,
    gs, gr, hs, hr, as_, ar, ms, mr, lsem,
):
    place = Place()
    g = place.g
    half = place.t % 2
    own_rows = pl.ds(pl.multiple_of(half * 64, 64), 64)
    other_rows = pl.ds(pl.multiple_of((1 - half) * 64, 64), 64)
    loads = [
        pltpu.make_async_copy(wk, wkv.at[0, own_rows, :], lsem.at[1]),
        pltpu.make_async_copy(wv, wkv.at[1, own_rows, :], lsem.at[2]),
        pltpu.make_async_copy(tok, xbuf.at[0], lsem.at[0]),
        pltpu.make_async_copy(wq, wqt, lsem.at[3]),
        pltpu.make_async_copy(og, gz.at[0], lsem.at[4]),
    ]

    def columns_of(dz, dx):
        return pl.ds(pl.multiple_of(place.tensor(dz, dx) * 256, 256), 256)

    for dz in range(4):
        loads.append(pltpu.make_async_copy(wo.at[:, columns_of(dz, 0)], wob.at[0, dz], lsem.at[5 + dz]))
    for load in loads:
        load.start()
    greet(place)
    xg = Gather(place, tok, xbuf, xs, xr)
    gg = LineGather(place, False, og, gz, gs, gr)
    head_sum = LineScatter(place, True, hp, hfar, hnear, hs, hr)
    ag = LineGather(place, True, ax.at[0], ax, as_, ar)
    mixed = LineScatter(place, False, mp, mfar, mnear, ms, mr)
    xg.stage0()

    def group_at(dy, dcore=0):
        return place.at(dy=dy, dcore=dcore)[0]

    partner = (g, place.t + 1 - 2 * half)
    sibling = place.at(dcore=1)
    up, down = place.at(dy=1), place.at(dy=3)
    below, above, across = group_at(3), group_at(1), group_at(2)
    sib_own, sib_below, sib_above, sib_across = (group_at(dy, 1) for dy in (0, 3, 1, 2))
    first_rows, last_rows = pl.ds(0, 256), pl.ds(256, 256)

    def slice_of(rows, group, kind=None):
        columns = pl.ds(pl.multiple_of(group * 512, 512), 512)
        return wkv.at[pl.ds(0, 2) if kind is None else kind, rows, columns]

    wl = Links(ws, wr)
    loads[0].wait()
    loads[1].wait()
    wl.push(0, slice_of(own_rows, g), slice_of(own_rows, g), partner)

    ol = Links(os_, or_)
    own_slice = pl.ds(pl.multiple_of(g * 32, 32), 32)
    for d in (1, 3, 2):
        for dz in range(4):
            ol.push(
                (d - 1) * 4 + dz,
                wo.at[own_slice, columns_of(dz, d)],
                wob.at[4 - d, dz, own_slice, :],
                place.at(dx=d),
            )

    def out_slice(group, part=None):
        if part is None:
            rows = pl.ds(pl.multiple_of(group * 32, 32), 32)
        else:
            rows = pl.ds(pl.multiple_of(group * 32 + part * 16, 16), 16)
        return wob.at[pl.ds(1, 3), pl.ds(0, 4), rows, :]

    def out_one():
        for d in (1, 3, 2):
            for dz in range(4):
                ol.arrive((d - 1) * 4 + dz, wob.at[4 - d, dz, own_slice, :], place.at(dx=4 - d))
        ref = out_slice(g)
        ol.push(12, ref, ref, up)
        ol.push(13, ref, ref, down)
        ol.push(20, ref, ref, sibling)

    def out_two():
        ref = out_slice(below)
        ol.arrive(12, ref, down)
        ol.push(14, out_slice(below, 0), out_slice(below, 0), up)
        ol.push(21, ref, ref, sibling)
        ref = out_slice(above)
        ol.arrive(13, ref, up)
        ol.push(15, out_slice(above, 1), out_slice(above, 1), down)
        ol.push(22, ref, ref, sibling)

    def out_three():
        ol.arrive(14, out_slice(across, 0), down)
        ol.arrive(15, out_slice(across, 1), up)
        ref = out_slice(across)
        ol.push(23, ref, ref, sibling)

    def out_four():
        for index, group in ((20, sib_own), (21, sib_below), (22, sib_above), (23, sib_across)):
            ol.arrive(index, out_slice(group), sibling)

    def weights_one():
        ref = slice_of(other_rows, g)
        wl.arrive(0, ref, partner)
        wl.push(1, ref, ref, up)
        wl.push(2, ref, ref, down)
        wl.push(8, ref, ref, sibling)

    def weights_two():
        ref = slice_of(other_rows, below)
        wl.arrive(1, ref, down)
        wl.push(3, slice_of(other_rows, below, 0), slice_of(other_rows, below, 0), up)
        wl.push(9, ref, ref, sibling)
        ref = slice_of(other_rows, above)
        wl.arrive(2, ref, up)
        wl.push(4, slice_of(other_rows, above, 1), slice_of(other_rows, above, 1), down)
        wl.push(10, ref, ref, sibling)

    def weights_three():
        wl.arrive(3, slice_of(other_rows, across, 0), down)
        wl.arrive(4, slice_of(other_rows, across, 1), up)
        ref = slice_of(other_rows, across)
        wl.push(11, ref, ref, sibling)

    def weights_four():
        for index, group in ((8, sib_own), (9, sib_below), (10, sib_above), (11, sib_across)):
            wl.arrive(index, slice_of(other_rows, group), sibling)

    def clear(i, _):
        dkv16[i] = jnp.zeros((512, 256), BF16)
        return 0

    lax.fori_loop(0, 8, clear, 0)
    loads[2].wait()
    loads[3].wait()

    def span(slot):
        chunk = place.tensor(slot // 4, slot % 4)
        return pl.ds(pl.multiple_of(chunk * 256, 256), 256)

    def head_weights(slot):
        return wkv[:, :, span(slot)].reshape(256, 256)

    def gathered(total_ref, buf, weight, cb, pairs, first=False):
        for h in (0, 1):
            rows = pl.ds(h * 256, 256)
            total = None
            for du, dv in pairs:
                slot = Gather.slot(h, du, dv)
                part = dot(buf[slot, rows, :], weight(slot), 1, cb)
                total = part if total is None else total + part
            total_ref[rows, :] = total if first else total_ref[rows, :] + total

    def project(pairs, first=False):
        gathered(acc, xbuf, lambda slot: wqt[span(slot), :], 0, pairs, first)

    def project_kv(pairs, first=False):
        gathered(kacc, xbuf, head_weights, 1, pairs, first)

    def head_part(dx):
        total = dot(gz[0], wob[dx, 0], 1, 1)
        for dz in (1, 2, 3):
            total = total + dot(gz[dz], wob[dx, dz], 1, 1)
        hp[dx] = total.astype(BF16)

    def mixed_part(dz, r):
        rows = pl.ds(r * 256, 256)
        total = dot(ax[0, rows, :], wob[0, dz])
        for dx in (1, 2, 3):
            total = total + dot(ax[dx, rows, :], wob[dx, dz])
        mp[dz, rows, :] = total.astype(BF16)

    project(READY[0], True)
    xg.stage1()
    gg.stage0()
    weights_one()
    out_one()
    project(READY[1])
    xg.stage2a()
    xg.stage2b()
    weights_two()
    out_two()
    project(READY[2])
    xg.stage3()
    gg.stage1()
    weights_three()
    out_three()
    project(READY[3])
    weights_four()
    project_kv(READY[0], True)
    project_kv(READY[1])
    project_kv(READY[2])
    project_kv(READY[3])
    xg.stage4()
    project_kv(READY[4])

    kv = Links(ks, kr)
    kvall[g] = kacc[...].astype(BF16)
    kv.push(1, kvall.at[g], kvall.at[g], up)
    kv.push(2, kvall.at[g], kvall.at[g], down)
    kv.push(8, kvall.at[g], kvall.at[g], sibling)
    project(READY[4])
    qs[0] = acc[:, 0:128].astype(BF16)
    qs[1] = acc[:, 128:256].astype(BF16)
    for load in loads[4:]:
        load.wait()

    lane = lax.broadcasted_iota(jnp.int32, (1, 512), 1)
    position = lane + g * 512
    low_key = jnp.where(lane < 256, firsts[2 * g], firsts[2 * g + 1]) * 256
    end = lens[0]
    for i in range(1, 5):
        low_key = jnp.maximum(low_key, jnp.where(position >= end, end, 0))
        if i < 4:
            end = end + lens[i]
    for h in (0, 1):
        peak[h] = jnp.full((1, 512), -1e30, F32)
        sums[h] = jnp.zeros((1, 512), F32)
        outs[h] = jnp.zeros((128, 512), F32)
        dqt[h] = jnp.zeros((128, 512), F32)

    def score(k):
        @pl.when(k <= g)
        def _():
            key = lax.broadcasted_iota(jnp.int32, (512, 512), 0) + k * 512
            visible = (key >= low_key) & (key <= position)
            for h in (0, 1):
                raw = dot(kvall[k, :, 0:128], qs[h], 1, 1) * (SCALE * LOG2E)
                raw = jnp.where(visible, raw, -1e30)
                logits[k, h] = raw
                peak[h] = jnp.maximum(peak[h], jnp.max(raw, axis=0, keepdims=True))

    def weigh(k, _):
        for h in (0, 1):
            prob = jnp.exp2(logits[k, h] - peak[h])
            rounded = prob.astype(BF16)
            probs[k, h] = rounded
            sums[h] += jnp.sum(prob, axis=0, keepdims=True)
            outs[h] += dot(kvall[k, :, 128:256], rounded, 0, 0)
        return 0

    each([g], score)
    out_four()
    gg.stage2()
    head_part(2)
    head_sum.start()
    for dx in (1, 3, 0):
        head_part(dx)
    kv.arrive(1, kvall.at[below], down)
    kv.push(3, kvall.at[below, first_rows, :], kvall.at[below, first_rows, :], up)
    kv.push(9, kvall.at[below], kvall.at[below], sibling)
    kv.arrive(2, kvall.at[above], up)
    kv.push(4, kvall.at[above, last_rows, :], kvall.at[above, last_rows, :], down)
    kv.push(10, kvall.at[above], kvall.at[above], sibling)
    kv.arrive(8, kvall.at[sib_own], sibling)
    each([sib_own, below, above], score)
    head_sum.pass_on()
    kv.arrive(3, kvall.at[across, first_rows, :], down)
    kv.arrive(4, kvall.at[across, last_rows, :], up)
    kv.push(11, kvall.at[across], kvall.at[across], sibling)
    kv.arrive(9, kvall.at[sib_below], sibling)
    kv.arrive(10, kvall.at[sib_above], sibling)
    each([sib_below, sib_above, across], score)
    kv.arrive(11, kvall.at[sib_across], sibling)
    each([sib_across], score)
    lax.fori_loop(0, (g + 1) // 2, weigh, 0)
    head_sum.total(hacc)
    for h in (0, 1):
        grad_t[h] = hacc[:, h * 128 : (h + 1) * 128].T
    lax.fori_loop((g + 1) // 2, g + 1, weigh, 0)

    for h in (0, 1):
        inverse = 1.0 / sums[h]
        outs[h] = outs[h] * inverse
        out_t = outs[h].astype(BF16).astype(F32)
        dlt[h] = jnp.sum(grad_t[h] * out_t, axis=0, keepdims=True) * inverse
        column = jnp.broadcast_to(inverse, (8, 512)).T[:, 0:1]
        dos[h] = (hacc[:, h * 128 : (h + 1) * 128] * column).astype(BF16)

    def backward(k):
        @pl.when(k <= g)
        def _():
            keys, values = kvall[k, :, 0:128], kvall[k, :, 128:256]
            key_part, value_part = None, None
            for h in (0, 1):
                prob = probs[k, h]
                dprob = dot(values, dos[h], 1, 1)
                grad = (prob.astype(F32) * (dprob - dlt[h])).astype(BF16)
                dqt[h] += dot(keys, grad, 0, 0)
                one, two = dot(grad, qs[h]), dot(prob, dos[h])
                key_part = one if h == 0 else key_part + one
                value_part = two if h == 0 else value_part + two
            dkv16[k, :, 0:128] = (key_part * SCALE).astype(BF16)
            dkv16[k, :, 128:256] = value_part.astype(BF16)

    kvg = Links(ds_, dr)

    def to_sibling(dy, group):
        kvg.push(dy, dkv16.at[group], core_in.at[dy], sibling)

    def join_cores(dy, group):
        kvg.arrive(dy, core_in.at[dy], sibling)
        dkv16[group] = (dkv16[group].astype(F32) + core_in[dy].astype(F32)).astype(BF16)

    def add_far(part, group, rows, source):
        kvg.arrive(4 + part, yfar.at[part], source)
        dkv16[group, rows, :] = (dkv16[group, rows, :].astype(F32) + yfar[part].astype(F32)).astype(BF16)

    for h in (0, 1):
        ax[0, :, h * 128 : (h + 1) * 128] = outs[h].T.astype(BF16)
    ag.stage0()
    each([sib_across], backward)
    to_sibling(2, sib_across)
    each([across, sib_below], backward)
    to_sibling(3, sib_below)
    join_cores(2, across)
    kvg.push(4, dkv16.at[across, first_rows, :], yfar.at[0], down)
    kvg.push(5, dkv16.at[across, last_rows, :], yfar.at[1], up)
    ag.stage1((0,))
    each([sib_above, below], backward)
    to_sibling(1, sib_above)
    ag.stage1((1,))
    join_cores(3, below)
    add_far(0, below, first_rows, up)
    kvg.push(6, dkv16.at[below], ynear.at[0], down)
    each([above], backward)
    join_cores(1, above)
    add_far(1, above, last_rows, down)
    kvg.push(7, dkv16.at[above], ynear.at[1], up)
    ag.stage2((0,))
    mixed_part(2, 0)
    mixed.start((0,))
    each([sib_own], backward)
    to_sibling(0, sib_own)
    ag.stage2((1,))
    mixed_part(2, 1)
    mixed.start((1,))
    for r in (0, 1):
        mixed_part(1, r)
        mixed_part(3, r)
    mixed.pass_on((0,))
    each([g], backward)
    for r in (0, 1):
        mixed_part(0, r)
    mixed.pass_on((1,))
    xg.finish()
    for h in (0, 1):
        grads[:, h * 128 : (h + 1) * 128] = (dqt[h] * SCALE).T.astype(BF16)
    join_cores(0, g)
    kvg.arrive(6, ynear.at[0], up)
    kvg.arrive(7, ynear.at[1], down)
    grads[:, 256:512] = (
        dkv16[g].astype(F32) + ynear[0].astype(F32) + ynear[1].astype(F32)
    ).astype(BF16)

    final = Scatter(place, xbuf, tfar, tnear, ts, tfs, tns)

    def spread(slot):
        xbuf[slot] = (
            dot(grads[:, 0:256], wqt[span(slot), :], 1, 1)
            + dot(grads[:, 256:512], head_weights(slot), 1, 0)
        ).astype(BF16)

    final.stage0(spread)
    mixed.total(mixed_out)
    final.stage1()
    final.stage2()
    final.stage3()
    final.stage4(grad_out)
    for links in (wl, ol, kv, kvg, gg.links, head_sum.links, ag.links, mixed.links, final):
        links.finish()


def hand_on(mixed, grad):
    def body(a, b, c, d):
        c[...] = a[...]
        d[...] = b[...]

    spec = pl.BlockSpec((512, 256), lambda: (0, 0))
    return pl.pallas_call(
        body,
        out_shape=(jax.ShapeDtypeStruct((512, 256), BF16),) * 2,
        in_specs=[spec] * 2,
        out_specs=[spec] * 2,
        name="hand_on",
    )(mixed, grad)


def local(tokens, w_query, w_key, w_value, w_out, out_grad, lengths, kv_first):
    return hand_on(
        *pl.pallas_call(
            layer,
            out_shape=(
                jax.ShapeDtypeStruct((512, 256), BF16),
                jax.ShapeDtypeStruct((512, 256), BF16),
            ),
            in_specs=[pl.BlockSpec(memory_space=pl.ANY)] * 6
            + [pl.BlockSpec(memory_space=pltpu.SMEM)] * 2,
            out_specs=[pl.BlockSpec(memory_space=pltpu.VMEM)] * 2,
            scratch_shapes=[
                pltpu.VMEM((16, 512, 256), BF16),
                pltpu.VMEM((4096, 256), BF16),
                pltpu.VMEM((2, 128, 4096), BF16),
                pltpu.VMEM((4, 4, 256, 256), BF16),
                pltpu.VMEM((512, 256), F32),
                pltpu.VMEM((512, 256), F32),
                pltpu.VMEM((512, 256), F32),
                pltpu.VMEM((2, 512, 128), BF16),
                pltpu.VMEM((8, 512, 256), BF16),
                pltpu.VMEM((8, 2, 512, 512), F32),
                pltpu.VMEM((8, 2, 512, 512), BF16),
                pltpu.VMEM((2, 1, 512), F32),
                pltpu.VMEM((2, 1, 512), F32),
                pltpu.VMEM((2, 128, 512), F32),
                pltpu.VMEM((2, 128, 512), F32),
                pltpu.VMEM((2, 512, 128), BF16),
                pltpu.VMEM((2, 1, 512), F32),
                pltpu.VMEM((2, 128, 512), F32),
                pltpu.VMEM((8, 512, 256), BF16),
                pltpu.VMEM((4, 512, 256), BF16),
                pltpu.VMEM((2, 256, 256), BF16),
                pltpu.VMEM((2, 512, 256), BF16),
                pltpu.VMEM((512, 512), BF16),
                *SCATTER_BUFS,
                pltpu.VMEM((4, 512, 256), BF16),
                *LINE_BUFS,
                pltpu.VMEM((4, 512, 256), BF16),
                *LINE_BUFS,
                *GATHER_SEMS,
                *SCATTER_SEMS,
                *LINK_SEMS,
                *LINK_SEMS,
                *LINK_SEMS,
                pltpu.SemaphoreType.DMA((24,)),
                pltpu.SemaphoreType.DMA((24,)),
                *LINE_SEMS,
                *LINE_SEMS,
                pltpu.SemaphoreType.DMA((9,)),
            ],
            compiler_params=pltpu.CompilerParams(
                collective_id=0, has_side_effects=True, vmem_limit_bytes=62 * 1024 * 1024
            ),
            name="layer",
        )(tokens, w_query, w_key.T, w_value.T, w_out, out_grad, lengths, kv_first)
    )


def solution(mesh):
    return jax.shard_map(
        local,
        mesh=mesh,
        in_specs=(
            P("group", "tensor"),
            P(None, "tensor"),
            P(None, "tensor"),
            P(None, "tensor"),
            P("tensor", None),
            P("group", "tensor"),
            P(),
            P(),
        ),
        out_specs=(P("group", "tensor"), P("group", "tensor")),
        check_vma=False,
    )
```

```python
import jax
import jax.numpy as jnp
from jax import lax
from jax.experimental import pallas as pl
from jax.experimental.pallas import tpu as pltpu
from jax.sharding import PartitionSpec as P

HD = 128
LOG2E = 1.4426950408889634
SCALE = HD**-0.5
MESH = pl.DeviceIdType.MESH
F32 = jnp.float32
BF16 = jnp.bfloat16


def dot(a, b, ca=1, cb=0):
    return lax.dot_general(a, b, (((ca,), (cb,)), ((), ())), preferred_element_type=F32)


class Place:
    def __init__(self):
        self.g = lax.axis_index("group")
        self.t = lax.axis_index("tensor")
        self.y, self.core = self.g // 2, self.g % 2
        self.z, self.x = self.t // 4, self.t % 4

    def tensor(self, dz, dx):
        return (self.z + dz) % 4 * 4 + (self.x + dx) % 4

    def at(self, dz=0, dx=0, dy=0, dcore=0):
        return (
            (self.y + dy) % 4 * 2 + (self.core + dcore) % 2,
            self.tensor(dz, dx),
        )


def greet(place):
    barrier = pltpu.get_barrier_semaphore()
    others = [place.at(dx=1), place.at(dx=2), place.at(dx=3), place.at(dz=1), place.at(dz=3)]
    others += [place.at(dy=1), place.at(dy=3), place.at(dcore=1)]
    for other in others:
        pl.semaphore_signal(barrier, inc=1, device_id=other, device_id_type=MESH)
    pl.semaphore_wait(barrier, len(others))


class Gather:
    def __init__(self, place, own, buf, send, recv):
        self.place, self.own, self.buf, self.send_sems, self.recv_sems = place, own, buf, send, recv
        self.sent = []

    @staticmethod
    def slot(h, du, dv):
        return (dv % 4) * 4 + du % 4 if h == 0 else (du % 4) * 4 + dv % 4

    @staticmethod
    def rows(h, part):
        return pl.ds(h * 256, 256) if part is None else pl.ds(h * 256 + part * 128, 128)

    def ref(self, h, du, dv, part):
        rows = self.rows(h, part)
        if du % 4 == 0 and dv % 4 == 0:
            return self.own.at[rows, :]
        return self.buf.at[self.slot(h, du, dv), rows, :]

    def push(self, h, axis, sign, du, dv, part=None):
        if axis == 0:
            tu, tv = du - sign, dv
        else:
            tu, tv = du, dv - sign
        along_x = (axis == 0) == (h == 0)
        target = self.place.at(dx=sign) if along_x else self.place.at(dz=sign)
        copy = pltpu.make_async_remote_copy(
            src_ref=self.ref(h, du, dv, part),
            dst_ref=self.buf.at[self.slot(h, tu, tv), self.rows(h, part), :],
            send_sem=self.send_sems.at[len(self.sent)],
            recv_sem=self.recv_sems.at[h, self.slot(h, tu, tv), part or 0],
            device_id=target,
            device_id_type=MESH,
        )
        copy.start()
        self.sent.append(copy)

    def arrive(self, h, du, dv, part=None):
        ref = self.buf.at[self.slot(h, du, dv), self.rows(h, part), :]
        pltpu.make_async_remote_copy(
            src_ref=ref,
            dst_ref=ref,
            send_sem=self.send_sems.at[0],
            recv_sem=self.recv_sems.at[h, self.slot(h, du, dv), part or 0],
            device_id=self.place.at(dx=1),
            device_id_type=MESH,
        ).wait_recv()

    def far(self, h, axis, du, dv, sign):
        self.push(h, axis, sign, du, dv, 0 if sign == 1 else 1)

    def stage0(self):
        for h in (0, 1):
            for s in (1, -1):
                self.push(h, 0, s, 0, 0)
        for h in (0, 1):
            for s in (1, -1):
                self.push(h, 1, s, 0, 0)

    def stage1(self):
        for s in (1, -1):
            for h in (0, 1):
                self.arrive(h, -s, 0)
                self.far(h, 0, -s, 0, s)
                for w in (1, -1):
                    self.push(h, 1, w, -s, 0)
        for s in (1, -1):
            for h in (0, 1):
                self.arrive(h, 0, -s)
                self.far(h, 1, 0, -s, s)

    def stage2a(self):
        for h in (0, 1):
            for part in (0, 1):
                self.arrive(h, 2, 0, part)
            for w in (1, -1):
                self.push(h, 1, w, 2, 0)

    def stage2b(self):
        for s in (1, -1):
            for w in (1, -1):
                for h in (0, 1):
                    self.arrive(h, -s, -w)
                    self.far(h, 1, -s, -w, w)

    def stage3(self):
        for w in (1, -1):
            for h in (0, 1):
                self.arrive(h, 2, -w)
                self.far(h, 1, 2, -w, w)

    def stage4(self):
        for du in range(4):
            for h in (0, 1):
                for part in (0, 1):
                    self.arrive(h, du, 2, part)

    def finish(self):
        for copy in self.sent:
            copy.wait_send()


GATHER_SEMS = [pltpu.SemaphoreType.DMA((40,)), pltpu.SemaphoreType.DMA((2, 16, 2))]

READY = [
    [(0, 0)],
    [(1, 0), (3, 0), (0, 1), (0, 3)],
    [(2, 0), (1, 1), (1, 3), (3, 1), (3, 3)],
    [(2, 1), (2, 3)],
    [(0, 2), (1, 2), (2, 2), (3, 2)],
]


class Scatter:
    def __init__(self, place, buf, far, near, send, far_sems, near_sems):
        self.place, self.buf, self.far, self.near = place, buf, far, near
        self.send_sems, self.far_sems, self.near_sems = send, far_sems, near_sems
        self.sent = []

    def where(self, h, line, offset):
        return Gather.slot(h, line, offset) if line < 4 else Gather.slot(h, offset, 0)

    def push(self, h, line, sign, src, dst, sem):
        along_x = (line == 4) == (h == 0)
        target = self.place.at(dx=sign) if along_x else self.place.at(dz=sign)
        copy = pltpu.make_async_remote_copy(
            src_ref=src,
            dst_ref=dst,
            send_sem=self.send_sems.at[len(self.sent)],
            recv_sem=sem,
            device_id=target,
            device_id_type=MESH,
        )
        copy.start()
        self.sent.append(copy)

    def arrive(self, ref, sem):
        pltpu.make_async_remote_copy(
            src_ref=ref,
            dst_ref=ref,
            send_sem=self.send_sems.at[0],
            recv_sem=sem,
            device_id=self.place.at(dx=1),
            device_id_type=MESH,
        ).wait_recv()

    def start(self, h, line):
        slot = self.where(h, line, 2)
        for part, sign in ((0, -1), (1, 1)):
            self.push(
                h, line, sign,
                self.buf.at[slot, Gather.rows(h, part), :],
                self.far.at[h, line, part],
                self.far_sems.at[h, line, part],
            )

    def pass_on(self, h, line):
        for part, sign in ((0, -1), (1, 1)):
            slot = self.where(h, line, sign)
            rows = Gather.rows(h, part)
            self.arrive(self.far.at[h, line, part], self.far_sems.at[h, line, part])
            self.buf[slot, rows, :] = (
                self.buf[slot, rows, :].astype(F32) + self.far[h, line, part].astype(F32)
            ).astype(BF16)
            self.push(
                h, line, sign,
                self.buf.at[slot, Gather.rows(h, None), :],
                self.near.at[h, line, part],
                self.near_sems.at[h, line, part],
            )

    def total(self, h, line):
        for part in (0, 1):
            self.arrive(self.near.at[h, line, part], self.near_sems.at[h, line, part])
        slot = self.where(h, line, 0)
        rows = Gather.rows(h, None)
        value = (
            self.buf[slot, rows, :].astype(F32)
            + self.near[h, line, 0].astype(F32)
            + self.near[h, line, 1].astype(F32)
        ).astype(BF16)
        return slot, rows, value

    def stage0(self, fill):
        done = []
        for line in (2, 1, 3, 0):
            for h in (0, 1):
                slot = self.where(h, line, 2)
                if slot not in done:
                    fill(slot)
                    done.append(slot)
                self.start(h, line)
        for slot in range(16):
            if slot not in done:
                fill(slot)

    def stage1(self):
        for line in (2, 1, 3, 0):
            for h in (0, 1):
                self.pass_on(h, line)

    def settle(self, line):
        for h in (0, 1):
            slot, rows, value = self.total(h, line)
            self.buf[slot, rows, :] = value

    def stage2(self):
        self.settle(2)
        for h in (0, 1):
            self.start(h, 4)

    def stage3(self):
        self.settle(1)
        self.settle(3)
        for h in (0, 1):
            self.pass_on(h, 4)

    def stage4(self, out):
        self.settle(0)
        for h in (0, 1):
            _, rows, value = self.total(h, 4)
            out[rows, :] = value

    def finish(self):
        for copy in self.sent:
            copy.wait_send()


SCATTER_BUFS = [pltpu.VMEM((2, 5, 2, 128, 256), BF16), pltpu.VMEM((2, 5, 2, 256, 256), BF16)]
SCATTER_SEMS = [
    pltpu.SemaphoreType.DMA((40,)),
    pltpu.SemaphoreType.DMA((2, 5, 2)),
    pltpu.SemaphoreType.DMA((2, 5, 2)),
]


class Links:
    def __init__(self, send, recv):
        self.send_sems, self.recv_sems, self.sent = send, recv, []

    def push(self, index, src, dst, target):
        copy = pltpu.make_async_remote_copy(
            src_ref=src,
            dst_ref=dst,
            send_sem=self.send_sems.at[index],
            recv_sem=self.recv_sems.at[index],
            device_id=target,
            device_id_type=MESH,
        )
        copy.start()
        self.sent.append(copy)

    def arrive(self, index, ref, source):
        pltpu.make_async_remote_copy(
            src_ref=ref,
            dst_ref=ref,
            send_sem=self.send_sems.at[index],
            recv_sem=self.recv_sems.at[index],
            device_id=source,
            device_id_type=MESH,
        ).wait_recv()

    def finish(self):
        for copy in self.sent:
            copy.wait_send()


class LineGather:
    def __init__(self, place, along_x, own, buf, send, recv):
        self.links, self.own, self.buf = Links(send, recv), own, buf
        self.next = lambda sign: place.at(dx=sign) if along_x else place.at(dz=sign)

    def stage0(self):
        for r in (0, 1):
            for s in (1, -1):
                rows = Gather.rows(r, None)
                self.links.push(
                    r * 4 + (s < 0), self.own.at[rows, :], self.buf.at[-s % 4, rows, :], self.next(s)
                )

    def stage1(self, halves=(0, 1)):
        for r in halves:
            for part, s in ((0, 1), (1, -1)):
                whole, rows = Gather.rows(r, None), Gather.rows(r, part)
                self.links.arrive(r * 4 + (s < 0), self.buf.at[-s % 4, whole, :], self.next(-s))
                self.links.push(
                    r * 4 + 2 + part, self.buf.at[-s % 4, rows, :], self.buf.at[2, rows, :], self.next(s)
                )

    def stage2(self, halves=(0, 1)):
        for r in halves:
            for part, s in ((0, 1), (1, -1)):
                self.links.arrive(r * 4 + 2 + part, self.buf.at[2, Gather.rows(r, part), :], self.next(-s))


class LineScatter:
    def __init__(self, place, along_x, buf, far, near, send, recv):
        self.links, self.buf, self.far, self.near = Links(send, recv), buf, far, near
        self.next = lambda sign: place.at(dx=sign) if along_x else place.at(dz=sign)

    def start(self, halves=(0, 1)):
        for r in halves:
            for part, s in ((0, -1), (1, 1)):
                self.links.push(
                    r * 4 + part, self.buf.at[2, Gather.rows(r, part), :], self.far.at[r, part], self.next(s)
                )

    def pass_on(self, halves=(0, 1)):
        for r in halves:
            for part, s in ((0, -1), (1, 1)):
                whole, rows = Gather.rows(r, None), Gather.rows(r, part)
                self.links.arrive(r * 4 + part, self.far.at[r, part], self.next(-s))
                self.buf[s % 4, rows, :] = (
                    self.buf[s % 4, rows, :].astype(F32) + self.far[r, part].astype(F32)
                ).astype(BF16)
                self.links.push(
                    r * 4 + 2 + part, self.buf.at[s % 4, whole, :], self.near.at[r, part], self.next(s)
                )

    def total(self, out):
        for r in (0, 1):
            rows = Gather.rows(r, None)
            for part, s in ((0, -1), (1, 1)):
                self.links.arrive(r * 4 + 2 + part, self.near.at[r, part], self.next(-s))
            out[rows, :] = (
                self.buf[0, rows, :].astype(F32)
                + self.near[r, 0].astype(F32)
                + self.near[r, 1].astype(F32)
            ).astype(out.dtype)


LINE_BUFS = [
    pltpu.VMEM((4, 512, 256), BF16),
    pltpu.VMEM((2, 2, 128, 256), BF16),
    pltpu.VMEM((2, 2, 256, 256), BF16),
]
LINE_SEMS = [pltpu.SemaphoreType.DMA((8,))] * 4

LINK_SEMS = [pltpu.SemaphoreType.DMA((16,)), pltpu.SemaphoreType.DMA((16,))]


def each(items, body):
    def step(i, _):
        item = items[0]
        for j in range(1, len(items)):
            item = jnp.where(i == j, items[j], item)
        body(item)
        return 0

    lax.fori_loop(0, len(items), step, 0)


def layer(
    tok, wq, wk, wv, wo, og, lens, firsts, mixed_out, grad_out,
    xbuf, wqt, wkv, wob, acc, kacc, hacc,
    qs, kvall, logits, probs, peak, sums, outs, grad_t, dos, dlt, dqt, dkv16, core_in,
    yfar, ynear, grads, tfar, tnear,
    gz, hp, hfar, hnear, ax, mp, mfar, mnear,
    xs, xr, ts, tfs, tns, ws, wr, ks, kr, ds_, dr, os_, or_,
    gs, gr, hs, hr, as_, ar, ms, mr, lsem,
):
    place = Place()
    g = place.g
    half = place.t % 2
    own_rows = pl.ds(pl.multiple_of(half * 64, 64), 64)
    other_rows = pl.ds(pl.multiple_of((1 - half) * 64, 64), 64)
    loads = [
        pltpu.make_async_copy(wk, wkv.at[0, own_rows, :], lsem.at[1]),
        pltpu.make_async_copy(wv, wkv.at[1, own_rows, :], lsem.at[2]),
        pltpu.make_async_copy(tok, xbuf.at[0], lsem.at[0]),
        pltpu.make_async_copy(wq, wqt, lsem.at[3]),
        pltpu.make_async_copy(og, gz.at[0], lsem.at[4]),
    ]

    def columns_of(dz, dx):
        return pl.ds(pl.multiple_of(place.tensor(dz, dx) * 256, 256), 256)

    for dz in range(4):
        loads.append(pltpu.make_async_copy(wo.at[:, columns_of(dz, 0)], wob.at[0, dz], lsem.at[5 + dz]))
    for load in loads:
        load.start()
    greet(place)
    xg = Gather(place, tok, xbuf, xs, xr)
    gg = LineGather(place, False, og, gz, gs, gr)
    head_sum = LineScatter(place, True, hp, hfar, hnear, hs, hr)
    ag = LineGather(place, True, ax.at[0], ax, as_, ar)
    mixed = LineScatter(place, False, mp, mfar, mnear, ms, mr)
    xg.stage0()

    def group_at(dy, dcore=0):
        return place.at(dy=dy, dcore=dcore)[0]

    partner = (g, place.t + 1 - 2 * half)
    sibling = place.at(dcore=1)
    up, down = place.at(dy=1), place.at(dy=3)
    below, above, across = group_at(3), group_at(1), group_at(2)
    sib_own, sib_below, sib_above, sib_across = (group_at(dy, 1) for dy in (0, 3, 1, 2))
    first_rows, last_rows = pl.ds(0, 256), pl.ds(256, 256)

    def slice_of(rows, group, kind=None):
        columns = pl.ds(pl.multiple_of(group * 512, 512), 512)
        return wkv.at[pl.ds(0, 2) if kind is None else kind, rows, columns]

    wl = Links(ws, wr)
    loads[0].wait()
    loads[1].wait()
    wl.push(0, slice_of(own_rows, g), slice_of(own_rows, g), partner)

    ol = Links(os_, or_)
    own_slice = pl.ds(pl.multiple_of(g * 32, 32), 32)
    for d in (1, 3, 2):
        for dz in range(4):
            ol.push(
                (d - 1) * 4 + dz,
                wo.at[own_slice, columns_of(dz, d)],
                wob.at[4 - d, dz, own_slice, :],
                place.at(dx=d),
            )

    def out_slice(group, part=None):
        if part is None:
            rows = pl.ds(pl.multiple_of(group * 32, 32), 32)
        else:
            rows = pl.ds(pl.multiple_of(group * 32 + part * 16, 16), 16)
        return wob.at[pl.ds(1, 3), pl.ds(0, 4), rows, :]

    def out_one():
        for d in (1, 3, 2):
            for dz in range(4):
                ol.arrive((d - 1) * 4 + dz, wob.at[4 - d, dz, own_slice, :], place.at(dx=4 - d))
        ref = out_slice(g)
        ol.push(12, ref, ref, up)
        ol.push(13, ref, ref, down)
        ol.push(20, ref, ref, sibling)

    def out_two():
        ref = out_slice(below)
        ol.arrive(12, ref, down)
        ol.push(14, out_slice(below, 0), out_slice(below, 0), up)
        ol.push(21, ref, ref, sibling)
        ref = out_slice(above)
        ol.arrive(13, ref, up)
        ol.push(15, out_slice(above, 1), out_slice(above, 1), down)
        ol.push(22, ref, ref, sibling)

    def out_three():
        ol.arrive(14, out_slice(across, 0), down)
        ol.arrive(15, out_slice(across, 1), up)
        ref = out_slice(across)
        ol.push(23, ref, ref, sibling)

    def out_four():
        for index, group in ((20, sib_own), (21, sib_below), (22, sib_above), (23, sib_across)):
            ol.arrive(index, out_slice(group), sibling)

    def weights_one():
        ref = slice_of(other_rows, g)
        wl.arrive(0, ref, partner)
        wl.push(1, ref, ref, up)
        wl.push(2, ref, ref, down)
        wl.push(8, ref, ref, sibling)

    def weights_two():
        ref = slice_of(other_rows, below)
        wl.arrive(1, ref, down)
        wl.push(3, slice_of(other_rows, below, 0), slice_of(other_rows, below, 0), up)
        wl.push(9, ref, ref, sibling)
        ref = slice_of(other_rows, above)
        wl.arrive(2, ref, up)
        wl.push(4, slice_of(other_rows, above, 1), slice_of(other_rows, above, 1), down)
        wl.push(10, ref, ref, sibling)

    def weights_three():
        wl.arrive(3, slice_of(other_rows, across, 0), down)
        wl.arrive(4, slice_of(other_rows, across, 1), up)
        ref = slice_of(other_rows, across)
        wl.push(11, ref, ref, sibling)

    def weights_four():
        for index, group in ((8, sib_own), (9, sib_below), (10, sib_above), (11, sib_across)):
            wl.arrive(index, slice_of(other_rows, group), sibling)

    def clear(i, _):
        dkv16[i] = jnp.zeros((512, 256), BF16)
        return 0

    lax.fori_loop(0, 8, clear, 0)
    loads[2].wait()
    loads[3].wait()

    def span(slot):
        chunk = place.tensor(slot // 4, slot % 4)
        return pl.ds(pl.multiple_of(chunk * 256, 256), 256)

    def head_weights(slot):
        return wkv[:, :, span(slot)].reshape(256, 256)

    def gathered(total_ref, buf, weight, cb, pairs, first=False):
        for h in (0, 1):
            rows = pl.ds(h * 256, 256)
            total = None
            for du, dv in pairs:
                slot = Gather.slot(h, du, dv)
                part = dot(buf[slot, rows, :], weight(slot), 1, cb)
                total = part if total is None else total + part
            total_ref[rows, :] = total if first else total_ref[rows, :] + total

    def project(pairs, first=False):
        gathered(acc, xbuf, lambda slot: wqt[span(slot), :], 0, pairs, first)

    def project_kv(pairs, first=False):
        gathered(kacc, xbuf, head_weights, 1, pairs, first)

    def head_part(dx):
        total = dot(gz[0], wob[dx, 0], 1, 1)
        for dz in (1, 2, 3):
            total = total + dot(gz[dz], wob[dx, dz], 1, 1)
        hp[dx] = total.astype(BF16)

    def mixed_part(dz, r):
        rows = pl.ds(r * 256, 256)
        total = dot(ax[0, rows, :], wob[0, dz])
        for dx in (1, 2, 3):
            total = total + dot(ax[dx, rows, :], wob[dx, dz])
        mp[dz, rows, :] = total.astype(BF16)

    project(READY[0], True)
    xg.stage1()
    gg.stage0()
    weights_one()
    out_one()
    project(READY[1])
    xg.stage2a()
    xg.stage2b()
    weights_two()
    out_two()
    project(READY[2])
    xg.stage3()
    gg.stage1()
    weights_three()
    out_three()
    project(READY[3])
    weights_four()
    project_kv(READY[0], True)
    project_kv(READY[1])
    project_kv(READY[2])
    project_kv(READY[3])
    xg.stage4()
    project_kv(READY[4])

    kv = Links(ks, kr)
    kvall[g] = kacc[...].astype(BF16)
    own_first, own_last = kvall.at[g, first_rows, :], kvall.at[g, last_rows, :]
    kv.push(1, own_first, own_first, up)
    kv.push(2, own_last, own_last, down)
    kv.push(5, own_last, own_last, up)
    kv.push(6, own_first, own_first, down)
    kv.push(8, kvall.at[g], kvall.at[g], sibling)
    project(READY[4])
    qs[0] = acc[:, 0:128].astype(BF16)
    qs[1] = acc[:, 128:256].astype(BF16)
    for load in loads[4:]:
        load.wait()

    lane = lax.broadcasted_iota(jnp.int32, (1, 512), 1)
    position = lane + g * 512
    low_key = jnp.where(lane < 256, firsts[2 * g], firsts[2 * g + 1]) * 256
    end = lens[0]
    for i in range(1, 5):
        low_key = jnp.maximum(low_key, jnp.where(position >= end, end, 0))
        if i < 4:
            end = end + lens[i]
    for h in (0, 1):
        peak[h] = jnp.full((1, 512), -1e30, F32)
        sums[h] = jnp.zeros((1, 512), F32)
        outs[h] = jnp.zeros((128, 512), F32)
        dqt[h] = jnp.zeros((128, 512), F32)

    def score(k):
        @pl.when(k <= g)
        def _():
            key = lax.broadcasted_iota(jnp.int32, (512, 512), 0) + k * 512
            visible = (key >= low_key) & (key <= position)
            for h in (0, 1):
                raw = dot(kvall[k, :, 0:128], qs[h], 1, 1) * (SCALE * LOG2E)
                raw = jnp.where(visible, raw, -1e30)
                logits[k, h] = raw
                peak[h] = jnp.maximum(peak[h], jnp.max(raw, axis=0, keepdims=True))

    def weigh(k, _):
        for h in (0, 1):
            prob = jnp.exp2(logits[k, h] - peak[h])
            rounded = prob.astype(BF16)
            probs[k, h] = rounded
            sums[h] += jnp.sum(prob, axis=0, keepdims=True)
            outs[h] += dot(kvall[k, :, 128:256], rounded, 0, 0)
        return 0

    each([g], score)
    out_four()
    gg.stage2()
    head_part(2)
    head_sum.start()
    for dx in (1, 3, 0):
        head_part(dx)
    kv.arrive(1, kvall.at[below, first_rows, :], down)
    kv.push(3, kvall.at[below, first_rows, :], kvall.at[below, first_rows, :], up)
    kv.arrive(2, kvall.at[above, last_rows, :], up)
    kv.push(4, kvall.at[above, last_rows, :], kvall.at[above, last_rows, :], down)
    kv.arrive(5, kvall.at[below, last_rows, :], down)
    kv.push(9, kvall.at[below], kvall.at[below], sibling)
    kv.arrive(6, kvall.at[above, first_rows, :], up)
    kv.push(10, kvall.at[above], kvall.at[above], sibling)
    kv.arrive(8, kvall.at[sib_own], sibling)
    each([sib_own, below, above], score)
    head_sum.pass_on()
    kv.arrive(3, kvall.at[across, first_rows, :], down)
    kv.arrive(4, kvall.at[across, last_rows, :], up)
    kv.push(11, kvall.at[across], kvall.at[across], sibling)
    kv.arrive(9, kvall.at[sib_below], sibling)
    kv.arrive(10, kvall.at[sib_above], sibling)
    each([sib_below, sib_above, across], score)
    kv.arrive(11, kvall.at[sib_across], sibling)
    each([sib_across], score)
    lax.fori_loop(0, (g + 1) // 2, weigh, 0)
    head_sum.total(hacc)
    for h in (0, 1):
        grad_t[h] = hacc[:, h * 128 : (h + 1) * 128].T
    lax.fori_loop((g + 1) // 2, g + 1, weigh, 0)

    for h in (0, 1):
        inverse = 1.0 / sums[h]
        outs[h] = outs[h] * inverse
        out_t = outs[h].astype(BF16).astype(F32)
        dlt[h] = jnp.sum(grad_t[h] * out_t, axis=0, keepdims=True) * inverse
        column = jnp.broadcast_to(inverse, (8, 512)).T[:, 0:1]
        dos[h] = (hacc[:, h * 128 : (h + 1) * 128] * column).astype(BF16)

    def backward(k):
        @pl.when(k <= g)
        def _():
            keys, values = kvall[k, :, 0:128], kvall[k, :, 128:256]
            key_part, value_part = None, None
            for h in (0, 1):
                prob = probs[k, h]
                dprob = dot(values, dos[h], 1, 1)
                grad = (prob.astype(F32) * (dprob - dlt[h])).astype(BF16)
                dqt[h] += dot(keys, grad, 0, 0)
                one, two = dot(grad, qs[h]), dot(prob, dos[h])
                key_part = one if h == 0 else key_part + one
                value_part = two if h == 0 else value_part + two
            dkv16[k, :, 0:128] = (key_part * SCALE).astype(BF16)
            dkv16[k, :, 128:256] = value_part.astype(BF16)

    kvg = Links(ds_, dr)

    def to_sibling(dy, group):
        kvg.push(dy, dkv16.at[group], core_in.at[dy], sibling)

    def join_cores(dy, group):
        kvg.arrive(dy, core_in.at[dy], sibling)
        dkv16[group] = (dkv16[group].astype(F32) + core_in[dy].astype(F32)).astype(BF16)

    def add_far(part, group, rows, source):
        kvg.arrive(4 + part, yfar.at[part], source)
        dkv16[group, rows, :] = (dkv16[group, rows, :].astype(F32) + yfar[part].astype(F32)).astype(BF16)

    for h in (0, 1):
        ax[0, :, h * 128 : (h + 1) * 128] = outs[h].T.astype(BF16)
    ag.stage0()
    each([sib_across], backward)
    to_sibling(2, sib_across)
    each([across, sib_below], backward)
    to_sibling(3, sib_below)
    join_cores(2, across)
    kvg.push(4, dkv16.at[across, first_rows, :], yfar.at[0], down)
    kvg.push(5, dkv16.at[across, last_rows, :], yfar.at[1], up)
    ag.stage1((0,))
    each([sib_above, below], backward)
    to_sibling(1, sib_above)
    ag.stage1((1,))
    join_cores(3, below)
    add_far(0, below, first_rows, up)
    kvg.push(6, dkv16.at[below], ynear.at[0], down)
    each([above], backward)
    join_cores(1, above)
    add_far(1, above, last_rows, down)
    kvg.push(7, dkv16.at[above], ynear.at[1], up)
    ag.stage2((0,))
    mixed_part(2, 0)
    mixed.start((0,))
    each([sib_own], backward)
    to_sibling(0, sib_own)
    ag.stage2((1,))
    mixed_part(2, 1)
    mixed.start((1,))
    for r in (0, 1):
        mixed_part(1, r)
        mixed_part(3, r)
    mixed.pass_on((0,))
    each([g], backward)
    for r in (0, 1):
        mixed_part(0, r)
    mixed.pass_on((1,))
    xg.finish()
    for h in (0, 1):
        grads[:, h * 128 : (h + 1) * 128] = (dqt[h] * SCALE).T.astype(BF16)
    join_cores(0, g)
    kvg.arrive(6, ynear.at[0], up)
    kvg.arrive(7, ynear.at[1], down)
    grads[:, 256:512] = (
        dkv16[g].astype(F32) + ynear[0].astype(F32) + ynear[1].astype(F32)
    ).astype(BF16)

    final = Scatter(place, xbuf, tfar, tnear, ts, tfs, tns)

    def spread(slot):
        xbuf[slot] = (
            dot(grads[:, 0:256], wqt[span(slot), :], 1, 1)
            + dot(grads[:, 256:512], head_weights(slot), 1, 0)
        ).astype(BF16)

    final.stage0(spread)
    mixed.total(mixed_out)
    final.stage1()
    final.stage2()
    final.stage3()
    final.stage4(grad_out)
    for links in (wl, ol, kv, kvg, gg.links, head_sum.links, ag.links, mixed.links, final):
        links.finish()


def hand_on(mixed, grad):
    def body(a, b, c, d):
        c[...] = a[...]
        d[...] = b[...]

    spec = pl.BlockSpec((512, 256), lambda: (0, 0))
    return pl.pallas_call(
        body,
        out_shape=(jax.ShapeDtypeStruct((512, 256), BF16),) * 2,
        in_specs=[spec] * 2,
        out_specs=[spec] * 2,
        name="hand_on",
    )(mixed, grad)


def local(tokens, w_query, w_key, w_value, w_out, out_grad, lengths, kv_first):
    return hand_on(
        *pl.pallas_call(
            layer,
            out_shape=(
                jax.ShapeDtypeStruct((512, 256), BF16),
                jax.ShapeDtypeStruct((512, 256), BF16),
            ),
            in_specs=[pl.BlockSpec(memory_space=pl.ANY)] * 6
            + [pl.BlockSpec(memory_space=pltpu.SMEM)] * 2,
            out_specs=[pl.BlockSpec(memory_space=pltpu.VMEM)] * 2,
            scratch_shapes=[
                pltpu.VMEM((16, 512, 256), BF16),
                pltpu.VMEM((4096, 256), BF16),
                pltpu.VMEM((2, 128, 4096), BF16),
                pltpu.VMEM((4, 4, 256, 256), BF16),
                pltpu.VMEM((512, 256), F32),
                pltpu.VMEM((512, 256), F32),
                pltpu.VMEM((512, 256), F32),
                pltpu.VMEM((2, 512, 128), BF16),
                pltpu.VMEM((8, 512, 256), BF16),
                pltpu.VMEM((8, 2, 512, 512), F32),
                pltpu.VMEM((8, 2, 512, 512), BF16),
                pltpu.VMEM((2, 1, 512), F32),
                pltpu.VMEM((2, 1, 512), F32),
                pltpu.VMEM((2, 128, 512), F32),
                pltpu.VMEM((2, 128, 512), F32),
                pltpu.VMEM((2, 512, 128), BF16),
                pltpu.VMEM((2, 1, 512), F32),
                pltpu.VMEM((2, 128, 512), F32),
                pltpu.VMEM((8, 512, 256), BF16),
                pltpu.VMEM((4, 512, 256), BF16),
                pltpu.VMEM((2, 256, 256), BF16),
                pltpu.VMEM((2, 512, 256), BF16),
                pltpu.VMEM((512, 512), BF16),
                *SCATTER_BUFS,
                pltpu.VMEM((4, 512, 256), BF16),
                *LINE_BUFS,
                pltpu.VMEM((4, 512, 256), BF16),
                *LINE_BUFS,
                *GATHER_SEMS,
                *SCATTER_SEMS,
                *LINK_SEMS,
                *LINK_SEMS,
                *LINK_SEMS,
                pltpu.SemaphoreType.DMA((24,)),
                pltpu.SemaphoreType.DMA((24,)),
                *LINE_SEMS,
                *LINE_SEMS,
                pltpu.SemaphoreType.DMA((9,)),
            ],
            compiler_params=pltpu.CompilerParams(
                collective_id=0, has_side_effects=True, vmem_limit_bytes=62 * 1024 * 1024
            ),
            name="layer",
        )(tokens, w_query, w_key.T, w_value.T, w_out, out_grad, lengths, kv_first)
    )


def solution(mesh):
    return jax.shard_map(
        local,
        mesh=mesh,
        in_specs=(
            P("group", "tensor"),
            P(None, "tensor"),
            P(None, "tensor"),
            P(None, "tensor"),
            P("tensor", None),
            P("group", "tensor"),
            P(),
            P(),
        ),
        out_specs=(P("group", "tensor"), P("group", "tensor")),
        check_vma=False,
    )
```
